256 devices in a mesh: dp: 16 (over z_hi, x), seq: 16 (over z_lo, y, core).
Axes of the slice: x: 4, y: 4, z: 8 (z_hi: 4, z_lo: 2; z = z_hi * 2 + z_lo), core: 2. Of those that a mesh axis runs over, the one named last changes fastest.
Arguments:
- inputs: bfloat16 [4096, 5120], P('seq', 'dp'), may hold values from -24 to 24
- tangents: bfloat16 [4096, 5120], P('seq', 'dp'), may hold values from -6 to 6
- query_weight: bfloat16 [5120, 4096], P('dp', 'seq'), may hold values from -1 to 1
- key_weight: bfloat16 [5120, 4096], P('dp', 'seq'), may hold values from -1 to 1
- value_weight: bfloat16 [5120, 4096], P('dp', 'seq'), may hold values from -0.078125 to 0.078125
- query_gain: float32 [4096], P('seq'), may hold values from 0.5 to 5.5
- key_gain: float32 [4096], P('seq'), may hold values from 0.5 to 5.5
- out_weight: bfloat16 [4096, 5120], P('seq', 'dp'), may hold values from -0.09375 to 0.09375
Outputs:
- attended: bfloat16 [4096, 5120], P('dp', 'seq')
- attended_tangent: bfloat16 [4096, 5120], P('dp', 'seq')
The draws below stay inside these ranges and needn't reach their ends.
All inputs are finite; a program needn't handle non-finite values.
Results may differ from the reference program's by a relative error of at most 0.035.
Values may be sent and summed in bfloat16 or wider, within the bound.
A program may use at most 128 MiB of HBM per device.

```python
import jax
import jax.numpy as jnp
from jax import lax

D = 5120
HEADS = 32
HD = 128
TOKENS = 4096
N_DP = 16


def shared_projection(key):
    return jax.random.normal(key, (D, HEADS * HD), jnp.float32) * D ** (-0.5)


def draw_inputs(key, part):
    key = jax.random.fold_in(key, 11)
    first = jax.random.fold_in(key, 0)
    base = jax.random.normal(first, (TOKENS, D), jnp.float32)
    return jnp.clip(base, -6.0, 6.0).astype(jnp.bfloat16)


def draw_tangents(key, part):
    key = jax.random.fold_in(key, 41)
    first = jax.random.fold_in(key, 0)
    base = jax.random.normal(first, (TOKENS, D), jnp.float32)
    return jnp.clip(base, -6.0, 6.0).astype(jnp.bfloat16)


def draw_query_weight(key, part):
    return jnp.clip(shared_projection(key), -1.0, 1.0).astype(jnp.bfloat16)


def draw_key_weight(key, part):
    key = jax.random.fold_in(key, 22)
    own = jax.random.normal(key, (D, HEADS * HD), jnp.float32) * D ** (-0.5)
    return jnp.clip(own, -1.0, 1.0).astype(jnp.bfloat16)


def draw_query_gain(key, part):
    key = jax.random.fold_in(key, 31)
    return jax.random.uniform(key, (HEADS * HD,), jnp.float32, 0.5, 1.5)


def draw_key_gain(key, part):
    key = jax.random.fold_in(key, 32)
    return jax.random.uniform(key, (HEADS * HD,), jnp.float32, 0.5, 1.5)


def shard_levels(own_key, shape, pieces, low, largest):
    def one(axis_at, blocks):
        heights = jax.random.uniform(jax.random.fold_in(jax.random.fold_in(own_key, 6), axis_at), (blocks,), jnp.float32, low / len(pieces), largest / len(pieces))
        return jnp.repeat(jnp.exp(heights), shape[axis_at] // blocks).reshape((-1,) + (1,) * (len(shape) - axis_at - 1))

    level = one(*pieces[0])
    for cut in pieces[1:]:
        level = level * one(*cut)
    return level


def gaussian(key, extent, scale, reach, pieces=(), held_as=jnp.bfloat16):
    loudness = shard_levels(key, extent, pieces, -0.22, 0.18) if pieces else 1.0
    result = jax.random.normal(key, extent, jnp.float32) * scale * loudness
    return jnp.minimum(jnp.maximum(result, -reach), reach).astype(held_as)


def setup_inputs(seed: int = 0) -> dict:
    streams_of = jax.random.split(jax.random.key(seed), 9)
    return {
        "inputs": draw_inputs(jax.random.fold_in(streams_of[8], 71), 0),
        "tangents": draw_tangents(jax.random.fold_in(streams_of[8], 71), 0),
        "query_weight": draw_query_weight(jax.random.fold_in(streams_of[8], 71), 0),
        "key_weight": draw_key_weight(jax.random.fold_in(streams_of[8], 71), 0),
        "value_weight": gaussian(streams_of[4], (D, HEADS * HD), D ** -0.5, 0.078125, ((0, 16), (1, 16))),
        "query_gain": draw_query_gain(jax.random.fold_in(streams_of[8], 71), 0),
        "key_gain": draw_key_gain(jax.random.fold_in(streams_of[8], 71), 0),
        "out_weight": gaussian(streams_of[7], (HEADS * HD, D), (HEADS * HD) ** -0.5, 0.09375, ((0, 16), (1, 16))),
    }


def head_norm(raw, raw_tan, gain):
    ms = lax.optimization_barrier(jnp.mean(raw * raw, axis=-1, keepdims=True))
    inv = lax.rsqrt(ms + 1e-06)
    inner = lax.optimization_barrier(jnp.mean(raw * raw_tan, axis=-1, keepdims=True))
    normed = gain * raw * inv
    normed_tan = gain * inv * (raw_tan - raw * inner * inv * inv)
    return (normed.astype(jnp.bfloat16), normed_tan.astype(jnp.bfloat16))

def project(inputs, tangents, weight):
    block = D // N_DP
    total = jnp.zeros((TOKENS, weight.shape[1]), jnp.float32)
    total_tan = jnp.zeros((TOKENS, weight.shape[1]), jnp.float32)
    for index in range(N_DP):
        piece = weight[index * block:(index + 1) * block]
        first = jnp.dot(inputs[:, index * block:(index + 1) * block], piece, preferred_element_type=jnp.float32)
        second = jnp.dot(tangents[:, index * block:(index + 1) * block], piece, preferred_element_type=jnp.float32)
        first = lax.optimization_barrier(first.astype(jnp.bfloat16))
        second = lax.optimization_barrier(second.astype(jnp.bfloat16))
        total = total + first.astype(jnp.float32)
        total_tan = total_tan + second.astype(jnp.float32)
    return (total, total_tan)

def one_head(packed):
    query, query_tan, keys, keys_tan, values, values_tan = packed
    scale = 1.0 / jnp.sqrt(jnp.float32(HD))
    scores = jnp.dot(query, keys.T, preferred_element_type=jnp.float32) * scale
    scores_tan = (jnp.dot(query_tan, keys.T, preferred_element_type=jnp.float32) + jnp.dot(query, keys_tan.T, preferred_element_type=jnp.float32)) * scale
    top = lax.optimization_barrier(jnp.max(scores, axis=-1, keepdims=True))
    expo = jnp.exp(scores - top)
    probs = expo / lax.optimization_barrier(jnp.sum(expo, axis=-1, keepdims=True))
    probs_tan = probs * (scores_tan - lax.optimization_barrier(jnp.sum(probs * scores_tan, axis=-1, keepdims=True)))
    probs_b = probs.astype(jnp.bfloat16)
    probs_tan_b = probs_tan.astype(jnp.bfloat16)
    heads_out = jnp.dot(probs_b, values, preferred_element_type=jnp.float32)
    heads_tan = jnp.dot(probs_tan_b, values, preferred_element_type=jnp.float32) + jnp.dot(probs_b, values_tan, preferred_element_type=jnp.float32)
    return (heads_out.astype(jnp.bfloat16), heads_tan.astype(jnp.bfloat16))

def reference(inputs, tangents, query_weight, key_weight, value_weight, query_gain, key_gain, out_weight):
    q_raw, q_raw_tan = project(inputs, tangents, query_weight)
    k_raw, k_raw_tan = project(inputs, tangents, key_weight)
    v_raw, v_raw_tan = project(inputs, tangents, value_weight)
    shape = (TOKENS, HEADS, HD)
    query, query_tan = head_norm(q_raw.reshape(shape), q_raw_tan.reshape(shape), query_gain.reshape(HEADS, HD))
    keys, keys_tan = head_norm(k_raw.reshape(shape), k_raw_tan.reshape(shape), key_gain.reshape(HEADS, HD))
    values = v_raw.astype(jnp.bfloat16).reshape(shape)
    values_tan = v_raw_tan.astype(jnp.bfloat16).reshape(shape)
    packed = tuple((jnp.transpose(item, (1, 0, 2)) for item in (query, query_tan, keys, keys_tan, values, values_tan)))
    heads_out, heads_tan = lax.map(one_head, packed)
    heads_out = jnp.transpose(heads_out, (1, 0, 2)).reshape(TOKENS, HEADS * HD)
    heads_tan = jnp.transpose(heads_tan, (1, 0, 2)).reshape(TOKENS, HEADS * HD)
    attended = jnp.dot(heads_out, out_weight, preferred_element_type=jnp.float32).astype(jnp.bfloat16)
    attended_tangent = jnp.dot(heads_tan, out_weight, preferred_element_type=jnp.float32).astype(jnp.bfloat16)
    return (attended, attended_tangent)
```

```python
import jax
import jax.numpy as jnp
from jax import lax
from jax.experimental import pallas as pl
from jax.experimental.pallas import tpu as pltpu
from jax.sharding import PartitionSpec as P

HD = 128
F = 320
TB = 256
TOKENS = 4096
HALF = 128
BF16 = jnp.bfloat16
F32 = jnp.float32
N_SEMS = 192


def kernel(
    in_ref, tin_ref, wq_ref, wk_ref, wv_ref, gq_ref, gk_ref, wo_ref,
    out_ref,
    WB, GB, AB, AN, WOB, PART, SB, RB, HOLD, OWN, KB, VB, QB, S, ST, MX, LI, EB, UB, AO, AT, HS, HB, ACC, XS, XR,
    ssem, rsem, bssem, brsem, lsem,
):
    dp = lax.axis_index("dp")
    sq = lax.axis_index("seq")
    zh, x = lax.div(dp, 4), lax.rem(dp, 4)
    zl, y, c = lax.div(sq, 8), lax.rem(lax.div(sq, 2), 4), lax.rem(sq, 2)

    def dev(zh_=zh, x_=x, zl_=zl, y_=y, c_=c):
        return (zh_ * 4 + x_, zl_ * 8 + y_ * 2 + c_)

    def rot(v, k):
        return lax.rem(v + (k % 4), 4)

    xr, xl, xo = rot(x, 1), rot(x, -1), rot(x, 2)
    yr, yl, yo = rot(y, 1), rot(y, -1), rot(y, 2)
    zr, zf, zo = rot(zh, 1), rot(zh, -1), rot(zh, 2)
    x_right, x_left = dev(x_=xr), dev(x_=xl)
    y_right, y_left = dev(y_=yr), dev(y_=yl)
    z_right, z_left = dev(zh_=zr), dev(zh_=zf)
    nz = 1 - zl
    pair = dev(zl_=nz)
    sibling = dev(c_=1 - c)
    a_to = dev(x_=2 * lax.rem(y, 2) + c, zl_=1 - lax.div(y, 2), y_=x, c_=zl)
    a_from = dev(x_=y, zl_=c, y_=2 * nz + lax.div(x, 2), c_=lax.rem(x, 2))

    wo_row = 2 * lax.div(sq, 2) + 1 - lax.rem(dp, 2)
    wo_to = (wo_row, 2 * lax.div(dp, 2) + c)
    wo_from = (
        2 * lax.div(sq, 2) + 1 - lax.rem(dp, 2), 2 * lax.div(dp, 2) + c
    )

    barrier = pltpu.get_barrier_semaphore()
    greet = [x_right, x_left, y_right, y_left, pair, a_to, a_from, wo_to, wo_from]
    for k in range(1, 8):
        peer = lax.rem(zh * 2 + c + k, 8)
        greet.append(dev(zh_=lax.div(peer, 2), c_=lax.rem(peer, 2)))
    for d in greet:
        pl.semaphore_signal(barrier, inc=1, device_id=d, device_id_type=pl.DeviceIdType.MESH)

    def rows_of(xx):
        return pl.ds(pl.multiple_of(xx * F, 64), F)

    def half_rows(xx, h):
        return pl.ds(pl.multiple_of(xx * F + h * (F // 2), 32), F // 2)

    WB[c, 0, rows_of(x), :] = wk_ref[...]
    WB[c, 1, rows_of(x), :] = wq_ref[...]
    WB[c, 2, rows_of(x), :] = wv_ref[...]
    GB[c, 0] = jnp.broadcast_to(gq_ref[...], (8, 2 * HD))
    GB[c, 1] = jnp.broadcast_to(gk_ref[...], (8, 2 * HD))

    pl.semaphore_wait(barrier, len(greet))

    sent = []

    def send(src, dst, device):
        k = len(sent)
        copy = pltpu.make_async_remote_copy(
            src_ref=src, dst_ref=dst, send_sem=ssem.at[k], recv_sem=rsem.at[k],
            device_id=device, device_id_type=pl.DeviceIdType.MESH,
        )
        copy.start()
        sent.append(copy)
        return copy

    def same(ref, device):
        return send(ref, ref, device)

    def wait(copies):
        for copy in copies:
            copy.wait_recv()

    def w_piece(w, xx):
        return WB.at[c, w, rows_of(xx), :]

    def w_half(w, xx, h):
        return WB.at[c, w, half_rows(xx, h), :]

    w_near, w_far, w_sib = {}, {}, {0: [], 1: [], 2: []}

    def w_start(w):
        w_near[w] = (same(w_piece(w, x), x_right), same(w_piece(w, x), x_left))
        w_sib[w].append(same(w_piece(w, x), sibling))

    def w_relay(w):
        right, left = w_near[w]
        right.wait_recv()
        a = same(w_half(w, xl, 0), x_right)
        w_sib[w].append(same(w_piece(w, xl), sibling))
        left.wait_recv()
        b = same(w_half(w, xr, 1), x_left)
        w_sib[w].append(same(w_piece(w, xr), sibling))
        w_far[w] = (a, b)

    def w_last(w):
        for h in range(2):
            w_far[w][h].wait_recv()
            w_sib[w].append(same(w_half(w, xo, h), sibling))

    def cols_of(g):
        return pl.ds(g * TB, TB)

    def a_piece(z, yy, g):
        return AB.at[z, rows_of(yy), cols_of(g)]

    def a_half(z, yy, h, g):
        return AB.at[z, half_rows(yy, h), cols_of(g)]

    a_perm = [
        send(ref, AB.at[lax.div(y, 2), rows_of(x), cols_of(g)], a_to)
        for g, ref in enumerate((in_ref, tin_ref))
    ]
    wo_perm = send(wo_ref, WOB.at[wo_row], wo_to)

    a_own, a_pair = [], []
    for g in range(2):
        a_perm[g].wait_recv()
        own = a_piece(nz, y, g)
        a_own.append((same(own, y_right), same(own, y_left)))
        a_pair.append(same(own, pair))
        if g == 0:
            w_start(0)
            w_sib[0].append(same(GB.at[c], sibling))

    def wo_block(zz, xx):
        return zz * 4 + xx

    def wo_half(b, h):
        return WOB.at[b, pl.ds(h * (F // 2), F // 2), :]

    w_relay(0)
    a_own_opp = []
    for g, (right, left) in enumerate(a_own):
        right.wait_recv()
        a_own_opp.append(same(a_half(nz, yl, 0, g), y_right))
        left.wait_recv()
        a_own_opp.append(same(a_half(nz, yr, 1, g), y_left))

    wait(a_pair)
    two = AB.at[zl, rows_of(y), :]
    a_two_r, a_two_l = same(two, y_right), same(two, y_left)

    w_start(2)
    wo_perm.wait_recv()
    wo_zr = same(WOB.at[wo_block(zh, x)], z_right)
    wo_zl = same(WOB.at[wo_block(zh, x)], z_left)
    w_last(0)

    def wo_relay_z():
        wo_zr.wait_recv()
        a = same(wo_half(wo_block(zf, x), 0), z_right)
        wo_zl.wait_recv()
        return [a, same(wo_half(wo_block(zr, x), 1), z_left)]

    wo_x = []

    def wo_send_x(zz):
        b = WOB.at[wo_block(zz, x)]
        wo_x.append((zz, same(b, x_right), same(b, x_left)))

    block_at = (nz, zl)

    def turn(t):
        @pl.loop(0, 5)
        def _(i):
            cut = pl.ds(pl.multiple_of(i * 256, 256), 256)
            piece = AB[block_at[t], cut, :].T
            for h in range(2):
                for s in range(2):
                    at = h * TB + s * HALF
                    AN[t, h, s, :, cut] = piece[at:at + HALF, :]

    def tile(kind, k):
        d = rot(zh, k)
        cw = lax.div(d, 2)
        cols = pl.ds(pl.multiple_of(lax.rem(d, 2) * HD, HD), HD)
        queries = kind // 2 == 1
        PART[...] = jnp.zeros((2 * TB, HD), F32)

        @pl.loop(0, 5)
        def _(i):
            deep = pl.ds(pl.multiple_of(i * 256, 256), 256)
            tokens = AN[:, :, kind % 2, :, deep] if queries else AN[kind % 2, :, :, :, deep]
            PART[...] += jnp.dot(
                tokens.reshape(2 * TB, 256), WB[cw, kind // 2, deep, cols],
                preferred_element_type=F32,
            )

        part = PART[...].reshape(2, 2, HALF, HD)
        return [(part[:, h] if queries else part[h]).reshape(TB, HD) for h in range(2)]

    relay, direct, summed = {}, {}, {}

    def rs_send(kind, slot, h, part, to):
        SB[kind, slot, h] = part.astype(BF16)
        return send(SB.at[kind, slot, h], RB.at[kind, slot, h], to)

    def rs_opposite(kind):
        part = tile(kind, 2)
        for h in range(2):
            relay[kind, h] = rs_send(kind, 0, h, part[h], z_right if h == 0 else z_left)

    def rs_direct(kind):
        for slot, k, h, to in ((1, 1, 1, z_right), (2, 3, 0, z_left)):
            part = tile(kind, k)
            direct[kind, slot] = rs_send(kind, slot, h, part[h], to)
            HOLD[kind, 1 - h] = part[1 - h]

    def rs_summed(kind):
        for slot, h, to in ((1, 0, z_right), (2, 1, z_left)):
            relay[kind, h].wait_recv()
            part = HOLD[kind, h] + RB[kind, 0, h].astype(F32)
            summed[kind, slot] = rs_send(kind, slot, h, part, to)

    def rs_own(kind):
        part = tile(kind, 0)
        for h in range(2):
            OWN[kind, h] = part[h]

    def rs_result(kind):
        for slot in (1, 2):
            direct[kind, slot].wait_recv()
            summed[kind, slot].wait_recv()
        return [
            OWN[kind, h] + RB[kind, 1, h].astype(F32) + RB[kind, 2, h].astype(F32)
            for h in range(2)
        ]

    cw = lax.div(zh, 2)
    head_cols = pl.ds(pl.multiple_of(lax.rem(zh, 2) * HD, HD), HD)

    def norm(raw, tan, gain):
        ms = jnp.mean(raw * raw, axis=-1, keepdims=True)
        inv = lax.rsqrt(ms + 1e-06)
        inner = jnp.mean(raw * tan, axis=-1, keepdims=True)
        normed = gain * raw * inv
        normed_tan = gain * inv * (tan - raw * inner * inv * inv)
        return normed.astype(BF16), normed_tan.astype(BF16)

    def slot_of(xx, cc):
        return xx * 2 + cc

    g_near, g_far = {}, {}
    g_sib = {(b, t, j): [] for b in range(2) for t in range(2) for j in range(4)}

    def g_block(b, t, xx, rows=0, count=TB):
        return (KB, VB)[b].at[slot_of(xx, c), pl.ds(t * TB + rows, count), :]

    def g_start(b, t):
        block = g_block(b, t, x)
        g_near[b, t] = (same(block, x_right), same(block, x_left))
        g_sib[b, t, 0].append(same(block, sibling))

    def g_relay(b, t):
        right, left = g_near[b, t]
        right.wait_recv()
        first = same(g_block(b, t, xl, 0, HALF), x_right)
        g_sib[b, t, 1].append(same(g_block(b, t, xl), sibling))
        left.wait_recv()
        second = same(g_block(b, t, xr, HALF, HALF), x_left)
        g_sib[b, t, 2].append(same(g_block(b, t, xr), sibling))
        g_far[b, t] = (first, second)

    def g_last(b, t):
        for h in range(2):
            g_far[b, t][h].wait_recv()
            g_sib[b, t, 3].append(same(g_block(b, t, xo, h * HALF, HALF), sibling))

    def keys_out(t):
        key, key_tan = norm(*rs_result(t), GB[cw, 1, 0:1, head_cols])
        rows = slice(t * TB, (t + 1) * TB)
        KB[slot_of(x, c), rows, 0:HD] = key
        KB[slot_of(x, c), rows, HD:] = key_tan
        g_start(0, t)

    def values_out(t):
        raw, tan = rs_result(4 + t)
        rows = slice(t * TB, (t + 1) * TB)
        VB[slot_of(x, c), rows, 0:HD] = raw.astype(BF16)
        VB[slot_of(x, c), rows, HD:] = tan.astype(BF16)
        g_start(1, t)

    wo_xopp = []

    def wo_relay_x(n):
        zz, right, left = wo_x[n]
        right.wait_recv()
        wo_xopp.append(same(wo_half(wo_block(zz, xl), 0), x_right))
        left.wait_recv()
        wo_xopp.append(same(wo_half(wo_block(zz, xr), 1), x_left))

    to_exp2 = HD ** -0.5 * 1.4426950408889634
    ln2 = 0.6931471805599453
    ROWS = 32

    def queries(s):
        gain = GB[cw, 0, 0:1, head_cols] * to_exp2
        query, query_tan = norm(*rs_result(2 + s), gain)
        QB[s, :, 0:HD] = query_tan
        QB[s, :, HD:] = query

    def arrived(b):
        for t in range(2):
            for j in range(4):
                wait(g_sib[b, t, j])

    def scores(s):
        MX[...] = jnp.full((TB, 128), -jnp.inf, F32)

        @pl.loop(0, 8)
        def _(j):
            keys = KB[j]
            cut = pl.ds(pl.multiple_of(j * 512, 512), 512)
            part = lax.dot_general(
                QB[s, :, HD:], keys[:, :HD], (((1,), (1,)), ((), ())), preferred_element_type=F32
            )
            S[:, cut] = part
            top = jnp.maximum(
                jnp.maximum(part[:, 0:128], part[:, 128:256]),
                jnp.maximum(part[:, 256:384], part[:, 384:512]),
            )
            MX[...] = jnp.maximum(MX[...], top)
            ST[:, cut] = lax.dot_general(
                QB[s], keys, (((1,), (1,)), ((), ())), preferred_element_type=F32
            )

    def softmax(s):
        @pl.loop(0, TB // ROWS)
        def _(i):
            at = pl.multiple_of(i * ROWS, ROWS)
            rows = pl.ds(at, ROWS)
            to = pl.ds(s * TB + at, ROWS)
            shift = jnp.max(MX[rows, :], axis=-1, keepdims=True)
            total = jnp.zeros((ROWS, 128), F32)
            inner = jnp.zeros((ROWS, 128), F32)
            for j in range(16):
                cut = slice(j * 256, (j + 1) * 256)
                e = jnp.exp2(S[rows, cut] - shift)
                EB[to, cut] = e.astype(BF16)
                es = e * ST[rows, cut]
                total += e[:, :128] + e[:, 128:]
                inner += es[:, :128] + es[:, 128:]
            total = jnp.sum(total, axis=-1, keepdims=True)
            mean = jnp.sum(inner, axis=-1, keepdims=True) / total
            LI[to, :] = jnp.broadcast_to(1.0 / total, (ROWS, HD))
            for j in range(16):
                cut = slice(j * 256, (j + 1) * 256)
                UB[to, cut] = (EB[to, cut].astype(F32) * (ST[rows, cut] - mean)).astype(BF16)

    def products(s):
        rows = slice(s * TB, (s + 1) * TB)
        AO[rows, :] = jnp.zeros((TB, 2 * HD), F32)
        AT[rows, :] = jnp.zeros((TB, HD), F32)

        @pl.loop(0, 8)
        def _(j):
            values = VB[j]
            cut = pl.ds(pl.multiple_of(j * 512, 512), 512)
            AO[rows, :] += jnp.dot(EB[rows, cut], values, preferred_element_type=F32)
            AT[rows, :] += jnp.dot(UB[rows, cut], values[:, :HD], preferred_element_type=F32)

    my_pair = zl * 8 + y * 2
    head_at = lax.rem(zh, 2)
    back = []

    def heads_back(s):
        rows = slice(s * TB, (s + 1) * TB)
        inv = LI[rows, :]
        primal = (AO[rows, :HD] * inv).astype(BF16)
        tangent = ((AO[rows, HD:] + AT[rows, :] * ln2) * inv).astype(BF16)
        target = HB.at[my_pair + cw, s, :, head_cols]
        for t in range(2):
            HS[s, t, 0:HALF, :] = primal[t * HALF:(t + 1) * HALF, :]
            HS[s, t, HALF:, :] = tangent[t * HALF:(t + 1) * HALF, :]
            zeta = 2 * c + block_at[t]
            copy = pltpu.make_async_remote_copy(
                src_ref=HS.at[s, t], dst_ref=target, send_sem=bssem.at[2 * s + t],
                recv_sem=brsem.at[2 * s + head_at],
                device_id=dev(zh_=zeta, c_=cw), device_id_type=pl.DeviceIdType.MESH,
            )
            stay = pltpu.make_async_copy(HS.at[s, t], target, lsem.at[2 * s + t])
            here = zeta == zh

            @pl.when(here)
            def _(stay=stay):
                stay.start()
                stay.wait()

            @pl.when(jnp.logical_not(here))
            def _(copy=copy):
                copy.start()

            back.append((copy, here))

    def hp(zz, yy):
        return zz * 8 + yy * 2 + c

    def h_part(p, s):
        return HB.at[p, s]

    def h_half(p, s, h):
        return HB.at[p, s, pl.ds(h * HALF, HALF), :]

    h_own, h_two, h_opp, swapped = {}, {}, {}, {}

    def heads_start(s):
        for h in range(2):
            came = pltpu.make_async_remote_copy(
                src_ref=HS.at[s, h], dst_ref=HB.at[sq, s, :, pl.ds(h * HD, HD)],
                send_sem=bssem.at[2 * s + h], recv_sem=brsem.at[2 * s + h],
                device_id=sibling, device_id_type=pl.DeviceIdType.MESH,
            )

            @pl.when(2 * c + h != zh)
            def _(came=came):
                came.wait_recv()

        mine = h_part(sq, s)
        h_own[s] = (same(mine, y_right), same(mine, y_left), same(mine, pair))

    def heads_pair(s):
        h_own[s][2].wait_recv()
        p = hp(nz, y)
        h_two[s] = (same(h_part(p, s), y_right), same(h_part(p, s), y_left))

    def heads_relay(s, zz, right, left):
        right.wait_recv()
        p = hp(zz, yl)
        first = same(h_half(p, s, 0), y_right)
        left.wait_recv()
        p = hp(zz, yr)
        second = same(h_half(p, s, 1), y_left)
        h_opp.setdefault(s, []).append((zz, first, second))

    def heads_relay_own(s):
        heads_relay(s, zl, *h_own[s][:2])

    def heads_relay_two(s):
        heads_relay(s, nz, *h_two[s])

    def multiply(s, zz, near, first=False):
        total = None if first else ACC[s]
        for yy in (y, yl, yr) if near else (yo,):
            p = hp(zz, yy)
            part = lax.dot_general(
                WOB[pl.ds(p - c, 2)].reshape(2 * F, 2 * HD), HB[p, s], (((1,), (1,)), ((), ())),
                preferred_element_type=F32,
            )
            total = part if total is None else total + part
        ACC[s] = total

    def multiply_far(s):
        for zz, first, second in h_opp[s]:
            first.wait_recv()
            second.wait_recv()
            multiply(s, zz, False)
        XS[s] = ACC[s, pl.ds(pl.multiple_of(c * F, 64), F), :].astype(BF16)
        swapped[s] = send(XS.at[s], XR.at[s], sibling)

    def finish(s):
        swapped[s].wait_recv()
        mine = ACC[s, pl.ds(pl.multiple_of((1 - c) * F, 64), F), :] + XR[s].astype(F32)
        cut = slice(s * HALF, (s + 1) * HALF)
        out_ref[0:F, cut] = mine[:, 0:HALF].astype(BF16)
        out_ref[F:, cut] = mine[:, HALF:].astype(BF16)

    wait(a_own_opp)
    turn(0)
    wait(w_sib[0])
    rs_opposite(0)
    rs_direct(0)
    wo_zopp = wo_relay_z()
    a_two_r.wait_recv()
    a_two_opp = [same(AB.at[zl, half_rows(yl, 0), :], y_right)]
    a_two_l.wait_recv()
    a_two_opp.append(same(AB.at[zl, half_rows(yr, 1), :], y_left))
    w_relay(2)
    w_start(1)
    rs_summed(0)
    rs_own(0)
    wait(a_two_opp)
    turn(1)
    rs_opposite(1)
    rs_direct(1)
    w_last(2)
    w_relay(1)
    for zz in (zh, zf, zr):
        wo_send_x(zz)
    wait(w_sib[2])
    rs_opposite(4)
    rs_summed(1)
    rs_direct(4)
    keys_out(0)
    rs_own(1)
    rs_opposite(5)
    w_last(1)
    rs_summed(4)
    rs_direct(5)
    keys_out(1)
    wait(wo_zopp)
    wo_send_x(zo)
    wait(w_sib[1])
    rs_opposite(2)
    g_relay(0, 0)
    rs_own(4)
    rs_summed(5)
    rs_direct(2)
    g_relay(0, 1)
    values_out(0)
    rs_own(5)
    rs_opposite(3)
    rs_own(2)
    rs_own(3)
    for n in range(4):
        wo_relay_x(n)
    g_last(0, 0)
    g_last(0, 1)
    rs_summed(2)
    rs_direct(3)
    values_out(1)
    g_relay(1, 0)
    rs_summed(3)
    g_last(1, 0)
    g_relay(1, 1)
    queries(0)
    arrived(0)
    scores(0)
    g_last(1, 1)
    softmax(0)
    arrived(1)
    products(0)
    heads_back(0)
    queries(1)
    scores(1)
    wait(wo_xopp)
    heads_start(0)
    softmax(1)
    heads_pair(0)
    heads_relay_own(0)
    products(1)
    heads_back(1)
    multiply(0, zl, True, first=True)
    heads_relay_two(0)
    multiply(0, nz, True)
    heads_start(1)
    heads_pair(1)
    multiply_far(0)
    heads_relay_own(1)
    multiply(1, zl, True, first=True)
    heads_relay_two(1)
    multiply(1, nz, True)
    finish(0)
    multiply_far(1)
    finish(1)

    for copy in sent:
        copy.wait_send()
    for copy, here in back:
        @pl.when(jnp.logical_not(here))
        def _(copy=copy):
            copy.wait_send()


def shards(
    inputs, tangents, query_weight, key_weight, value_weight, query_gain, key_gain, out_weight
):
    vmem = pl.BlockSpec(memory_space=pltpu.VMEM)
    v = pltpu.VMEM
    both = pl.pallas_call(
        kernel,
        out_shape=jax.ShapeDtypeStruct((2 * F, TB), BF16),
        in_specs=[vmem] * 8,
        out_specs=vmem,
        scratch_shapes=[
            v((2, 3, 4 * F, 256), BF16),
            v((2, 2, 8, 256), F32),
            v((2, 4 * F, 512), BF16),
            v((2, 2, 2, HALF, 4 * F), BF16),
            v((16, F, 256), BF16),
            v((2 * TB, HD), F32),
            v((6, 3, 2, TB, HD), BF16),
            v((6, 3, 2, TB, HD), BF16),
            v((6, 2, TB, HD), F32),
            v((6, 2, TB, HD), F32),
            v((8, 512, 256), BF16),
            v((8, 512, 256), BF16),
            v((2, TB, 256), BF16),
            v((TB, TOKENS), F32),
            v((TB, TOKENS), F32),
            v((TB, 128), F32),
            v((2 * TB, HD), F32),
            v((2 * TB, TOKENS), BF16),
            v((2 * TB, TOKENS), BF16),
            v((2 * TB, 2 * HD), F32),
            v((2 * TB, HD), F32),
            v((2, 2, TB, HD), BF16),
            v((16, 2, TB, 256), BF16),
            v((2, 2 * F, TB), F32),
            v((2, F, TB), BF16),
            v((2, F, TB), BF16),
            pltpu.SemaphoreType.DMA((N_SEMS,)),
            pltpu.SemaphoreType.DMA((N_SEMS,)),
            pltpu.SemaphoreType.DMA((4,)),
            pltpu.SemaphoreType.DMA((4,)),
            pltpu.SemaphoreType.DMA((4,)),
        ],
        compiler_params=pltpu.CompilerParams(
            collective_id=0, has_side_effects=True, vmem_limit_bytes=60 * 2**20
        ),
    )(
        inputs.T, tangents.T, query_weight, key_weight, value_weight,
        query_gain.reshape(1, 2 * HD), key_gain.reshape(1, 2 * HD), out_weight.T,
    )
    return both[:F].T, both[F:].T


def solution(mesh):
    in_specs = (
        P("seq", "dp"),
        P("seq", "dp"),
        P("dp", "seq"),
        P("dp", "seq"),
        P("dp", "seq"),
        P("seq"),
        P("seq"),
        P("seq", "dp"),
    )
    out_specs = (P("dp", "seq"), P("dp", "seq"))
    return jax.shard_map(shards, mesh=mesh, in_specs=in_specs, out_specs=out_specs, check_vma=False)
```

```python
import jax
import jax.numpy as jnp
from jax import lax
from jax.experimental import pallas as pl
from jax.experimental.pallas import tpu as pltpu
from jax.sharding import PartitionSpec as P

HD = 128
F = 320
TB = 256
TOKENS = 4096
HALF = 128
BF16 = jnp.bfloat16
F32 = jnp.float32
N_SEMS = 192


def kernel(
    in_ref, tin_ref, wq_ref, wk_ref, wv_ref, gq_ref, gk_ref, wo_ref,
    out_ref,
    WB, GB, AB, AN, WOB, PART, SB, RB, HOLD, OWN, KB, VB, QB, S, ST, MX, LI, EB, UB, AO, AT, HS, HB, ACC, XS, XR,
    ssem, rsem, bssem, brsem, lsem,
):
    dp = lax.axis_index("dp")
    sq = lax.axis_index("seq")
    zh, x = lax.div(dp, 4), lax.rem(dp, 4)
    zl, y, c = lax.div(sq, 8), lax.rem(lax.div(sq, 2), 4), lax.rem(sq, 2)

    def dev(zh_=zh, x_=x, zl_=zl, y_=y, c_=c):
        return (zh_ * 4 + x_, zl_ * 8 + y_ * 2 + c_)

    def ring(v):
        return lax.rem(v + 1 + 2 * c, 4), lax.rem(v + 3 - 2 * c, 4), lax.rem(v + 2, 4)

    xr, xl, xo = ring(x)
    yr, yl, yo = ring(y)
    zr, zf, zo = ring(zh)
    x_right, x_left = dev(x_=xr), dev(x_=xl)
    y_right, y_left = dev(y_=yr), dev(y_=yl)
    z_right, z_left = dev(zh_=zr), dev(zh_=zf)
    nz = 1 - zl
    pair = dev(zl_=nz)
    sibling = dev(c_=1 - c)
    a_to = dev(x_=2 * lax.rem(y, 2) + c, zl_=1 - lax.div(y, 2), y_=x, c_=zl)
    a_from = dev(x_=y, zl_=c, y_=2 * nz + lax.div(x, 2), c_=lax.rem(x, 2))

    wo_row = 2 * lax.div(sq, 2) + 1 - lax.rem(dp, 2)
    wo_to = (wo_row, 2 * lax.div(dp, 2) + c)
    wo_from = (
        2 * lax.div(sq, 2) + 1 - lax.rem(dp, 2), 2 * lax.div(dp, 2) + c
    )

    barrier = pltpu.get_barrier_semaphore()
    greet = [x_right, x_left, y_right, y_left, pair, a_to, a_from, wo_to, wo_from]
    for k in range(1, 8):
        peer = lax.rem(zh * 2 + c + k, 8)
        greet.append(dev(zh_=lax.div(peer, 2), c_=lax.rem(peer, 2)))
    for d in greet:
        pl.semaphore_signal(barrier, inc=1, device_id=d, device_id_type=pl.DeviceIdType.MESH)

    def rows_of(xx):
        return pl.ds(pl.multiple_of(xx * F, 64), F)

    def half_rows(xx, h):
        return pl.ds(pl.multiple_of(xx * F + h * (F // 2), 32), F // 2)

    WB[c, 0, rows_of(x), :] = wk_ref[...]
    WB[c, 1, rows_of(x), :] = wq_ref[...]
    WB[c, 2, rows_of(x), :] = wv_ref[...]
    GB[c, 0] = jnp.broadcast_to(gq_ref[...], (8, 2 * HD))
    GB[c, 1] = jnp.broadcast_to(gk_ref[...], (8, 2 * HD))

    pl.semaphore_wait(barrier, len(greet))

    sent = []

    def send(src, dst, device):
        k = len(sent)
        copy = pltpu.make_async_remote_copy(
            src_ref=src, dst_ref=dst, send_sem=ssem.at[k], recv_sem=rsem.at[k],
            device_id=device, device_id_type=pl.DeviceIdType.MESH,
        )
        copy.start()
        sent.append(copy)
        return copy

    def same(ref, device):
        return send(ref, ref, device)

    def wait(copies):
        for copy in copies:
            copy.wait_recv()

    def w_piece(w, xx):
        return WB.at[c, w, rows_of(xx), :]

    def w_half(w, xx, h):
        return WB.at[c, w, half_rows(xx, h), :]

    w_near, w_far, w_sib = {}, {}, {0: [], 1: [], 2: []}

    def w_start(w):
        w_near[w] = (same(w_piece(w, x), x_right), same(w_piece(w, x), x_left))
        w_sib[w].append(same(w_piece(w, x), sibling))

    def w_relay(w):
        right, left = w_near[w]
        right.wait_recv()
        a = same(w_half(w, xl, 0), x_right)
        w_sib[w].append(same(w_piece(w, xl), sibling))
        left.wait_recv()
        b = same(w_half(w, xr, 1), x_left)
        w_sib[w].append(same(w_piece(w, xr), sibling))
        w_far[w] = (a, b)

    def w_last(w):
        for h in range(2):
            w_far[w][h].wait_recv()
            w_sib[w].append(same(w_half(w, xo, h), sibling))

    def cols_of(g):
        return pl.ds(g * TB, TB)

    def a_piece(z, yy, g):
        return AB.at[z, rows_of(yy), cols_of(g)]

    def a_half(z, yy, h, g):
        return AB.at[z, half_rows(yy, h), cols_of(g)]

    a_perm = [
        send(ref, AB.at[lax.div(y, 2), rows_of(x), cols_of(g)], a_to)
        for g, ref in enumerate((in_ref, tin_ref))
    ]
    wo_perm = send(wo_ref, WOB.at[wo_row], wo_to)

    a_own, a_pair = [], []
    for g in range(2):
        a_perm[g].wait_recv()
        own = a_piece(nz, y, g)
        a_own.append((same(own, y_right), same(own, y_left)))
        a_pair.append(same(own, pair))
        if g == 0:
            w_start(0)
            w_sib[0].append(same(GB.at[c], sibling))

    def wo_block(zz, xx):
        return zz * 4 + xx

    def wo_half(b, h):
        return WOB.at[b, pl.ds(h * (F // 2), F // 2), :]

    w_relay(0)
    a_own_opp = []
    for g, (right, left) in enumerate(a_own):
        right.wait_recv()
        a_own_opp.append(same(a_half(nz, yl, 0, g), y_right))
        left.wait_recv()
        a_own_opp.append(same(a_half(nz, yr, 1, g), y_left))

    wait(a_pair)
    two = AB.at[zl, rows_of(y), :]
    a_two_r, a_two_l = same(two, y_right), same(two, y_left)

    w_start(2)
    wo_perm.wait_recv()
    wo_zr = same(WOB.at[wo_block(zh, x)], z_right)
    wo_zl = same(WOB.at[wo_block(zh, x)], z_left)
    w_last(0)

    def wo_relay_z():
        wo_zr.wait_recv()
        a = same(wo_half(wo_block(zf, x), 0), z_right)
        wo_zl.wait_recv()
        return [a, same(wo_half(wo_block(zr, x), 1), z_left)]

    wo_x = []

    def wo_send_x(zz):
        b = WOB.at[wo_block(zz, x)]
        wo_x.append((zz, same(b, x_right), same(b, x_left)))

    block_at = (nz, zl)

    def turn(t):
        @pl.loop(0, 5)
        def _(i):
            cut = pl.ds(pl.multiple_of(i * 256, 256), 256)
            piece = AB[block_at[t], cut, :].T
            for h in range(2):
                for s in range(2):
                    at = h * TB + s * HALF
                    AN[t, h, s, :, cut] = piece[at:at + HALF, :]

    def tile(kind, k):
        d = (zh, zr, zo, zf)[k]
        cw = lax.div(d, 2)
        cols = pl.ds(pl.multiple_of(lax.rem(d, 2) * HD, HD), HD)
        queries = kind // 2 == 1
        PART[...] = jnp.zeros((2 * TB, HD), F32)

        @pl.loop(0, 5)
        def _(i):
            deep = pl.ds(pl.multiple_of(i * 256, 256), 256)
            tokens = AN[:, :, kind % 2, :, deep] if queries else AN[kind % 2, :, :, :, deep]
            PART[...] += jnp.dot(
                tokens.reshape(2 * TB, 256), WB[cw, kind // 2, deep, cols],
                preferred_element_type=F32,
            )

        part = PART[...].reshape(2, 2, HALF, HD)
        return [(part[:, h] if queries else part[h]).reshape(TB, HD) for h in range(2)]

    relay, direct, summed = {}, {}, {}

    def rs_send(kind, slot, h, part, to):
        SB[kind, slot, h] = part.astype(BF16)
        return send(SB.at[kind, slot, h], RB.at[kind, slot, h], to)

    def rs_opposite(kind):
        part = tile(kind, 2)
        for h in range(2):
            relay[kind, h] = rs_send(kind, 0, h, part[h], z_right if h == 0 else z_left)

    def rs_direct(kind):
        for slot, k, h, to in ((1, 1, 1, z_right), (2, 3, 0, z_left)):
            part = tile(kind, k)
            direct[kind, slot] = rs_send(kind, slot, h, part[h], to)
            HOLD[kind, 1 - h] = part[1 - h]

    def rs_summed(kind):
        for slot, h, to in ((1, 0, z_right), (2, 1, z_left)):
            relay[kind, h].wait_recv()
            part = HOLD[kind, h] + RB[kind, 0, h].astype(F32)
            summed[kind, slot] = rs_send(kind, slot, h, part, to)

    def rs_own(kind):
        part = tile(kind, 0)
        for h in range(2):
            OWN[kind, h] = part[h]

    def rs_result(kind):
        for slot in (1, 2):
            direct[kind, slot].wait_recv()
            summed[kind, slot].wait_recv()
        return [
            OWN[kind, h] + RB[kind, 1, h].astype(F32) + RB[kind, 2, h].astype(F32)
            for h in range(2)
        ]

    cw = lax.div(zh, 2)
    head_cols = pl.ds(pl.multiple_of(lax.rem(zh, 2) * HD, HD), HD)

    def norm(raw, tan, gain):
        ms = jnp.mean(raw * raw, axis=-1, keepdims=True)
        inv = lax.rsqrt(ms + 1e-06)
        inner = jnp.mean(raw * tan, axis=-1, keepdims=True)
        normed = gain * raw * inv
        normed_tan = gain * inv * (tan - raw * inner * inv * inv)
        return normed.astype(BF16), normed_tan.astype(BF16)

    def slot_of(xx, cc):
        return xx * 2 + cc

    g_near, g_far = {}, {}
    g_sib = {(b, t, j): [] for b in range(2) for t in range(2) for j in range(4)}

    def g_block(b, t, xx, rows=0, count=TB):
        return (KB, VB)[b].at[slot_of(xx, c), pl.ds(t * TB + rows, count), :]

    def g_start(b, t):
        block = g_block(b, t, x)
        g_near[b, t] = (same(block, x_right), same(block, x_left))
        g_sib[b, t, 0].append(same(block, sibling))

    def g_relay(b, t):
        right, left = g_near[b, t]
        right.wait_recv()
        first = same(g_block(b, t, xl, 0, HALF), x_right)
        g_sib[b, t, 1].append(same(g_block(b, t, xl), sibling))
        left.wait_recv()
        second = same(g_block(b, t, xr, HALF, HALF), x_left)
        g_sib[b, t, 2].append(same(g_block(b, t, xr), sibling))
        g_far[b, t] = (first, second)

    def g_last(b, t):
        for h in range(2):
            g_far[b, t][h].wait_recv()
            g_sib[b, t, 3].append(same(g_block(b, t, xo, h * HALF, HALF), sibling))

    def keys_out(t):
        key, key_tan = norm(*rs_result(t), GB[cw, 1, 0:1, head_cols])
        rows = slice(t * TB, (t + 1) * TB)
        KB[slot_of(x, c), rows, 0:HD] = key
        KB[slot_of(x, c), rows, HD:] = key_tan
        g_start(0, t)

    def values_out(t):
        raw, tan = rs_result(4 + t)
        rows = slice(t * TB, (t + 1) * TB)
        VB[slot_of(x, c), rows, 0:HD] = raw.astype(BF16)
        VB[slot_of(x, c), rows, HD:] = tan.astype(BF16)
        g_start(1, t)

    wo_xopp = []

    def wo_relay_x(n):
        zz, right, left = wo_x[n]
        right.wait_recv()
        wo_xopp.append(same(wo_half(wo_block(zz, xl), 0), x_right))
        left.wait_recv()
        wo_xopp.append(same(wo_half(wo_block(zz, xr), 1), x_left))

    to_exp2 = HD ** -0.5 * 1.4426950408889634
    ln2 = 0.6931471805599453
    ROWS = 32

    def queries(s):
        gain = GB[cw, 0, 0:1, head_cols] * to_exp2
        query, query_tan = norm(*rs_result(2 + s), gain)
        QB[s, :, 0:HD] = query_tan
        QB[s, :, HD:] = query

    def arrived(b):
        for t in range(2):
            for j in range(4):
                wait(g_sib[b, t, j])

    def scores(s):
        MX[...] = jnp.full((TB, 128), -jnp.inf, F32)

        @pl.loop(0, 8)
        def _(j):
            keys = KB[j]
            cut = pl.ds(pl.multiple_of(j * 512, 512), 512)
            part = lax.dot_general(
                QB[s, :, HD:], keys[:, :HD], (((1,), (1,)), ((), ())), preferred_element_type=F32
            )
            S[:, cut] = part
            top = jnp.maximum(
                jnp.maximum(part[:, 0:128], part[:, 128:256]),
                jnp.maximum(part[:, 256:384], part[:, 384:512]),
            )
            MX[...] = jnp.maximum(MX[...], top)
            ST[:, cut] = lax.dot_general(
                QB[s], keys, (((1,), (1,)), ((), ())), preferred_element_type=F32
            )

    def softmax(s):
        @pl.loop(0, TB // ROWS)
        def _(i):
            at = pl.multiple_of(i * ROWS, ROWS)
            rows = pl.ds(at, ROWS)
            to = pl.ds(s * TB + at, ROWS)
            shift = jnp.max(MX[rows, :], axis=-1, keepdims=True)
            total = jnp.zeros((ROWS, 128), F32)
            inner = jnp.zeros((ROWS, 128), F32)
            for j in range(16):
                cut = slice(j * 256, (j + 1) * 256)
                e = jnp.exp2(S[rows, cut] - shift)
                EB[to, cut] = e.astype(BF16)
                es = e * ST[rows, cut]
                total += e[:, :128] + e[:, 128:]
                inner += es[:, :128] + es[:, 128:]
            total = jnp.sum(total, axis=-1, keepdims=True)
            mean = jnp.sum(inner, axis=-1, keepdims=True) / total
            LI[to, :] = jnp.broadcast_to(1.0 / total, (ROWS, HD))
            for j in range(16):
                cut = slice(j * 256, (j + 1) * 256)
                UB[to, cut] = (EB[to, cut].astype(F32) * (ST[rows, cut] - mean)).astype(BF16)

    def products(s):
        rows = slice(s * TB, (s + 1) * TB)
        AO[rows, :] = jnp.zeros((TB, 2 * HD), F32)
        AT[rows, :] = jnp.zeros((TB, HD), F32)

        @pl.loop(0, 8)
        def _(j):
            values = VB[j]
            cut = pl.ds(pl.multiple_of(j * 512, 512), 512)
            AO[rows, :] += jnp.dot(EB[rows, cut], values, preferred_element_type=F32)
            AT[rows, :] += jnp.dot(UB[rows, cut], values[:, :HD], preferred_element_type=F32)

    my_pair = zl * 8 + y * 2
    head_at = lax.rem(zh, 2)
    back = []

    def heads_back(s):
        rows = slice(s * TB, (s + 1) * TB)
        inv = LI[rows, :]
        primal = (AO[rows, :HD] * inv).astype(BF16)
        tangent = ((AO[rows, HD:] + AT[rows, :] * ln2) * inv).astype(BF16)
        target = HB.at[my_pair + cw, s, :, head_cols]
        for t in range(2):
            HS[s, t, 0:HALF, :] = primal[t * HALF:(t + 1) * HALF, :]
            HS[s, t, HALF:, :] = tangent[t * HALF:(t + 1) * HALF, :]
            zeta = 2 * c + block_at[t]
            copy = pltpu.make_async_remote_copy(
                src_ref=HS.at[s, t], dst_ref=target, send_sem=bssem.at[2 * s + t],
                recv_sem=brsem.at[2 * s + head_at],
                device_id=dev(zh_=zeta, c_=cw), device_id_type=pl.DeviceIdType.MESH,
            )
            stay = pltpu.make_async_copy(HS.at[s, t], target, lsem.at[2 * s + t])
            here = zeta == zh

            @pl.when(here)
            def _(stay=stay):
                stay.start()
                stay.wait()

            @pl.when(jnp.logical_not(here))
            def _(copy=copy):
                copy.start()

            back.append((copy, here))

    def hp(zz, yy):
        return zz * 8 + yy * 2 + c

    def h_part(p, s):
        return HB.at[p, s]

    def h_half(p, s, h):
        return HB.at[p, s, pl.ds(h * HALF, HALF), :]

    h_own, h_two, h_opp, swapped = {}, {}, {}, {}

    def heads_start(s):
        for h in range(2):
            came = pltpu.make_async_remote_copy(
                src_ref=HS.at[s, h], dst_ref=HB.at[sq, s, :, pl.ds(h * HD, HD)],
                send_sem=bssem.at[2 * s + h], recv_sem=brsem.at[2 * s + h],
                device_id=sibling, device_id_type=pl.DeviceIdType.MESH,
            )

            @pl.when(2 * c + h != zh)
            def _(came=came):
                came.wait_recv()

        mine = h_part(sq, s)
        h_own[s] = (same(mine, y_right), same(mine, y_left), same(mine, pair))

    def heads_pair(s):
        h_own[s][2].wait_recv()
        p = hp(nz, y)
        h_two[s] = (same(h_part(p, s), y_right), same(h_part(p, s), y_left))

    def heads_relay(s, zz, right, left):
        right.wait_recv()
        p = hp(zz, yl)
        first = same(h_half(p, s, 0), y_right)
        left.wait_recv()
        p = hp(zz, yr)
        second = same(h_half(p, s, 1), y_left)
        h_opp.setdefault(s, []).append((zz, first, second))

    def heads_relay_own(s):
        heads_relay(s, zl, *h_own[s][:2])

    def heads_relay_two(s):
        heads_relay(s, nz, *h_two[s])

    def multiply(s, zz, near, first=False):
        total = None if first else ACC[s]
        for yy in (y, yl, yr) if near else (yo,):
            p = hp(zz, yy)
            part = lax.dot_general(
                WOB[pl.ds(p - c, 2)].reshape(2 * F, 2 * HD), HB[p, s], (((1,), (1,)), ((), ())),
                preferred_element_type=F32,
            )
            total = part if total is None else total + part
        ACC[s] = total

    def multiply_far(s):
        for zz, first, second in h_opp[s]:
            first.wait_recv()
            second.wait_recv()
            multiply(s, zz, False)
        XS[s] = ACC[s, pl.ds(pl.multiple_of(c * F, 64), F), :].astype(BF16)
        swapped[s] = send(XS.at[s], XR.at[s], sibling)

    def finish(s):
        swapped[s].wait_recv()
        mine = ACC[s, pl.ds(pl.multiple_of((1 - c) * F, 64), F), :] + XR[s].astype(F32)
        cut = slice(s * HALF, (s + 1) * HALF)
        out_ref[0:F, cut] = mine[:, 0:HALF].astype(BF16)
        out_ref[F:, cut] = mine[:, HALF:].astype(BF16)

    wait(a_own_opp)
    turn(0)
    wait(w_sib[0])
    rs_opposite(0)
    rs_direct(0)
    wo_zopp = wo_relay_z()
    a_two_r.wait_recv()
    a_two_opp = [same(AB.at[zl, half_rows(yl, 0), :], y_right)]
    a_two_l.wait_recv()
    a_two_opp.append(same(AB.at[zl, half_rows(yr, 1), :], y_left))
    w_relay(2)
    w_start(1)
    rs_summed(0)
    rs_own(0)
    wait(a_two_opp)
    turn(1)
    rs_opposite(1)
    rs_direct(1)
    w_last(2)
    w_relay(1)
    for zz in (zh, zf, zr):
        wo_send_x(zz)
    wait(w_sib[2])
    rs_opposite(4)
    rs_summed(1)
    rs_direct(4)
    keys_out(0)
    rs_own(1)
    rs_opposite(5)
    w_last(1)
    rs_summed(4)
    rs_direct(5)
    keys_out(1)
    wait(wo_zopp)
    wo_send_x(zo)
    wait(w_sib[1])
    rs_opposite(2)
    g_relay(0, 0)
    rs_own(4)
    rs_summed(5)
    rs_direct(2)
    g_relay(0, 1)
    values_out(0)
    rs_own(5)
    rs_opposite(3)
    rs_own(2)
    rs_own(3)
    for n in range(4):
        wo_relay_x(n)
    g_last(0, 0)
    g_last(0, 1)
    rs_summed(2)
    rs_direct(3)
    values_out(1)
    g_relay(1, 0)
    rs_summed(3)
    g_last(1, 0)
    g_relay(1, 1)
    queries(0)
    arrived(0)
    scores(0)
    g_last(1, 1)
    softmax(0)
    arrived(1)
    products(0)
    heads_back(0)
    queries(1)
    scores(1)
    wait(wo_xopp)
    heads_start(0)
    softmax(1)
    heads_pair(0)
    heads_relay_own(0)
    products(1)
    heads_back(1)
    multiply(0, zl, True, first=True)
    heads_relay_two(0)
    multiply(0, nz, True)
    heads_start(1)
    heads_pair(1)
    multiply_far(0)
    heads_relay_own(1)
    multiply(1, zl, True, first=True)
    heads_relay_two(1)
    multiply(1, nz, True)
    finish(0)
    multiply_far(1)
    finish(1)

    for copy in sent:
        copy.wait_send()
    for copy, here in back:
        @pl.when(jnp.logical_not(here))
        def _(copy=copy):
            copy.wait_send()


def shards(
    inputs, tangents, query_weight, key_weight, value_weight, query_gain, key_gain, out_weight
):
    vmem = pl.BlockSpec(memory_space=pltpu.VMEM)
    v = pltpu.VMEM
    both = pl.pallas_call(
        kernel,
        out_shape=jax.ShapeDtypeStruct((2 * F, TB), BF16),
        in_specs=[vmem] * 8,
        out_specs=vmem,
        scratch_shapes=[
            v((2, 3, 4 * F, 256), BF16),
            v((2, 2, 8, 256), F32),
            v((2, 4 * F, 512), BF16),
            v((2, 2, 2, HALF, 4 * F), BF16),
            v((16, F, 256), BF16),
            v((2 * TB, HD), F32),
            v((6, 3, 2, TB, HD), BF16),
            v((6, 3, 2, TB, HD), BF16),
            v((6, 2, TB, HD), F32),
            v((6, 2, TB, HD), F32),
            v((8, 512, 256), BF16),
            v((8, 512, 256), BF16),
            v((2, TB, 256), BF16),
            v((TB, TOKENS), F32),
            v((TB, TOKENS), F32),
            v((TB, 128), F32),
            v((2 * TB, HD), F32),
            v((2 * TB, TOKENS), BF16),
            v((2 * TB, TOKENS), BF16),
            v((2 * TB, 2 * HD), F32),
            v((2 * TB, HD), F32),
            v((2, 2, TB, HD), BF16),
            v((16, 2, TB, 256), BF16),
            v((2, 2 * F, TB), F32),
            v((2, F, TB), BF16),
            v((2, F, TB), BF16),
            pltpu.SemaphoreType.DMA((N_SEMS,)),
            pltpu.SemaphoreType.DMA((N_SEMS,)),
            pltpu.SemaphoreType.DMA((4,)),
            pltpu.SemaphoreType.DMA((4,)),
            pltpu.SemaphoreType.DMA((4,)),
        ],
        compiler_params=pltpu.CompilerParams(
            collective_id=0, has_side_effects=True, vmem_limit_bytes=60 * 2**20
        ),
    )(
        inputs.T, tangents.T, query_weight, key_weight, value_weight,
        query_gain.reshape(1, 2 * HD), key_gain.reshape(1, 2 * HD), out_weight.T,
    )
    return both[:F].T, both[F:].T


def solution(mesh):
    in_specs = (
        P("seq", "dp"),
        P("seq", "dp"),
        P("dp", "seq"),
        P("dp", "seq"),
        P("dp", "seq"),
        P("seq"),
        P("seq"),
        P("seq", "dp"),
    )
    out_specs = (P("dp", "seq"), P("dp", "seq"))
    return jax.shard_map(shards, mesh=mesh, in_specs=in_specs, out_specs=out_specs, check_vma=False)
```

```python
import jax
import jax.numpy as jnp
from jax import lax
from jax.experimental import pallas as pl
from jax.experimental.pallas import tpu as pltpu
from jax.sharding import PartitionSpec as P

HD = 128
F = 320
TB = 256
TOKENS = 4096
HALF = 128
BF16 = jnp.bfloat16
F32 = jnp.float32
N_SEMS = 192


def kernel(
    in_ref, tin_ref, wq_ref, wk_ref, wv_ref, gq_ref, gk_ref, wo_ref,
    out_ref,
    WB, GB, AB, AN, WOB, PART, SB, RB, HOLD, OWN, KB, VB, QB, S, ST, MX, LI, EB, UB, AO, AT, HS, HB, ACC, XS, XR,
    ssem, rsem, bssem, brsem, lsem,
):
    dp = lax.axis_index("dp")
    sq = lax.axis_index("seq")
    zh, x = lax.div(dp, 4), lax.rem(dp, 4)
    zl, y, c = lax.div(sq, 8), lax.rem(lax.div(sq, 2), 4), lax.rem(sq, 2)

    def dev(zh_=zh, x_=x, zl_=zl, y_=y, c_=c):
        return (zh_ * 4 + x_, zl_ * 8 + y_ * 2 + c_)

    def ring(v):
        return lax.rem(v + 1 + 2 * c, 4), lax.rem(v + 3 - 2 * c, 4), lax.rem(v + 2, 4)

    xr, xl, xo = ring(x)
    yr, yl, yo = ring(y)
    zr, zf, zo = ring(zh)
    x_right, x_left = dev(x_=xr), dev(x_=xl)
    y_right, y_left = dev(y_=yr), dev(y_=yl)
    z_right, z_left = dev(zh_=zr), dev(zh_=zf)
    nz = 1 - zl
    pair = dev(zl_=nz)
    sibling = dev(c_=1 - c)
    a_to = dev(x_=2 * lax.rem(y, 2) + c, zl_=1 - lax.div(y, 2), y_=x, c_=zl)
    a_from = dev(x_=y, zl_=c, y_=2 * nz + lax.div(x, 2), c_=lax.rem(x, 2))

    wo_row = 2 * lax.div(sq, 2) + 1 - lax.rem(dp, 2)
    wo_to = (wo_row, 2 * lax.div(dp, 2) + c)
    wo_from = (
        2 * lax.div(sq, 2) + 1 - lax.rem(dp, 2), 2 * lax.div(dp, 2) + c
    )

    barrier = pltpu.get_barrier_semaphore()
    greet = [x_right, x_left, y_right, y_left, pair, a_to, a_from, wo_to, wo_from]
    for k in range(1, 8):
        peer = lax.rem(zh * 2 + c + k, 8)
        greet.append(dev(zh_=lax.div(peer, 2), c_=lax.rem(peer, 2)))
    for d in greet:
        pl.semaphore_signal(barrier, inc=1, device_id=d, device_id_type=pl.DeviceIdType.MESH)

    def rows_of(xx):
        return pl.ds(pl.multiple_of(xx * F, 64), F)

    def half_rows(xx, h):
        return pl.ds(pl.multiple_of(xx * F + h * (F // 2), 32), F // 2)

    WB[c, 0, rows_of(x), :] = wk_ref[...]
    WB[c, 1, rows_of(x), :] = wq_ref[...]
    WB[c, 2, rows_of(x), :] = wv_ref[...]
    GB[c, 0] = jnp.broadcast_to(gq_ref[...], (8, 2 * HD))
    GB[c, 1] = jnp.broadcast_to(gk_ref[...], (8, 2 * HD))

    pl.semaphore_wait(barrier, len(greet))

    sent = []

    def send(src, dst, device):
        k = len(sent)
        copy = pltpu.make_async_remote_copy(
            src_ref=src, dst_ref=dst, send_sem=ssem.at[k], recv_sem=rsem.at[k],
            device_id=device, device_id_type=pl.DeviceIdType.MESH,
        )
        copy.start()
        sent.append(copy)
        return copy

    def same(ref, device):
        return send(ref, ref, device)

    def wait(copies):
        for copy in copies:
            copy.wait_recv()

    def w_piece(w, xx):
        return WB.at[c, w, rows_of(xx), :]

    def w_half(w, xx, h):
        return WB.at[c, w, half_rows(xx, h), :]

    w_near, w_far, w_sib = {}, {}, {0: [], 1: [], 2: []}

    def w_start(w):
        w_near[w] = (same(w_piece(w, x), x_right), same(w_piece(w, x), x_left))
        w_sib[w].append(same(w_piece(w, x), sibling))

    def w_relay(w):
        right, left = w_near[w]
        right.wait_recv()
        a = same(w_half(w, xl, 0), x_right)
        w_sib[w].append(same(w_piece(w, xl), sibling))
        left.wait_recv()
        b = same(w_half(w, xr, 1), x_left)
        w_sib[w].append(same(w_piece(w, xr), sibling))
        w_far[w] = (a, b)

    def w_last(w):
        for h in range(2):
            w_far[w][h].wait_recv()
            w_sib[w].append(same(w_half(w, xo, h), sibling))

    def cols_of(g):
        return pl.ds(g * TB, TB)

    def a_piece(z, yy, g):
        return AB.at[z, rows_of(yy), cols_of(g)]

    def a_half(z, yy, h, g):
        return AB.at[z, half_rows(yy, h), cols_of(g)]

    a_perm = [
        send(ref, AB.at[lax.div(y, 2), rows_of(x), cols_of(g)], a_to)
        for g, ref in enumerate((in_ref, tin_ref))
    ]

    a_own, a_pair = [], []
    for g in range(2):
        a_perm[g].wait_recv()
        own = a_piece(nz, y, g)
        a_own.append((same(own, y_right), same(own, y_left)))
        a_pair.append(same(own, pair))
        if g == 0:
            wo_perm = send(wo_ref, WOB.at[wo_row], wo_to)
            w_start(0)
            w_sib[0].append(same(GB.at[c], sibling))

    def wo_block(zz, xx):
        return zz * 4 + xx

    def wo_half(b, h):
        return WOB.at[b, pl.ds(h * (F // 2), F // 2), :]

    w_relay(0)
    a_own_opp = []
    for g, (right, left) in enumerate(a_own):
        right.wait_recv()
        a_own_opp.append(same(a_half(nz, yl, 0, g), y_right))
        left.wait_recv()
        a_own_opp.append(same(a_half(nz, yr, 1, g), y_left))

    wait(a_pair)
    two = AB.at[zl, rows_of(y), :]
    a_two_r, a_two_l = same(two, y_right), same(two, y_left)

    def wo_start_z():
        block = WOB.at[wo_block(zh, x)]
        return same(block, z_right), same(block, z_left)

    def wo_relay_z():
        return [
            same(wo_half(wo_block(zf, x), 0), z_right),
            same(wo_half(wo_block(zr, x), 1), z_left),
        ]

    w_start(2)
    wo_perm.wait_recv()
    wo_z = wo_start_z()
    w_last(0)

    wo_x = []

    def wo_send_x(zz):
        b = WOB.at[wo_block(zz, x)]
        wo_x.append((zz, same(b, x_right), same(b, x_left)))

    block_at = (nz, zl)

    def turn(t):
        @pl.loop(0, 5)
        def _(i):
            cut = pl.ds(pl.multiple_of(i * 256, 256), 256)
            piece = AB[block_at[t], cut, :].T
            for h in range(2):
                for s in range(2):
                    at = h * TB + s * HALF
                    AN[t, h, s, :, cut] = piece[at:at + HALF, :]

    def tile(kind, k):
        d = (zh, zr, zo, zf)[k]
        cw = lax.div(d, 2)
        cols = pl.ds(pl.multiple_of(lax.rem(d, 2) * HD, HD), HD)
        queries = kind // 2 == 1
        PART[...] = jnp.zeros((2 * TB, HD), F32)

        @pl.loop(0, 5)
        def _(i):
            deep = pl.ds(pl.multiple_of(i * 256, 256), 256)
            tokens = AN[:, :, kind % 2, :, deep] if queries else AN[kind % 2, :, :, :, deep]
            PART[...] += jnp.dot(
                tokens.reshape(2 * TB, 256), WB[cw, kind // 2, deep, cols],
                preferred_element_type=F32,
            )

        part = PART[...].reshape(2, 2, HALF, HD)
        return [(part[:, h] if queries else part[h]).reshape(TB, HD) for h in range(2)]

    relay, direct, summed = {}, {}, {}

    def rs_send(kind, slot, h, part, to):
        SB[kind, slot, h] = part.astype(BF16)
        return send(SB.at[kind, slot, h], RB.at[kind, slot, h], to)

    def rs_opposite(kind):
        part = tile(kind, 2)
        for h in range(2):
            relay[kind, h] = rs_send(kind, 0, h, part[h], z_right if h == 0 else z_left)

    def rs_direct(kind):
        for slot, k, h, to in ((1, 1, 1, z_right), (2, 3, 0, z_left)):
            part = tile(kind, k)
            direct[kind, slot] = rs_send(kind, slot, h, part[h], to)
            HOLD[kind, 1 - h] = part[1 - h]

    def rs_summed(kind):
        for slot, h, to in ((1, 0, z_right), (2, 1, z_left)):
            relay[kind, h].wait_recv()
            part = HOLD[kind, h] + RB[kind, 0, h].astype(F32)
            summed[kind, slot] = rs_send(kind, slot, h, part, to)

    def rs_own(kind):
        part = tile(kind, 0)
        for h in range(2):
            OWN[kind, h] = part[h]

    def rs_result(kind):
        for slot in (1, 2):
            direct[kind, slot].wait_recv()
            summed[kind, slot].wait_recv()
        return [
            OWN[kind, h] + RB[kind, 1, h].astype(F32) + RB[kind, 2, h].astype(F32)
            for h in range(2)
        ]

    cw = lax.div(zh, 2)
    head_cols = pl.ds(pl.multiple_of(lax.rem(zh, 2) * HD, HD), HD)

    def norm(raw, tan, gain):
        ms = jnp.mean(raw * raw, axis=-1, keepdims=True)
        inv = lax.rsqrt(ms + 1e-06)
        inner = jnp.mean(raw * tan, axis=-1, keepdims=True)
        normed = gain * raw * inv
        normed_tan = gain * inv * (tan - raw * inner * inv * inv)
        return normed.astype(BF16), normed_tan.astype(BF16)

    def slot_of(xx, cc):
        return xx * 2 + cc

    g_near, g_far = {}, {}
    g_sib = {(b, t, j): [] for b in range(2) for t in range(2) for j in range(4)}

    def g_block(b, t, xx, rows=0, count=TB):
        return (KB, VB)[b].at[slot_of(xx, c), pl.ds(t * TB + rows, count), :]

    def g_start(b, t):
        block = g_block(b, t, x)
        g_near[b, t] = (same(block, x_right), same(block, x_left))
        g_sib[b, t, 0].append(same(block, sibling))

    def g_relay(b, t):
        right, left = g_near[b, t]
        right.wait_recv()
        first = same(g_block(b, t, xl, 0, HALF), x_right)
        g_sib[b, t, 1].append(same(g_block(b, t, xl), sibling))
        left.wait_recv()
        second = same(g_block(b, t, xr, HALF, HALF), x_left)
        g_sib[b, t, 2].append(same(g_block(b, t, xr), sibling))
        g_far[b, t] = (first, second)

    def g_last(b, t):
        for h in range(2):
            g_far[b, t][h].wait_recv()
            g_sib[b, t, 3].append(same(g_block(b, t, xo, h * HALF, HALF), sibling))

    def keys_out(t):
        key, key_tan = norm(*rs_result(t), GB[cw, 1, 0:1, head_cols])
        rows = slice(t * TB, (t + 1) * TB)
        KB[slot_of(x, c), rows, 0:HD] = key
        KB[slot_of(x, c), rows, HD:] = key_tan
        g_start(0, t)

    def values_out(t):
        raw, tan = rs_result(4 + t)
        rows = slice(t * TB, (t + 1) * TB)
        VB[slot_of(x, c), rows, 0:HD] = raw.astype(BF16)
        VB[slot_of(x, c), rows, HD:] = tan.astype(BF16)
        g_start(1, t)

    wo_xopp = []

    def wo_relay_x(n):
        zz, right, left = wo_x[n]
        right.wait_recv()
        wo_xopp.append(same(wo_half(wo_block(zz, xl), 0), x_right))
        left.wait_recv()
        wo_xopp.append(same(wo_half(wo_block(zz, xr), 1), x_left))

    to_exp2 = HD ** -0.5 * 1.4426950408889634
    ln2 = 0.6931471805599453
    ROWS = 32

    def queries(s):
        gain = GB[cw, 0, 0:1, head_cols] * to_exp2
        query, query_tan = norm(*rs_result(2 + s), gain)
        QB[s, :, 0:HD] = query_tan
        QB[s, :, HD:] = query

    def arrived(b):
        for t in range(2):
            for j in range(4):
                wait(g_sib[b, t, j])

    def scores(s):
        MX[...] = jnp.full((TB, 128), -jnp.inf, F32)

        @pl.loop(0, 8)
        def _(j):
            keys = KB[j]
            cut = pl.ds(pl.multiple_of(j * 512, 512), 512)
            part = lax.dot_general(
                QB[s, :, HD:], keys[:, :HD], (((1,), (1,)), ((), ())), preferred_element_type=F32
            )
            S[:, cut] = part
            top = jnp.maximum(
                jnp.maximum(part[:, 0:128], part[:, 128:256]),
                jnp.maximum(part[:, 256:384], part[:, 384:512]),
            )
            MX[...] = jnp.maximum(MX[...], top)
            ST[:, cut] = lax.dot_general(
                QB[s], keys, (((1,), (1,)), ((), ())), preferred_element_type=F32
            )

    def softmax(s):
        @pl.loop(0, TB // ROWS)
        def _(i):
            at = pl.multiple_of(i * ROWS, ROWS)
            rows = pl.ds(at, ROWS)
            to = pl.ds(s * TB + at, ROWS)
            shift = jnp.max(MX[rows, :], axis=-1, keepdims=True)
            total = jnp.zeros((ROWS, 128), F32)
            inner = jnp.zeros((ROWS, 128), F32)
            for j in range(16):
                cut = slice(j * 256, (j + 1) * 256)
                e = jnp.exp2(S[rows, cut] - shift)
                EB[to, cut] = e.astype(BF16)
                es = e * ST[rows, cut]
                total += e[:, :128] + e[:, 128:]
                inner += es[:, :128] + es[:, 128:]
            total = jnp.sum(total, axis=-1, keepdims=True)
            mean = jnp.sum(inner, axis=-1, keepdims=True) / total
            LI[to, :] = jnp.broadcast_to(1.0 / total, (ROWS, HD))
            for j in range(16):
                cut = slice(j * 256, (j + 1) * 256)
                UB[to, cut] = (EB[to, cut].astype(F32) * (ST[rows, cut] - mean)).astype(BF16)

    def products(s):
        rows = slice(s * TB, (s + 1) * TB)
        AO[rows, :] = jnp.zeros((TB, 2 * HD), F32)
        AT[rows, :] = jnp.zeros((TB, HD), F32)

        @pl.loop(0, 8)
        def _(j):
            values = VB[j]
            cut = pl.ds(pl.multiple_of(j * 512, 512), 512)
            AO[rows, :] += jnp.dot(EB[rows, cut], values, preferred_element_type=F32)
            AT[rows, :] += jnp.dot(UB[rows, cut], values[:, :HD], preferred_element_type=F32)

    my_pair = zl * 8 + y * 2
    head_at = lax.rem(zh, 2)
    back = []

    def heads_back(s):
        rows = slice(s * TB, (s + 1) * TB)
        inv = LI[rows, :]
        primal = (AO[rows, :HD] * inv).astype(BF16)
        tangent = ((AO[rows, HD:] + AT[rows, :] * ln2) * inv).astype(BF16)
        for t in range(2):
            HS[s, t, 0:HALF, :] = primal[t * HALF:(t + 1) * HALF, :]
            HS[s, t, HALF:, :] = tangent[t * HALF:(t + 1) * HALF, :]
        for g in range(2):
            q = 2 * s + g
            target = HB.at[my_pair + cw, q, :, head_cols]
            for t in range(2):
                zeta = 2 * c + block_at[t]
                source = HS.at[s, t, pl.ds(g * HALF, HALF), :]
                copy = pltpu.make_async_remote_copy(
                    src_ref=source, dst_ref=target, send_sem=bssem.at[2 * q + t],
                    recv_sem=brsem.at[2 * q + head_at],
                    device_id=dev(zh_=zeta, c_=cw), device_id_type=pl.DeviceIdType.MESH,
                )
                stay = pltpu.make_async_copy(source, target, lsem.at[2 * q + t])
                here = zeta == zh

                @pl.when(here)
                def _(stay=stay):
                    stay.start()
                    stay.wait()

                @pl.when(jnp.logical_not(here))
                def _(copy=copy):
                    copy.start()

                back.append((copy, here))

    def hp(zz, yy):
        return zz * 8 + yy * 2 + c

    def h_part(p, q):
        return HB.at[p, q]

    def h_half(p, q, h):
        return HB.at[p, q, pl.ds(h * (HALF // 2), HALF // 2), :]

    h_own, h_two, h_opp, swapped = {}, {}, {}, {}

    def heads_start(s):
        for q in (2 * s, 2 * s + 1):
            for h in range(2):
                came = pltpu.make_async_remote_copy(
                    src_ref=HS.at[s, h, pl.ds(0, HALF), :],
                    dst_ref=HB.at[sq, q, :, pl.ds(h * HD, HD)],
                    send_sem=bssem.at[2 * q + h], recv_sem=brsem.at[2 * q + h],
                    device_id=sibling, device_id_type=pl.DeviceIdType.MESH,
                )

                @pl.when(2 * c + h != zh)
                def _(came=came):
                    came.wait_recv()

            mine = h_part(sq, q)
            across = same(mine, pair)
            h_own[q] = (same(mine, y_right), same(mine, y_left), across)

    def heads_pair(s):
        for q in (2 * s, 2 * s + 1):
            h_own[q][2].wait_recv()
            p = hp(nz, y)
            h_two[q] = (same(h_part(p, q), y_right), same(h_part(p, q), y_left))

    def heads_relay(s, zz, arrivals):
        for q in (2 * s, 2 * s + 1):
            right, left = arrivals[q][:2]
            right.wait_recv()
            first = same(h_half(hp(zz, yl), q, 0), y_right)
            left.wait_recv()
            second = same(h_half(hp(zz, yr), q, 1), y_left)
            h_opp.setdefault((s, zz is zl), []).extend([first, second])

    def heads_relay_own(s):
        heads_relay(s, zl, h_own)

    def heads_relay_two(s):
        heads_relay(s, nz, h_two)

    def multiply(s, zz, near, first=False):
        total = None if first else ACC[s]
        for yy in (y, yl, yr) if near else (yo,):
            p = hp(zz, yy)
            part = lax.dot_general(
                WOB[pl.ds(p - c, 2)].reshape(2 * F, 2 * HD),
                HB[p, 2 * s:2 * s + 2].reshape(TB, 2 * HD), (((1,), (1,)), ((), ())),
                preferred_element_type=F32,
            )
            total = part if total is None else total + part
        ACC[s] = total

    def multiply_far(s):
        for zz in (zl, nz):
            wait(h_opp[s, zz is zl])
            multiply(s, zz, False)
        XS[s] = ACC[s, pl.ds(pl.multiple_of(c * F, 64), F), :].astype(BF16)
        swapped[s] = send(XS.at[s], XR.at[s], sibling)

    def finish(s):
        swapped[s].wait_recv()
        mine = ACC[s, pl.ds(pl.multiple_of((1 - c) * F, 64), F), :] + XR[s].astype(F32)
        cut = slice(s * HALF, (s + 1) * HALF)
        out_ref[0:F, cut] = mine[:, 0:HALF].astype(BF16)
        out_ref[F:, cut] = mine[:, HALF:].astype(BF16)

    wait(a_own_opp)
    turn(0)
    wait(w_sib[0])
    rs_opposite(0)
    rs_direct(0)
    a_two_r.wait_recv()
    a_two_opp = [same(AB.at[zl, half_rows(yl, 0), :], y_right)]
    a_two_l.wait_recv()
    a_two_opp.append(same(AB.at[zl, half_rows(yr, 1), :], y_left))
    w_relay(2)
    w_start(1)
    rs_own(0)
    rs_summed(0)
    wait(a_two_opp)
    turn(1)
    rs_opposite(1)
    rs_direct(1)
    w_last(2)
    w_relay(1)
    wo_send_x(zh)
    wait(wo_z)
    wo_send_x(zf)
    wo_send_x(zr)
    wait(w_sib[2])
    rs_opposite(4)
    rs_summed(1)
    rs_direct(4)
    keys_out(0)
    rs_own(1)
    rs_opposite(5)
    w_last(1)
    rs_summed(4)
    rs_direct(5)
    keys_out(1)
    wait(w_sib[1])
    rs_opposite(2)
    g_relay(0, 0)
    rs_own(4)
    rs_summed(5)
    rs_direct(2)
    g_relay(0, 1)
    values_out(0)
    rs_own(5)
    rs_opposite(3)
    rs_own(2)
    rs_own(3)
    g_last(0, 0)
    g_last(0, 1)
    for n in range(3):
        wo_relay_x(n)
    rs_summed(2)
    rs_direct(3)
    values_out(1)
    g_relay(1, 0)
    rs_summed(3)
    wo_zopp = wo_relay_z()
    g_last(1, 0)
    g_relay(1, 1)
    queries(0)
    arrived(0)
    scores(0)
    g_last(1, 1)
    softmax(0)
    arrived(1)
    products(0)
    heads_back(0)
    queries(1)
    scores(1)
    heads_start(0)
    softmax(1)
    wait(wo_zopp)
    wo_send_x(zo)
    heads_pair(0)
    heads_relay_own(0)
    products(1)
    heads_back(1)
    heads_relay_two(0)
    heads_start(1)
    wo_relay_x(3)
    heads_pair(1)
    heads_relay_own(1)
    wait(wo_xopp)
    multiply(0, zl, True, first=True)
    multiply(0, nz, True)
    multiply_far(0)
    heads_relay_two(1)
    multiply(1, zl, True, first=True)
    multiply(1, nz, True)
    multiply_far(1)
    finish(0)
    finish(1)

    for copy in sent:
        copy.wait_send()
    for copy, here in back:
        @pl.when(jnp.logical_not(here))
        def _(copy=copy):
            copy.wait_send()


def shards(
    inputs, tangents, query_weight, key_weight, value_weight, query_gain, key_gain, out_weight
):
    vmem = pl.BlockSpec(memory_space=pltpu.VMEM)
    v = pltpu.VMEM
    both = pl.pallas_call(
        kernel,
        out_shape=jax.ShapeDtypeStruct((2 * F, TB), BF16),
        in_specs=[vmem] * 8,
        out_specs=vmem,
        scratch_shapes=[
            v((2, 3, 4 * F, 256), BF16),
            v((2, 2, 8, 256), F32),
            v((2, 4 * F, 512), BF16),
            v((2, 2, 2, HALF, 4 * F), BF16),
            v((16, F, 256), BF16),
            v((2 * TB, HD), F32),
            v((6, 3, 2, TB, HD), BF16),
            v((6, 3, 2, TB, HD), BF16),
            v((6, 2, TB, HD), F32),
            v((6, 2, TB, HD), F32),
            v((8, 512, 256), BF16),
            v((8, 512, 256), BF16),
            v((2, TB, 256), BF16),
            v((TB, TOKENS), F32),
            v((TB, TOKENS), F32),
            v((TB, 128), F32),
            v((2 * TB, HD), F32),
            v((2 * TB, TOKENS), BF16),
            v((2 * TB, TOKENS), BF16),
            v((2 * TB, 2 * HD), F32),
            v((2 * TB, HD), F32),
            v((2, 2, TB, HD), BF16),
            v((16, 4, HALF, 256), BF16),
            v((2, 2 * F, TB), F32),
            v((2, F, TB), BF16),
            v((2, F, TB), BF16),
            pltpu.SemaphoreType.DMA((N_SEMS,)),
            pltpu.SemaphoreType.DMA((N_SEMS,)),
            pltpu.SemaphoreType.DMA((8,)),
            pltpu.SemaphoreType.DMA((8,)),
            pltpu.SemaphoreType.DMA((8,)),
        ],
        compiler_params=pltpu.CompilerParams(
            collective_id=0, has_side_effects=True, vmem_limit_bytes=60 * 2**20
        ),
    )(
        inputs.T, tangents.T, query_weight, key_weight, value_weight,
        query_gain.reshape(1, 2 * HD), key_gain.reshape(1, 2 * HD), out_weight.T,
    )
    return both[:F].T, both[F:].T


def solution(mesh):
    in_specs = (
        P("seq", "dp"),
        P("seq", "dp"),
        P("dp", "seq"),
        P("dp", "seq"),
        P("dp", "seq"),
        P("seq"),
        P("seq"),
        P("seq", "dp"),
    )
    out_specs = (P("dp", "seq"), P("dp", "seq"))
    return jax.shard_map(shards, mesh=mesh, in_specs=in_specs, out_specs=out_specs, check_vma=False)
```

```python
import jax
import jax.numpy as jnp
from jax import lax
from jax.experimental import pallas as pl
from jax.experimental.pallas import tpu as pltpu
from jax.sharding import PartitionSpec as P

HD = 128
F = 320
TB = 256
TOKENS = 4096
HALF = 128
BF16 = jnp.bfloat16
F32 = jnp.float32
N_SEMS = 192


def kernel(
    in_ref, tin_ref, wq_ref, wk_ref, wv_ref, gq_ref, gk_ref, wo_ref,
    out_ref,
    WB, GB, AB, AN, WOB, PART, SB, RB, HOLD, OWN, KB, VB, QB, S, MX, LI, EB, AO, HS, HB, ACC, XS, XR,
    ssem, rsem, bssem, brsem, lsem,
):
    dp = lax.axis_index("dp")
    sq = lax.axis_index("seq")
    zh, x = lax.div(dp, 4), lax.rem(dp, 4)
    zl, y, c = lax.div(sq, 8), lax.rem(lax.div(sq, 2), 4), lax.rem(sq, 2)

    def dev(zh_=zh, x_=x, zl_=zl, y_=y, c_=c):
        return (zh_ * 4 + x_, zl_ * 8 + y_ * 2 + c_)

    def ring(v):
        return lax.rem(v + 1 + 2 * c, 4), lax.rem(v + 3 - 2 * c, 4), lax.rem(v + 2, 4)

    xr, xl, xo = ring(x)
    yr, yl, yo = ring(y)
    zr, zf, zo = ring(zh)
    x_right, x_left = dev(x_=xr), dev(x_=xl)
    y_right, y_left = dev(y_=yr), dev(y_=yl)
    z_right, z_left = dev(zh_=zr), dev(zh_=zf)
    nz = 1 - zl
    pair = dev(zl_=nz)
    sibling = dev(c_=1 - c)
    a_to = dev(x_=2 * lax.rem(y, 2) + c, zl_=1 - lax.div(y, 2), y_=x, c_=zl)
    a_from = dev(x_=y, zl_=c, y_=2 * nz + lax.div(x, 2), c_=lax.rem(x, 2))

    wo_row = 2 * lax.div(sq, 2) + 1 - lax.rem(dp, 2)
    wo_to = (wo_row, 2 * lax.div(dp, 2) + c)
    wo_from = (
        2 * lax.div(sq, 2) + 1 - lax.rem(dp, 2), 2 * lax.div(dp, 2) + c
    )

    barrier = pltpu.get_barrier_semaphore()
    greet = [x_right, x_left, y_right, y_left, pair, a_to, a_from, wo_to, wo_from]
    for k in range(1, 8):
        peer = lax.rem(zh * 2 + c + k, 8)
        greet.append(dev(zh_=lax.div(peer, 2), c_=lax.rem(peer, 2)))
    for d in greet:
        pl.semaphore_signal(barrier, inc=1, device_id=d, device_id_type=pl.DeviceIdType.MESH)

    def rows_of(xx):
        return pl.ds(pl.multiple_of(xx * F, 64), F)

    def half_rows(xx, h):
        return pl.ds(pl.multiple_of(xx * F + h * (F // 2), 32), F // 2)

    WB[c, 0, rows_of(x), :] = wk_ref[...]
    WB[c, 1, rows_of(x), :] = wq_ref[...]
    WB[c, 2, rows_of(x), :] = wv_ref[...]
    GB[c, 0] = jnp.broadcast_to(gq_ref[...], (8, 2 * HD))
    GB[c, 1] = jnp.broadcast_to(gk_ref[...], (8, 2 * HD))

    pl.semaphore_wait(barrier, len(greet))

    sent = []

    def send(src, dst, device):
        k = len(sent)
        copy = pltpu.make_async_remote_copy(
            src_ref=src, dst_ref=dst, send_sem=ssem.at[k], recv_sem=rsem.at[k],
            device_id=device, device_id_type=pl.DeviceIdType.MESH,
        )
        copy.start()
        sent.append(copy)
        return copy

    def same(ref, device):
        return send(ref, ref, device)

    def wait(copies):
        for copy in copies:
            copy.wait_recv()

    def w_piece(w, xx):
        return WB.at[c, w, rows_of(xx), :]

    def w_half(w, xx, h):
        return WB.at[c, w, half_rows(xx, h), :]

    w_near, w_far, w_sib = {}, {}, {0: [], 1: [], 2: []}

    def w_start(w):
        w_near[w] = (same(w_piece(w, x), x_right), same(w_piece(w, x), x_left))
        w_sib[w].append(same(w_piece(w, x), sibling))

    def w_relay(w):
        right, left = w_near[w]
        right.wait_recv()
        a = same(w_half(w, xl, 0), x_right)
        w_sib[w].append(same(w_piece(w, xl), sibling))
        left.wait_recv()
        b = same(w_half(w, xr, 1), x_left)
        w_sib[w].append(same(w_piece(w, xr), sibling))
        w_far[w] = (a, b)

    def w_last(w):
        for h in range(2):
            w_far[w][h].wait_recv()
            w_sib[w].append(same(w_half(w, xo, h), sibling))

    def cols_of(g):
        return pl.ds(g * TB, TB)

    def a_piece(z, yy, g):
        return AB.at[z, rows_of(yy), cols_of(g)]

    def a_half(z, yy, h, g):
        return AB.at[z, half_rows(yy, h), cols_of(g)]

    a_perm = [
        send(ref, AB.at[lax.div(y, 2), rows_of(x), cols_of(g)], a_to)
        for g, ref in enumerate((in_ref, tin_ref))
    ]

    a_own, a_pair = [], []
    for g in range(2):
        a_perm[g].wait_recv()
        own = a_piece(nz, y, g)
        a_own.append((same(own, y_right), same(own, y_left)))
        a_pair.append(same(own, pair))
        if g == 0:
            wo_perm = send(wo_ref, WOB.at[wo_row], wo_to)
            w_start(0)
            w_sib[0].append(same(GB.at[c], sibling))

    def wo_block(zz, xx):
        return zz * 4 + xx

    def wo_half(b, h):
        return WOB.at[b, pl.ds(h * (F // 2), F // 2), :]

    w_relay(0)
    a_own_opp = []
    for g, (right, left) in enumerate(a_own):
        right.wait_recv()
        a_own_opp.append(same(a_half(nz, yl, 0, g), y_right))
        left.wait_recv()
        a_own_opp.append(same(a_half(nz, yr, 1, g), y_left))

    wait(a_pair)
    two = AB.at[zl, rows_of(y), :]
    a_two_r, a_two_l = same(two, y_right), same(two, y_left)

    def wo_start_z():
        block = WOB.at[wo_block(zh, x)]
        return same(block, z_right), same(block, z_left)

    def wo_relay_z():
        return [
            same(wo_half(wo_block(zf, x), 0), z_right),
            same(wo_half(wo_block(zr, x), 1), z_left),
        ]

    w_start(2)
    wo_perm.wait_recv()
    wo_z = wo_start_z()
    w_last(0)

    wo_x = []

    def wo_send_x(zz):
        b = WOB.at[wo_block(zz, x)]
        wo_x.append((zz, same(b, x_right), same(b, x_left)))

    block_at = (nz, zl)

    def turn(t, h):
        @pl.loop(0, 5)
        def _(i):
            cut = pl.ds(pl.multiple_of(i * 256, 256), 256)
            piece = AB[block_at[t], cut, h * TB:(h + 1) * TB].T
            for s in range(2):
                AN[t, h, s, :, cut] = piece[s * HALF:(s + 1) * HALF, :]

    def tile(kind, k):
        d = (zh, zr, zo, zf)[k]
        cw = lax.div(d, 2)
        cols = pl.ds(pl.multiple_of(lax.rem(d, 2) * HD, HD), HD)
        queries = kind // 2 == 1
        PART[...] = jnp.zeros((2 * TB, HD), F32)

        @pl.loop(0, 5)
        def _(i):
            deep = pl.ds(pl.multiple_of(i * 256, 256), 256)
            tokens = AN[:, :, kind % 2, :, deep] if queries else AN[kind % 2, :, :, :, deep]
            PART[...] += jnp.dot(
                tokens.reshape(2 * TB, 256), WB[cw, kind // 2, deep, cols],
                preferred_element_type=F32,
            )

        part = PART[...].reshape(2, 2, HALF, HD)
        return [(part[:, h] if queries else part[h]).reshape(TB, HD) for h in range(2)]

    relay, direct, summed = {}, {}, {}

    def rs_send(kind, slot, h, part, to):
        SB[kind, slot, h] = part.astype(BF16)
        return send(SB.at[kind, slot, h], RB.at[kind, slot, h], to)

    def rs_opposite(kind):
        part = tile(kind, 2)
        for h in range(2):
            relay[kind, h] = rs_send(kind, 0, h, part[h], z_right if h == 0 else z_left)

    def rs_direct(kind):
        for slot, k, h, to in ((1, 1, 1, z_right), (2, 3, 0, z_left)):
            part = tile(kind, k)
            direct[kind, slot] = rs_send(kind, slot, h, part[h], to)
            HOLD[kind, 1 - h] = part[1 - h]

    def rs_summed(kind):
        for slot, h, to in ((1, 0, z_right), (2, 1, z_left)):
            relay[kind, h].wait_recv()
            part = HOLD[kind, h] + RB[kind, 0, h].astype(F32)
            summed[kind, slot] = rs_send(kind, slot, h, part, to)

    def rs_own(kind):
        part = tile(kind, 0)
        for h in range(2):
            OWN[kind, h] = part[h]

    def rs_result(kind):
        for slot in (1, 2):
            direct[kind, slot].wait_recv()
            summed[kind, slot].wait_recv()
        return [
            OWN[kind, h] + RB[kind, 1, h].astype(F32) + RB[kind, 2, h].astype(F32)
            for h in range(2)
        ]

    cw = lax.div(zh, 2)
    head_cols = pl.ds(pl.multiple_of(lax.rem(zh, 2) * HD, HD), HD)

    def norm(raw, tan, gain):
        ms = jnp.mean(raw * raw, axis=-1, keepdims=True)
        inv = lax.rsqrt(ms + 1e-06)
        inner = jnp.mean(raw * tan, axis=-1, keepdims=True)
        normed = gain * raw * inv
        normed_tan = gain * inv * (tan - raw * inner * inv * inv)
        return normed.astype(BF16), normed_tan.astype(BF16)

    def slot_of(xx, cc):
        return xx * 2 + cc

    g_near, g_far = {}, {}
    g_sib = {(b, t, j): [] for b in range(2) for t in range(2) for j in range(4)}

    def g_block(b, t, xx, rows=0, count=TB):
        return (KB, VB)[b].at[slot_of(xx, c), pl.ds(t * TB + rows, count), :]

    def g_start(b, t):
        block = g_block(b, t, x)
        g_near[b, t] = (same(block, x_right), same(block, x_left))
        g_sib[b, t, 0].append(same(block, sibling))

    def g_relay(b, t):
        right, left = g_near[b, t]
        right.wait_recv()
        first = same(g_block(b, t, xl, 0, HALF), x_right)
        g_sib[b, t, 1].append(same(g_block(b, t, xl), sibling))
        left.wait_recv()
        second = same(g_block(b, t, xr, HALF, HALF), x_left)
        g_sib[b, t, 2].append(same(g_block(b, t, xr), sibling))
        g_far[b, t] = (first, second)

    def g_last(b, t):
        for h in range(2):
            g_far[b, t][h].wait_recv()
            g_sib[b, t, 3].append(same(g_block(b, t, xo, h * HALF, HALF), sibling))

    def keys_out(t):
        key, key_tan = norm(*rs_result(t), GB[cw, 1, 0:1, head_cols])
        rows = slice(t * TB, (t + 1) * TB)
        KB[slot_of(x, c), rows, 0:HD] = key
        KB[slot_of(x, c), rows, HD:] = key_tan
        g_start(0, t)

    def values_out(t):
        raw, tan = rs_result(4 + t)
        rows = slice(t * TB, (t + 1) * TB)
        VB[slot_of(x, c), rows, 0:HD] = raw.astype(BF16)
        VB[slot_of(x, c), rows, HD:] = tan.astype(BF16)
        g_start(1, t)

    wo_xopp = []

    def wo_relay_x(n):
        zz, right, left = wo_x[n]
        right.wait_recv()
        wo_xopp.append(same(wo_half(wo_block(zz, xl), 0), x_right))
        left.wait_recv()
        wo_xopp.append(same(wo_half(wo_block(zz, xr), 1), x_left))

    to_exp2 = HD ** -0.5 * 1.4426950408889634
    ln2 = 0.6931471805599453
    ROWS = 32

    def queries(s):
        gain = GB[cw, 0, 0:1, head_cols] * to_exp2
        query, query_tan = norm(*rs_result(2 + s), gain)
        QB[0:TB, 0:HD] = query_tan
        QB[0:TB, HD:] = query
        QB[TB:, 0:HD] = query
        QB[TB:, HD:] = jnp.zeros((TB, HD), BF16)

    def arrived(b):
        for t in range(2):
            for j in range(4):
                wait(g_sib[b, t, j])

    def scores(s):
        MX[...] = jnp.full((TB, 128), -jnp.inf, F32)

        @pl.loop(0, 8)
        def _(j):
            cut = pl.ds(pl.multiple_of(j * 512, 512), 512)
            part = lax.dot_general(
                QB[...], KB[j], (((1,), (1,)), ((), ())), preferred_element_type=F32
            )
            S[:, cut] = part
            part = part[TB:]
            top = jnp.maximum(
                jnp.maximum(part[:, 0:128], part[:, 128:256]),
                jnp.maximum(part[:, 256:384], part[:, 384:512]),
            )
            MX[...] = jnp.maximum(MX[...], top)

    def softmax(s):
        @pl.loop(0, TB // ROWS)
        def _(i):
            at = pl.multiple_of(i * ROWS, ROWS)
            rows = pl.ds(at, ROWS)
            raw = pl.ds(TB + at, ROWS)
            shift = jnp.max(MX[rows, :], axis=-1, keepdims=True)
            total = jnp.zeros((ROWS, 128), F32)
            inner = jnp.zeros((ROWS, 128), F32)
            for j in range(16):
                cut = slice(j * 256, (j + 1) * 256)
                e = jnp.exp2(S[raw, cut] - shift)
                EB[rows, cut] = e.astype(BF16)
                es = e * S[rows, cut]
                total += e[:, :128] + e[:, 128:]
                inner += es[:, :128] + es[:, 128:]
            total = jnp.sum(total, axis=-1, keepdims=True)
            mean = jnp.sum(inner, axis=-1, keepdims=True) / total
            LI[rows, :] = jnp.broadcast_to(1.0 / total, (ROWS, HD))
            for j in range(16):
                cut = slice(j * 256, (j + 1) * 256)
                EB[raw, cut] = (EB[rows, cut].astype(F32) * (S[rows, cut] - mean)).astype(BF16)

    def products(s):
        AO[...] = jnp.zeros((2 * TB, 2 * HD), F32)

        @pl.loop(0, 8)
        def _(j):
            cut = pl.ds(pl.multiple_of(j * 512, 512), 512)
            AO[...] += jnp.dot(EB[:, cut], VB[j], preferred_element_type=F32)

    my_pair = zl * 8 + y * 2
    head_at = lax.rem(zh, 2)
    back = []

    def heads_back(s):
        inv = LI[...]
        primal = (AO[0:TB, :HD] * inv).astype(BF16)
        tangent = ((AO[0:TB, HD:] + AO[TB:, :HD] * ln2) * inv).astype(BF16)
        for t in range(2):
            HS[s, t, 0:HALF, :] = primal[t * HALF:(t + 1) * HALF, :]
            HS[s, t, HALF:, :] = tangent[t * HALF:(t + 1) * HALF, :]
        for g in range(2):
            q = 2 * s + g
            target = HB.at[my_pair + cw, q, :, head_cols]
            for t in range(2):
                zeta = 2 * c + block_at[t]
                source = HS.at[s, t, pl.ds(g * HALF, HALF), :]
                copy = pltpu.make_async_remote_copy(
                    src_ref=source, dst_ref=target, send_sem=bssem.at[2 * q + t],
                    recv_sem=brsem.at[2 * q + head_at],
                    device_id=dev(zh_=zeta, c_=cw), device_id_type=pl.DeviceIdType.MESH,
                )
                stay = pltpu.make_async_copy(source, target, lsem.at[2 * q + t])
                here = zeta == zh

                @pl.when(here)
                def _(stay=stay):
                    stay.start()
                    stay.wait()

                @pl.when(jnp.logical_not(here))
                def _(copy=copy):
                    copy.start()

                back.append((copy, here))

    def hp(zz, yy):
        return zz * 8 + yy * 2 + c

    def h_part(p, q):
        return HB.at[p, q]

    def h_half(p, q, h):
        return HB.at[p, q, pl.ds(h * (HALF // 2), HALF // 2), :]

    h_own, h_two, h_opp, swapped = {}, {}, {}, {}

    def heads_start(s):
        for q in (2 * s, 2 * s + 1):
            for h in range(2):
                came = pltpu.make_async_remote_copy(
                    src_ref=HS.at[s, h, pl.ds(0, HALF), :],
                    dst_ref=HB.at[sq, q, :, pl.ds(h * HD, HD)],
                    send_sem=bssem.at[2 * q + h], recv_sem=brsem.at[2 * q + h],
                    device_id=sibling, device_id_type=pl.DeviceIdType.MESH,
                )

                @pl.when(2 * c + h != zh)
                def _(came=came):
                    came.wait_recv()

            mine = h_part(sq, q)
            across = same(mine, pair)
            h_own[q] = (same(mine, y_right), same(mine, y_left), across)

    def heads_pair(s):
        for q in (2 * s, 2 * s + 1):
            h_own[q][2].wait_recv()
            p = hp(nz, y)
            h_two[q] = (same(h_part(p, q), y_right), same(h_part(p, q), y_left))

    def heads_relay(s, zz, arrivals):
        for q in (2 * s, 2 * s + 1):
            right, left = arrivals[q][:2]
            right.wait_recv()
            first = same(h_half(hp(zz, yl), q, 0), y_right)
            left.wait_recv()
            second = same(h_half(hp(zz, yr), q, 1), y_left)
            h_opp.setdefault((s, zz is zl), []).extend([first, second])

    def heads_relay_own(s):
        heads_relay(s, zl, h_own)

    def heads_relay_two(s):
        heads_relay(s, nz, h_two)

    def multiply(s, zz, near, first=False):
        total = None if first else ACC[s]
        for yy in (y, yl, yr) if near else (yo,):
            p = hp(zz, yy)
            part = lax.dot_general(
                WOB[pl.ds(p - c, 2)].reshape(2 * F, 2 * HD),
                HB[p, 2 * s:2 * s + 2].reshape(TB, 2 * HD), (((1,), (1,)), ((), ())),
                preferred_element_type=F32,
            )
            total = part if total is None else total + part
        ACC[s] = total

    def multiply_far(s):
        for zz in (zl, nz):
            wait(h_opp[s, zz is zl])
            multiply(s, zz, False)
        XS[s] = ACC[s, pl.ds(pl.multiple_of(c * F, 64), F), :].astype(BF16)
        swapped[s] = send(XS.at[s], XR.at[s], sibling)

    def finish(s):
        swapped[s].wait_recv()
        mine = ACC[s, pl.ds(pl.multiple_of((1 - c) * F, 64), F), :] + XR[s].astype(F32)
        cut = slice(s * HALF, (s + 1) * HALF)
        out_ref[0:F, cut] = mine[:, 0:HALF].astype(BF16)
        out_ref[F:, cut] = mine[:, HALF:].astype(BF16)

    for h in range(2):
        wait(a_own_opp[2 * h:2 * h + 2])
        turn(0, h)
    wait(w_sib[0])
    rs_opposite(0)
    rs_direct(0)
    a_two_r.wait_recv()
    a_two_opp = [same(AB.at[zl, half_rows(yl, 0), :], y_right)]
    a_two_l.wait_recv()
    a_two_opp.append(same(AB.at[zl, half_rows(yr, 1), :], y_left))
    w_relay(2)
    w_start(1)
    rs_own(0)
    rs_summed(0)
    wait(a_two_opp)
    turn(1, 0)
    turn(1, 1)
    rs_opposite(1)
    rs_direct(1)
    w_last(2)
    w_relay(1)
    wo_send_x(zh)
    wait(wo_z)
    wo_send_x(zf)
    wo_send_x(zr)
    wait(w_sib[2])
    rs_opposite(4)
    rs_summed(1)
    rs_direct(4)
    keys_out(0)
    rs_own(1)
    rs_opposite(5)
    w_last(1)
    rs_summed(4)
    rs_direct(5)
    keys_out(1)
    wait(w_sib[1])
    rs_opposite(2)
    g_relay(0, 0)
    rs_own(4)
    rs_summed(5)
    rs_direct(2)
    g_relay(0, 1)
    values_out(0)
    rs_own(5)
    rs_opposite(3)
    rs_own(2)
    rs_own(3)
    g_last(0, 0)
    g_last(0, 1)
    for n in range(3):
        wo_relay_x(n)
    rs_summed(2)
    rs_direct(3)
    values_out(1)
    g_relay(1, 0)
    rs_summed(3)
    wo_zopp = wo_relay_z()
    g_last(1, 0)
    g_relay(1, 1)
    queries(0)
    arrived(0)
    scores(0)
    g_last(1, 1)
    softmax(0)
    arrived(1)
    products(0)
    heads_back(0)
    queries(1)
    scores(1)
    heads_start(0)
    softmax(1)
    wait(wo_zopp)
    wo_send_x(zo)
    heads_pair(0)
    heads_relay_own(0)
    products(1)
    heads_back(1)
    heads_relay_two(0)
    heads_start(1)
    wo_relay_x(3)
    heads_pair(1)
    heads_relay_own(1)
    wait(wo_xopp)
    multiply(0, zl, True, first=True)
    multiply(0, nz, True)
    multiply_far(0)
    heads_relay_two(1)
    multiply(1, zl, True, first=True)
    multiply(1, nz, True)
    multiply_far(1)
    finish(0)
    finish(1)

    for copy in sent:
        copy.wait_send()
    for copy, here in back:
        @pl.when(jnp.logical_not(here))
        def _(copy=copy):
            copy.wait_send()


def shards(
    inputs, tangents, query_weight, key_weight, value_weight, query_gain, key_gain, out_weight
):
    vmem = pl.BlockSpec(memory_space=pltpu.VMEM)
    v = pltpu.VMEM
    both = pl.pallas_call(
        kernel,
        out_shape=jax.ShapeDtypeStruct((2 * F, TB), BF16),
        in_specs=[vmem] * 8,
        out_specs=vmem,
        scratch_shapes=[
            v((2, 3, 4 * F, 256), BF16),
            v((2, 2, 8, 256), F32),
            v((2, 4 * F, 512), BF16),
            v((2, 2, 2, HALF, 4 * F), BF16),
            v((16, F, 256), BF16),
            v((2 * TB, HD), F32),
            v((6, 3, 2, TB, HD), BF16),
            v((6, 3, 2, TB, HD), BF16),
            v((6, 2, TB, HD), F32),
            v((6, 2, TB, HD), F32),
            v((8, 512, 256), BF16),
            v((8, 512, 256), BF16),
            v((2 * TB, 256), BF16),
            v((2 * TB, TOKENS), F32),
            v((TB, 128), F32),
            v((TB, HD), F32),
            v((2 * TB, TOKENS), BF16),
            v((2 * TB, 2 * HD), F32),
            v((2, 2, TB, HD), BF16),
            v((16, 4, HALF, 256), BF16),
            v((2, 2 * F, TB), F32),
            v((2, F, TB), BF16),
            v((2, F, TB), BF16),
            pltpu.SemaphoreType.DMA((N_SEMS,)),
            pltpu.SemaphoreType.DMA((N_SEMS,)),
            pltpu.SemaphoreType.DMA((8,)),
            pltpu.SemaphoreType.DMA((8,)),
            pltpu.SemaphoreType.DMA((8,)),
        ],
        compiler_params=pltpu.CompilerParams(
            collective_id=0, has_side_effects=True, vmem_limit_bytes=60 * 2**20
        ),
    )(
        inputs.T, tangents.T, query_weight, key_weight, value_weight,
        query_gain.reshape(1, 2 * HD), key_gain.reshape(1, 2 * HD), out_weight.T,
    )
    return both[:F].T, both[F:].T


def solution(mesh):
    in_specs = (
        P("seq", "dp"),
        P("seq", "dp"),
        P("dp", "seq"),
        P("dp", "seq"),
        P("dp", "seq"),
        P("seq"),
        P("seq"),
        P("seq", "dp"),
    )
    out_specs = (P("dp", "seq"), P("dp", "seq"))
    return jax.shard_map(shards, mesh=mesh, in_specs=in_specs, out_specs=out_specs, check_vma=False)
```

```python
import jax
import jax.numpy as jnp
from jax import lax
from jax.experimental import pallas as pl
from jax.experimental.pallas import tpu as pltpu
from jax.sharding import PartitionSpec as P

HD = 128
F = 320
TB = 256
TOKENS = 4096
HALF = 128
BF16 = jnp.bfloat16
F32 = jnp.float32
N_SEMS = 208


def kernel(
    in_ref, tin_ref, wq_ref, wk_ref, wv_ref, gq_ref, gk_ref, wo_ref,
    out_ref,
    WB, GB, AB, AN, WOB, PART, SB, RB, HOLD, OWN, KB, VB, QB, S, MX, LI, EB, AO, HS, HB, ACC, XS, XR,
    ssem, rsem, bssem, brsem, lsem,
):
    dp = lax.axis_index("dp")
    sq = lax.axis_index("seq")
    zh, x = lax.div(dp, 4), lax.rem(dp, 4)
    zl, y, c = lax.div(sq, 8), lax.rem(lax.div(sq, 2), 4), lax.rem(sq, 2)

    def dev(zh_=zh, x_=x, zl_=zl, y_=y, c_=c):
        return (zh_ * 4 + x_, zl_ * 8 + y_ * 2 + c_)

    def ring(v):
        return lax.rem(v + 1 + 2 * c, 4), lax.rem(v + 3 - 2 * c, 4), lax.rem(v + 2, 4)

    xr, xl, xo = ring(x)
    yr, yl, yo = ring(y)
    zr, zf, zo = ring(zh)
    x_right, x_left = dev(x_=xr), dev(x_=xl)
    y_right, y_left = dev(y_=yr), dev(y_=yl)
    z_right, z_left = dev(zh_=zr), dev(zh_=zf)
    nz = 1 - zl
    pair = dev(zl_=nz)
    sibling = dev(c_=1 - c)
    a_to = dev(x_=2 * lax.rem(y, 2) + c, zl_=1 - lax.div(y, 2), y_=x, c_=zl)
    a_from = dev(x_=y, zl_=c, y_=2 * nz + lax.div(x, 2), c_=lax.rem(x, 2))

    wo_row = 2 * lax.div(sq, 2) + 1 - lax.rem(dp, 2)
    wo_to = (wo_row, 2 * lax.div(dp, 2) + c)
    wo_from = (
        2 * lax.div(sq, 2) + 1 - lax.rem(dp, 2), 2 * lax.div(dp, 2) + c
    )

    barrier = pltpu.get_barrier_semaphore()
    greet = [x_right, x_left, y_right, y_left, pair, a_to, a_from, wo_to, wo_from]
    for k in range(1, 8):
        peer = lax.rem(zh * 2 + c + k, 8)
        greet.append(dev(zh_=lax.div(peer, 2), c_=lax.rem(peer, 2)))
    for d in greet:
        pl.semaphore_signal(barrier, inc=1, device_id=d, device_id_type=pl.DeviceIdType.MESH)

    def rows_of(xx):
        return pl.ds(pl.multiple_of(xx * F, 64), F)

    def half_rows(xx, h):
        return pl.ds(pl.multiple_of(xx * F + h * (F // 2), 32), F // 2)

    WB[c, 0, rows_of(x), :] = wk_ref[...]
    WB[c, 1, rows_of(x), :] = wq_ref[...]
    WB[c, 2, rows_of(x), :] = wv_ref[...]
    GB[c, 0] = jnp.broadcast_to(gq_ref[...], (8, 2 * HD))
    GB[c, 1] = jnp.broadcast_to(gk_ref[...], (8, 2 * HD))

    pl.semaphore_wait(barrier, len(greet))

    sent = []

    def send(src, dst, device):
        k = len(sent)
        copy = pltpu.make_async_remote_copy(
            src_ref=src, dst_ref=dst, send_sem=ssem.at[k], recv_sem=rsem.at[k],
            device_id=device, device_id_type=pl.DeviceIdType.MESH,
        )
        copy.start()
        sent.append(copy)
        return copy

    def same(ref, device):
        return send(ref, ref, device)

    def wait(copies):
        for copy in copies:
            copy.wait_recv()

    def w_piece(w, xx):
        return WB.at[c, w, rows_of(xx), :]

    def w_half(w, xx, h):
        return WB.at[c, w, half_rows(xx, h), :]

    w_near, w_far, w_sib = {}, {}, {0: [], 1: [], 2: []}

    def w_start(w):
        w_near[w] = (same(w_piece(w, x), x_right), same(w_piece(w, x), x_left))
        w_sib[w].append(same(w_piece(w, x), sibling))

    def w_relay(w):
        right, left = w_near[w]
        right.wait_recv()
        a = same(w_half(w, xl, 0), x_right)
        w_sib[w].append(same(w_piece(w, xl), sibling))
        left.wait_recv()
        b = same(w_half(w, xr, 1), x_left)
        w_sib[w].append(same(w_piece(w, xr), sibling))
        w_far[w] = (a, b)

    def w_last(w):
        for h in range(2):
            w_far[w][h].wait_recv()
            w_sib[w].append(same(w_half(w, xo, h), sibling))

    def cols_of(g):
        return pl.ds(g * TB, TB)

    def a_chunk(z, yy, k):
        return AB.at[z, half_rows(yy, k % 2), cols_of(k // 2)]

    a_perm = []
    for k in range(4):
        ref = (in_ref, tin_ref)[k // 2].at[pl.ds((k % 2) * (F // 2), F // 2), :]
        a_perm.append(
            send(ref, AB.at[lax.div(y, 2), half_rows(x, k % 2), cols_of(k // 2)], a_to)
        )

    a_own, a_pair, a_two, a_own_opp, a_two_opp = [], [], [], [], []

    def a_start(k):
        a_perm[k].wait_recv()
        own = a_chunk(nz, y, k)
        a_own.append((same(own, y_right), same(own, y_left)))
        a_pair.append(same(own, pair))

    def a_relay(z, arrivals, k):
        arrivals[k][k % 2].wait_recv()
        yy, to = ((yl, y_right), (yr, y_left))[k % 2]
        return same(a_chunk(z, yy, k), to)

    def wo_block(zz, xx):
        return zz * 4 + xx

    def wo_half(b, h):
        return WOB.at[b, pl.ds(h * (F // 2), F // 2), :]

    a_start(0)
    a_start(1)
    wo_perm = send(wo_ref, WOB.at[wo_row], wo_to)
    w_start(0)
    w_sib[0].append(same(GB.at[c], sibling))
    a_start(2)
    a_own_opp.append(a_relay(nz, a_own, 0))
    a_start(3)
    a_own_opp.append(a_relay(nz, a_own, 1))
    w_relay(0)
    a_own_opp.append(a_relay(nz, a_own, 2))
    a_own_opp.append(a_relay(nz, a_own, 3))
    for k in range(4):
        a_pair[k].wait_recv()
        two = a_chunk(zl, y, k)
        a_two.append((same(two, y_right), same(two, y_left)))

    def wo_start_z():
        block = WOB.at[wo_block(zh, x)]
        return same(block, z_right), same(block, z_left)

    def wo_relay_z():
        return [
            same(wo_half(wo_block(zf, x), 0), z_right),
            same(wo_half(wo_block(zr, x), 1), z_left),
        ]

    w_start(2)
    wo_perm.wait_recv()
    wo_z = wo_start_z()
    w_last(0)

    wo_x = []

    def wo_send_x(zz):
        b = WOB.at[wo_block(zz, x)]
        wo_x.append((zz, same(b, x_right), same(b, x_left)))

    block_at = (nz, zl)

    def turn(t, h):
        @pl.loop(0, 5)
        def _(i):
            cut = pl.ds(pl.multiple_of(i * 256, 256), 256)
            piece = AB[block_at[t], cut, h * TB:(h + 1) * TB].T
            for s in range(2):
                AN[t, h, s, :, cut] = piece[s * HALF:(s + 1) * HALF, :]

    def tile(kind, k):
        d = (zh, zr, zo, zf)[k]
        cw = lax.div(d, 2)
        cols = pl.ds(pl.multiple_of(lax.rem(d, 2) * HD, HD), HD)
        queries = kind // 2 == 1
        PART[...] = jnp.zeros((2 * TB, HD), F32)

        @pl.loop(0, 5)
        def _(i):
            deep = pl.ds(pl.multiple_of(i * 256, 256), 256)
            tokens = AN[:, :, kind % 2, :, deep] if queries else AN[kind % 2, :, :, :, deep]
            PART[...] += jnp.dot(
                tokens.reshape(2 * TB, 256), WB[cw, kind // 2, deep, cols],
                preferred_element_type=F32,
            )

        part = PART[...].reshape(2, 2, HALF, HD)
        return [(part[:, h] if queries else part[h]).reshape(TB, HD) for h in range(2)]

    relay, direct, summed = {}, {}, {}

    def rs_send(kind, slot, h, part, to):
        SB[kind, slot, h] = part.astype(BF16)
        return send(SB.at[kind, slot, h], RB.at[kind, slot, h], to)

    def rs_opposite(kind):
        part = tile(kind, 2)
        for h in range(2):
            relay[kind, h] = rs_send(kind, 0, h, part[h], z_right if h == 0 else z_left)

    def rs_direct(kind):
        for slot, k, h, to in ((1, 1, 1, z_right), (2, 3, 0, z_left)):
            part = tile(kind, k)
            direct[kind, slot] = rs_send(kind, slot, h, part[h], to)
            HOLD[kind, 1 - h] = part[1 - h]

    def rs_summed(kind):
        for slot, h, to in ((1, 0, z_right), (2, 1, z_left)):
            relay[kind, h].wait_recv()
            part = HOLD[kind, h] + RB[kind, 0, h].astype(F32)
            summed[kind, slot] = rs_send(kind, slot, h, part, to)

    def rs_own(kind):
        part = tile(kind, 0)
        for h in range(2):
            OWN[kind, h] = part[h]

    def rs_result(kind):
        for slot in (1, 2):
            direct[kind, slot].wait_recv()
            summed[kind, slot].wait_recv()
        return [
            OWN[kind, h] + RB[kind, 1, h].astype(F32) + RB[kind, 2, h].astype(F32)
            for h in range(2)
        ]

    cw = lax.div(zh, 2)
    head_cols = pl.ds(pl.multiple_of(lax.rem(zh, 2) * HD, HD), HD)

    def norm(raw, tan, gain):
        ms = jnp.mean(raw * raw, axis=-1, keepdims=True)
        inv = lax.rsqrt(ms + 1e-06)
        inner = jnp.mean(raw * tan, axis=-1, keepdims=True)
        normed = gain * raw * inv
        normed_tan = gain * inv * (tan - raw * inner * inv * inv)
        return normed.astype(BF16), normed_tan.astype(BF16)

    def slot_of(xx, cc):
        return xx * 2 + cc

    g_near, g_far = {}, {}
    g_sib = {(b, t, j): [] for b in range(2) for t in range(2) for j in range(4)}

    def g_block(b, t, xx, rows=0, count=TB):
        return (KB, VB)[b].at[slot_of(xx, c), pl.ds(t * TB + rows, count), :]

    def g_start(b, t):
        block = g_block(b, t, x)
        g_near[b, t] = (same(block, x_right), same(block, x_left))
        g_sib[b, t, 0].append(same(block, sibling))

    def g_relay(b, t):
        right, left = g_near[b, t]
        right.wait_recv()
        first = same(g_block(b, t, xl, 0, HALF), x_right)
        g_sib[b, t, 1].append(same(g_block(b, t, xl), sibling))
        left.wait_recv()
        second = same(g_block(b, t, xr, HALF, HALF), x_left)
        g_sib[b, t, 2].append(same(g_block(b, t, xr), sibling))
        g_far[b, t] = (first, second)

    def g_last(b, t):
        for h in range(2):
            g_far[b, t][h].wait_recv()
            g_sib[b, t, 3].append(same(g_block(b, t, xo, h * HALF, HALF), sibling))

    def keys_out(t):
        key, key_tan = norm(*rs_result(t), GB[cw, 1, 0:1, head_cols])
        rows = slice(t * TB, (t + 1) * TB)
        KB[slot_of(x, c), rows, 0:HD] = key
        KB[slot_of(x, c), rows, HD:] = key_tan
        g_start(0, t)

    def values_out(t):
        raw, tan = rs_result(4 + t)
        rows = slice(t * TB, (t + 1) * TB)
        VB[slot_of(x, c), rows, 0:HD] = raw.astype(BF16)
        VB[slot_of(x, c), rows, HD:] = tan.astype(BF16)
        g_start(1, t)

    wo_xopp = []

    def wo_relay_x(n):
        zz, right, left = wo_x[n]
        right.wait_recv()
        wo_xopp.append(same(wo_half(wo_block(zz, xl), 0), x_right))
        left.wait_recv()
        wo_xopp.append(same(wo_half(wo_block(zz, xr), 1), x_left))

    to_exp2 = HD ** -0.5 * 1.4426950408889634
    ln2 = 0.6931471805599453
    ROWS = 32

    def queries(s):
        gain = GB[cw, 0, 0:1, head_cols] * to_exp2
        query, query_tan = norm(*rs_result(2 + s), gain)
        QB[0:TB, 0:HD] = query_tan
        QB[0:TB, HD:] = query
        QB[TB:, 0:HD] = query
        QB[TB:, HD:] = jnp.zeros((TB, HD), BF16)

    def arrived(b):
        for t in range(2):
            for j in range(4):
                wait(g_sib[b, t, j])

    def scores(s):
        MX[...] = jnp.full((TB, 128), -jnp.inf, F32)

        @pl.loop(0, 8)
        def _(j):
            cut = pl.ds(pl.multiple_of(j * 512, 512), 512)
            part = lax.dot_general(
                QB[...], KB[j], (((1,), (1,)), ((), ())), preferred_element_type=F32
            )
            S[:, cut] = part
            part = part[TB:]
            top = jnp.maximum(
                jnp.maximum(part[:, 0:128], part[:, 128:256]),
                jnp.maximum(part[:, 256:384], part[:, 384:512]),
            )
            MX[...] = jnp.maximum(MX[...], top)

    def softmax(s):
        @pl.loop(0, TB // ROWS)
        def _(i):
            at = pl.multiple_of(i * ROWS, ROWS)
            rows = pl.ds(at, ROWS)
            raw = pl.ds(TB + at, ROWS)
            shift = jnp.max(MX[rows, :], axis=-1, keepdims=True)
            total = jnp.zeros((ROWS, 128), F32)
            inner = jnp.zeros((ROWS, 128), F32)
            for j in range(16):
                cut = slice(j * 256, (j + 1) * 256)
                e = jnp.exp2(S[raw, cut] - shift)
                EB[rows, cut] = e.astype(BF16)
                es = e * S[rows, cut]
                total += e[:, :128] + e[:, 128:]
                inner += es[:, :128] + es[:, 128:]
            total = jnp.sum(total, axis=-1, keepdims=True)
            mean = jnp.sum(inner, axis=-1, keepdims=True) / total
            LI[rows, :] = jnp.broadcast_to(1.0 / total, (ROWS, HD))
            for j in range(16):
                cut = slice(j * 256, (j + 1) * 256)
                EB[raw, cut] = (EB[rows, cut].astype(F32) * (S[rows, cut] - mean)).astype(BF16)

    def products(s):
        AO[...] = jnp.zeros((2 * TB, 2 * HD), F32)

        @pl.loop(0, 8)
        def _(j):
            cut = pl.ds(pl.multiple_of(j * 512, 512), 512)
            AO[...] += jnp.dot(EB[:, cut], VB[j], preferred_element_type=F32)

    my_pair = zl * 8 + y * 2
    head_at = lax.rem(zh, 2)
    back = []

    def heads_back(s):
        inv = LI[...]
        primal = (AO[0:TB, :HD] * inv).astype(BF16)
        tangent = ((AO[0:TB, HD:] + AO[TB:, :HD] * ln2) * inv).astype(BF16)
        for t in range(2):
            HS[s, t, 0:HALF, :] = primal[t * HALF:(t + 1) * HALF, :]
            HS[s, t, HALF:, :] = tangent[t * HALF:(t + 1) * HALF, :]
        for g in range(2):
            q = 2 * s + g
            target = HB.at[my_pair + cw, q, :, head_cols]
            for t in range(2):
                zeta = 2 * c + block_at[t]
                source = HS.at[s, t, pl.ds(g * HALF, HALF), :]
                copy = pltpu.make_async_remote_copy(
                    src_ref=source, dst_ref=target, send_sem=bssem.at[2 * q + t],
                    recv_sem=brsem.at[2 * q + head_at],
                    device_id=dev(zh_=zeta, c_=cw), device_id_type=pl.DeviceIdType.MESH,
                )
                stay = pltpu.make_async_copy(source, target, lsem.at[2 * q + t])
                here = zeta == zh

                @pl.when(here)
                def _(stay=stay):
                    stay.start()
                    stay.wait()

                @pl.when(jnp.logical_not(here))
                def _(copy=copy):
                    copy.start()

                back.append((copy, here))

    def hp(zz, yy):
        return zz * 8 + yy * 2 + c

    def h_part(p, q):
        return HB.at[p, q]

    def h_half(p, q, h):
        return HB.at[p, q, pl.ds(h * (HALF // 2), HALF // 2), :]

    h_own, h_two, h_opp, swapped = {}, {}, {}, {}

    def heads_start(s):
        for q in (2 * s, 2 * s + 1):
            for h in range(2):
                came = pltpu.make_async_remote_copy(
                    src_ref=HS.at[s, h, pl.ds(0, HALF), :],
                    dst_ref=HB.at[sq, q, :, pl.ds(h * HD, HD)],
                    send_sem=bssem.at[2 * q + h], recv_sem=brsem.at[2 * q + h],
                    device_id=sibling, device_id_type=pl.DeviceIdType.MESH,
                )

                @pl.when(2 * c + h != zh)
                def _(came=came):
                    came.wait_recv()

            mine = h_part(sq, q)
            across = same(mine, pair)
            h_own[q] = (same(mine, y_right), same(mine, y_left), across)

    def heads_pair(s):
        for q in (2 * s, 2 * s + 1):
            h_own[q][2].wait_recv()
            p = hp(nz, y)
            h_two[q] = (same(h_part(p, q), y_right), same(h_part(p, q), y_left))

    def heads_relay(s, zz, arrivals):
        for q in (2 * s, 2 * s + 1):
            right, left = arrivals[q][:2]
            right.wait_recv()
            first = same(h_half(hp(zz, yl), q, 0), y_right)
            left.wait_recv()
            second = same(h_half(hp(zz, yr), q, 1), y_left)
            h_opp.setdefault((s, zz is zl), []).extend([first, second])

    def heads_relay_own(s):
        heads_relay(s, zl, h_own)

    def heads_relay_two(s):
        heads_relay(s, nz, h_two)

    def multiply(s, zz, near, first=False):
        total = None if first else ACC[s]
        for yy in (y, yl, yr) if near else (yo,):
            p = hp(zz, yy)
            part = lax.dot_general(
                WOB[pl.ds(p - c, 2)].reshape(2 * F, 2 * HD),
                HB[p, 2 * s:2 * s + 2].reshape(TB, 2 * HD), (((1,), (1,)), ((), ())),
                preferred_element_type=F32,
            )
            total = part if total is None else total + part
        ACC[s] = total

    def multiply_far(s):
        for zz in (zl, nz):
            wait(h_opp[s, zz is zl])
            multiply(s, zz, False)
        XS[s] = ACC[s, pl.ds(pl.multiple_of(c * F, 64), F), :].astype(BF16)
        swapped[s] = send(XS.at[s], XR.at[s], sibling)

    def finish(s):
        swapped[s].wait_recv()
        mine = ACC[s, pl.ds(pl.multiple_of((1 - c) * F, 64), F), :] + XR[s].astype(F32)
        cut = slice(s * HALF, (s + 1) * HALF)
        out_ref[0:F, cut] = mine[:, 0:HALF].astype(BF16)
        out_ref[F:, cut] = mine[:, HALF:].astype(BF16)

    for h in range(2):
        wait(a_own_opp[2 * h:2 * h + 2])
        for k in (2 * h, 2 * h + 1):
            a_own[k][1 - k % 2].wait_recv()
        turn(0, h)
    wait(w_sib[0])
    rs_opposite(0)
    rs_direct(0)
    for k in range(4):
        a_two_opp.append(a_relay(zl, a_two, k))
    w_relay(2)
    w_start(1)
    rs_own(0)
    rs_summed(0)
    for h in range(2):
        wait(a_two_opp[2 * h:2 * h + 2])
        for k in (2 * h, 2 * h + 1):
            a_two[k][1 - k % 2].wait_recv()
        turn(1, h)
    rs_opposite(1)
    rs_direct(1)
    w_last(2)
    w_relay(1)
    wo_send_x(zh)
    wait(wo_z)
    wo_send_x(zf)
    wo_send_x(zr)
    wait(w_sib[2])
    rs_opposite(4)
    rs_summed(1)
    rs_direct(4)
    keys_out(0)
    rs_own(1)
    rs_opposite(5)
    w_last(1)
    rs_summed(4)
    rs_direct(5)
    keys_out(1)
    wait(w_sib[1])
    rs_opposite(2)
    g_relay(0, 0)
    rs_own(4)
    rs_summed(5)
    rs_direct(2)
    g_relay(0, 1)
    values_out(0)
    rs_own(5)
    rs_opposite(3)
    rs_own(2)
    rs_own(3)
    g_last(0, 0)
    g_last(0, 1)
    for n in range(3):
        wo_relay_x(n)
    rs_summed(2)
    rs_direct(3)
    values_out(1)
    g_relay(1, 0)
    rs_summed(3)
    wo_zopp = wo_relay_z()
    g_last(1, 0)
    g_relay(1, 1)
    queries(0)
    arrived(0)
    scores(0)
    g_last(1, 1)
    softmax(0)
    arrived(1)
    products(0)
    heads_back(0)
    queries(1)
    scores(1)
    heads_start(0)
    softmax(1)
    wait(wo_zopp)
    wo_send_x(zo)
    heads_pair(0)
    heads_relay_own(0)
    products(1)
    heads_back(1)
    heads_relay_two(0)
    heads_start(1)
    wo_relay_x(3)
    heads_pair(1)
    heads_relay_own(1)
    wait(wo_xopp)
    multiply(0, zl, True, first=True)
    multiply(0, nz, True)
    multiply_far(0)
    heads_relay_two(1)
    multiply(1, zl, True, first=True)
    multiply(1, nz, True)
    multiply_far(1)
    finish(0)
    finish(1)

    for copy in sent:
        copy.wait_send()
    for copy, here in back:
        @pl.when(jnp.logical_not(here))
        def _(copy=copy):
            copy.wait_send()


def shards(
    inputs, tangents, query_weight, key_weight, value_weight, query_gain, key_gain, out_weight
):
    vmem = pl.BlockSpec(memory_space=pltpu.VMEM)
    v = pltpu.VMEM
    both = pl.pallas_call(
        kernel,
        out_shape=jax.ShapeDtypeStruct((2 * F, TB), BF16),
        in_specs=[vmem] * 8,
        out_specs=vmem,
        scratch_shapes=[
            v((2, 3, 4 * F, 256), BF16),
            v((2, 2, 8, 256), F32),
            v((2, 4 * F, 512), BF16),
            v((2, 2, 2, HALF, 4 * F), BF16),
            v((16, F, 256), BF16),
            v((2 * TB, HD), F32),
            v((6, 3, 2, TB, HD), BF16),
            v((6, 3, 2, TB, HD), BF16),
            v((6, 2, TB, HD), F32),
            v((6, 2, TB, HD), F32),
            v((8, 512, 256), BF16),
            v((8, 512, 256), BF16),
            v((2 * TB, 256), BF16),
            v((2 * TB, TOKENS), F32),
            v((TB, 128), F32),
            v((TB, HD), F32),
            v((2 * TB, TOKENS), BF16),
            v((2 * TB, 2 * HD), F32),
            v((2, 2, TB, HD), BF16),
            v((16, 4, HALF, 256), BF16),
            v((2, 2 * F, TB), F32),
            v((2, F, TB), BF16),
            v((2, F, TB), BF16),
            pltpu.SemaphoreType.DMA((N_SEMS,)),
            pltpu.SemaphoreType.DMA((N_SEMS,)),
            pltpu.SemaphoreType.DMA((8,)),
            pltpu.SemaphoreType.DMA((8,)),
            pltpu.SemaphoreType.DMA((8,)),
        ],
        compiler_params=pltpu.CompilerParams(
            collective_id=0, has_side_effects=True, vmem_limit_bytes=60 * 2**20
        ),
    )(
        inputs.T, tangents.T, query_weight, key_weight, value_weight,
        query_gain.reshape(1, 2 * HD), key_gain.reshape(1, 2 * HD), out_weight.T,
    )
    return both[:F].T, both[F:].T


def solution(mesh):
    in_specs = (
        P("seq", "dp"),
        P("seq", "dp"),
        P("dp", "seq"),
        P("dp", "seq"),
        P("dp", "seq"),
        P("seq"),
        P("seq"),
        P("seq", "dp"),
    )
    out_specs = (P("dp", "seq"), P("dp", "seq"))
    return jax.shard_map(shards, mesh=mesh, in_specs=in_specs, out_specs=out_specs, check_vma=False)
```

```python
import jax
import jax.numpy as jnp
from jax import lax
from jax.experimental import pallas as pl
from jax.experimental.pallas import tpu as pltpu
from jax.sharding import PartitionSpec as P

HD = 128
F = 320
TB = 256
TOKENS = 4096
HALF = 128
BF16 = jnp.bfloat16
F32 = jnp.float32
N_SEMS = 208


def kernel(
    in_ref, tin_ref, wq_ref, wk_ref, wv_ref, gq_ref, gk_ref, wo_ref,
    out_ref,
    WB, GB, AB, AN, WOB, PART, SB, RB, HOLD, OWN, KB, VB, QB, S, MX, LI, EB, AO, HS, HB, ACC, XS, XR,
    ssem, rsem, bssem, brsem, lsem,
):
    dp = lax.axis_index("dp")
    sq = lax.axis_index("seq")
    zh, x = lax.div(dp, 4), lax.rem(dp, 4)
    zl, y, c = lax.div(sq, 8), lax.rem(lax.div(sq, 2), 4), lax.rem(sq, 2)

    def dev(zh_=zh, x_=x, zl_=zl, y_=y, c_=c):
        return (zh_ * 4 + x_, zl_ * 8 + y_ * 2 + c_)

    def ring(v):
        return lax.rem(v + 1 + 2 * c, 4), lax.rem(v + 3 - 2 * c, 4), lax.rem(v + 2, 4)

    xr, xl, xo = ring(x)
    yr, yl, yo = ring(y)
    zr, zf, zo = ring(zh)
    x_right, x_left = dev(x_=xr), dev(x_=xl)
    y_right, y_left = dev(y_=yr), dev(y_=yl)
    z_right, z_left = dev(zh_=zr), dev(zh_=zf)
    nz = 1 - zl
    pair = dev(zl_=nz)
    sibling = dev(c_=1 - c)
    a_to = dev(x_=2 * lax.rem(y, 2) + c, zl_=1 - lax.div(y, 2), y_=x, c_=zl)
    a_from = dev(x_=y, zl_=c, y_=2 * nz + lax.div(x, 2), c_=lax.rem(x, 2))

    wo_row = 2 * lax.div(sq, 2) + 1 - lax.rem(dp, 2)
    wo_to = (wo_row, 2 * lax.div(dp, 2) + c)
    wo_from = (
        2 * lax.div(sq, 2) + 1 - lax.rem(dp, 2), 2 * lax.div(dp, 2) + c
    )

    barrier = pltpu.get_barrier_semaphore()
    greet = [x_right, x_left, y_right, y_left, pair, a_to, a_from, wo_to, wo_from]
    for k in range(1, 8):
        peer = lax.rem(zh * 2 + c + k, 8)
        greet.append(dev(zh_=lax.div(peer, 2), c_=lax.rem(peer, 2)))
    for d in greet:
        pl.semaphore_signal(barrier, inc=1, device_id=d, device_id_type=pl.DeviceIdType.MESH)

    def rows_of(xx):
        return pl.ds(pl.multiple_of(xx * F, 64), F)

    def half_rows(xx, h):
        return pl.ds(pl.multiple_of(xx * F + h * (F // 2), 32), F // 2)

    WB[c, 0, rows_of(x), :] = wk_ref[...]
    WB[c, 1, rows_of(x), :] = wq_ref[...]
    WB[c, 2, rows_of(x), :] = wv_ref[...]
    GB[c, 0] = jnp.broadcast_to(gq_ref[...], (8, 2 * HD))
    GB[c, 1] = jnp.broadcast_to(gk_ref[...], (8, 2 * HD))

    pl.semaphore_wait(barrier, len(greet))

    sent = []

    def send(src, dst, device):
        k = len(sent)
        copy = pltpu.make_async_remote_copy(
            src_ref=src, dst_ref=dst, send_sem=ssem.at[k], recv_sem=rsem.at[k],
            device_id=device, device_id_type=pl.DeviceIdType.MESH,
        )
        copy.start()
        sent.append(copy)
        return copy

    def same(ref, device):
        return send(ref, ref, device)

    def wait(copies):
        for copy in copies:
            copy.wait_recv()

    def w_piece(w, xx):
        return WB.at[c, w, rows_of(xx), :]

    def w_half(w, xx, h):
        return WB.at[c, w, half_rows(xx, h), :]

    w_near, w_far, w_sib = {}, {}, {0: [], 1: [], 2: []}

    def w_start(w):
        w_near[w] = (same(w_piece(w, x), x_right), same(w_piece(w, x), x_left))
        w_sib[w].append(same(w_piece(w, x), sibling))

    def w_relay(w):
        right, left = w_near[w]
        right.wait_recv()
        a = same(w_half(w, xl, 0), x_right)
        w_sib[w].append(same(w_piece(w, xl), sibling))
        left.wait_recv()
        b = same(w_half(w, xr, 1), x_left)
        w_sib[w].append(same(w_piece(w, xr), sibling))
        w_far[w] = (a, b)

    def w_last(w):
        for h in range(2):
            w_far[w][h].wait_recv()
            w_sib[w].append(same(w_half(w, xo, h), sibling))

    def cols_of(g):
        return pl.ds(g * TB, TB)

    def a_chunk(z, yy, k):
        return AB.at[z, half_rows(yy, k % 2), cols_of(k // 2)]

    a_perm = []
    for k in range(4):
        ref = (in_ref, tin_ref)[k // 2].at[pl.ds((k % 2) * (F // 2), F // 2), :]
        a_perm.append(
            send(ref, AB.at[lax.div(y, 2), half_rows(x, k % 2), cols_of(k // 2)], a_to)
        )

    a_own, a_pair, a_two, a_own_opp, a_two_opp = [], [], [], [], []

    def a_start(k):
        a_perm[k].wait_recv()
        own = a_chunk(nz, y, k)
        a_own.append((same(own, y_right), same(own, y_left)))
        a_pair.append(same(own, pair))

    def a_relay(z, arrivals, k):
        arrivals[k][k % 2].wait_recv()
        yy, to = ((yl, y_right), (yr, y_left))[k % 2]
        return same(a_chunk(z, yy, k), to)

    def wo_block(zz, xx):
        return zz * 4 + xx

    def wo_half(b, h):
        return WOB.at[b, pl.ds(h * (F // 2), F // 2), :]

    a_start(0)
    a_start(1)
    wo_perm = send(wo_ref, WOB.at[wo_row], wo_to)
    w_start(0)
    w_sib[0].append(same(GB.at[c], sibling))
    a_start(2)
    a_own_opp.append(a_relay(nz, a_own, 0))
    a_start(3)
    a_own_opp.append(a_relay(nz, a_own, 1))
    w_relay(0)
    a_own_opp.append(a_relay(nz, a_own, 2))
    a_own_opp.append(a_relay(nz, a_own, 3))
    for k in range(4):
        a_pair[k].wait_recv()
        two = a_chunk(zl, y, k)
        a_two.append((same(two, y_right), same(two, y_left)))

    def wo_start_z():
        block = WOB.at[wo_block(zh, x)]
        return same(block, z_right), same(block, z_left)

    def wo_relay_z():
        return [
            same(wo_half(wo_block(zf, x), 0), z_right),
            same(wo_half(wo_block(zr, x), 1), z_left),
        ]

    w_start(2)
    wo_perm.wait_recv()
    wo_z = wo_start_z()
    w_last(0)

    wo_x = []

    def wo_send_x(zz):
        b = WOB.at[wo_block(zz, x)]
        wo_x.append((zz, same(b, x_right), same(b, x_left)))

    block_at = (nz, zl)

    def turn(t, h):
        @pl.loop(0, 5)
        def _(i):
            cut = pl.ds(pl.multiple_of(i * 256, 256), 256)
            piece = AB[block_at[t], cut, h * TB:(h + 1) * TB].T
            for s in range(2):
                AN[t, h, s, :, cut] = piece[s * HALF:(s + 1) * HALF, :]

    def tile(kind, k):
        d = (zh, zr, zo, zf)[k]
        cw = lax.div(d, 2)
        cols = pl.ds(pl.multiple_of(lax.rem(d, 2) * HD, HD), HD)
        queries = kind // 2 == 1
        PART[...] = jnp.zeros((2 * TB, HD), F32)

        @pl.loop(0, 5)
        def _(i):
            deep = pl.ds(pl.multiple_of(i * 256, 256), 256)
            tokens = AN[:, :, kind % 2, :, deep] if queries else AN[kind % 2, :, :, :, deep]
            PART[...] += jnp.dot(
                tokens.reshape(2 * TB, 256), WB[cw, kind // 2, deep, cols],
                preferred_element_type=F32,
            )

        part = PART[...].reshape(2, 2, HALF, HD)
        return [(part[:, h] if queries else part[h]).reshape(TB, HD) for h in range(2)]

    relay, direct, summed = {}, {}, {}

    def rs_send(kind, slot, h, part, to):
        SB[kind, slot, h] = part.astype(BF16)
        return send(SB.at[kind, slot, h], RB.at[kind, slot, h], to)

    def rs_opposite(kind):
        part = tile(kind, 2)
        for h in range(2):
            relay[kind, h] = rs_send(kind, 0, h, part[h], z_right if h == 0 else z_left)

    def rs_direct(kind):
        for slot, k, h, to in ((1, 1, 1, z_right), (2, 3, 0, z_left)):
            part = tile(kind, k)
            direct[kind, slot] = rs_send(kind, slot, h, part[h], to)
            HOLD[kind, 1 - h] = part[1 - h]

    def rs_summed(kind):
        for slot, h, to in ((1, 0, z_right), (2, 1, z_left)):
            relay[kind, h].wait_recv()
            part = HOLD[kind, h] + RB[kind, 0, h].astype(F32)
            summed[kind, slot] = rs_send(kind, slot, h, part, to)

    def rs_own(kind):
        part = tile(kind, 0)
        for h in range(2):
            OWN[kind, h] = part[h]

    def rs_result(kind):
        for slot in (1, 2):
            direct[kind, slot].wait_recv()
            summed[kind, slot].wait_recv()
        return [
            OWN[kind, h] + RB[kind, 1, h].astype(F32) + RB[kind, 2, h].astype(F32)
            for h in range(2)
        ]

    cw = lax.div(zh, 2)
    head_cols = pl.ds(pl.multiple_of(lax.rem(zh, 2) * HD, HD), HD)

    def norm(raw, tan, gain):
        ms = jnp.mean(raw * raw, axis=-1, keepdims=True)
        inv = lax.rsqrt(ms + 1e-06)
        inner = jnp.mean(raw * tan, axis=-1, keepdims=True)
        normed = gain * raw * inv
        normed_tan = gain * inv * (tan - raw * inner * inv * inv)
        return normed.astype(BF16), normed_tan.astype(BF16)

    def slot_of(xx, cc):
        return xx * 2 + cc

    g_near, g_far = {}, {}
    g_sib = {(b, t, j): [] for b in range(2) for t in range(2) for j in range(4)}

    def g_block(b, t, xx, rows=0, count=TB):
        return (KB, VB)[b].at[slot_of(xx, c), pl.ds(t * TB + rows, count), :]

    def g_start(b, t):
        block = g_block(b, t, x)
        g_near[b, t] = (same(block, x_right), same(block, x_left))
        g_sib[b, t, 0].append(same(block, sibling))

    def g_relay(b, t):
        right, left = g_near[b, t]
        right.wait_recv()
        first = same(g_block(b, t, xl, 0, HALF), x_right)
        g_sib[b, t, 1].append(same(g_block(b, t, xl), sibling))
        left.wait_recv()
        second = same(g_block(b, t, xr, HALF, HALF), x_left)
        g_sib[b, t, 2].append(same(g_block(b, t, xr), sibling))
        g_far[b, t] = (first, second)

    def g_last(b, t):
        for h in range(2):
            g_far[b, t][h].wait_recv()
            g_sib[b, t, 3].append(same(g_block(b, t, xo, h * HALF, HALF), sibling))

    def keys_out(t):
        key, key_tan = norm(*rs_result(t), GB[cw, 1, 0:1, head_cols])
        rows = slice(t * TB, (t + 1) * TB)
        KB[slot_of(x, c), rows, 0:HD] = key
        KB[slot_of(x, c), rows, HD:] = key_tan
        g_start(0, t)

    def values_out(t):
        raw, tan = rs_result(4 + t)
        rows = slice(t * TB, (t + 1) * TB)
        VB[slot_of(x, c), rows, 0:HD] = raw.astype(BF16)
        VB[slot_of(x, c), rows, HD:] = tan.astype(BF16)
        g_start(1, t)

    wo_xopp = []

    def wo_relay_x(n):
        zz, right, left = wo_x[n]
        right.wait_recv()
        wo_xopp.append(same(wo_half(wo_block(zz, xl), 0), x_right))
        left.wait_recv()
        wo_xopp.append(same(wo_half(wo_block(zz, xr), 1), x_left))

    to_exp2 = HD ** -0.5 * 1.4426950408889634
    ln2 = 0.6931471805599453
    ROWS = 32

    def queries(s):
        gain = GB[cw, 0, 0:1, head_cols] * to_exp2
        query, query_tan = norm(*rs_result(2 + s), gain)
        QB[0:TB, 0:HD] = query_tan
        QB[0:TB, HD:] = query
        QB[TB:, 0:HD] = query
        QB[TB:, HD:] = jnp.zeros((TB, HD), BF16)

    def arrived(b):
        for t in range(2):
            for j in range(4):
                wait(g_sib[b, t, j])

    def scores(s):
        MX[...] = jnp.full((TB, 128), -jnp.inf, F32)

        @pl.loop(0, 8)
        def _(j):
            cut = pl.ds(pl.multiple_of(j * 512, 512), 512)
            part = lax.dot_general(
                QB[...], KB[j], (((1,), (1,)), ((), ())), preferred_element_type=F32
            )
            S[:, cut] = part
            part = part[TB:]
            top = jnp.maximum(
                jnp.maximum(part[:, 0:128], part[:, 128:256]),
                jnp.maximum(part[:, 256:384], part[:, 384:512]),
            )
            MX[...] = jnp.maximum(MX[...], top)

    def softmax(s):
        @pl.loop(0, TB // ROWS)
        def _(i):
            at = pl.multiple_of(i * ROWS, ROWS)
            rows = pl.ds(at, ROWS)
            raw = pl.ds(TB + at, ROWS)
            shift = jnp.max(MX[rows, :], axis=-1, keepdims=True)
            total = jnp.zeros((ROWS, 128), F32)
            inner = jnp.zeros((ROWS, 128), F32)
            for j in range(16):
                cut = slice(j * 256, (j + 1) * 256)
                e = jnp.exp2(S[raw, cut] - shift)
                EB[rows, cut] = e.astype(BF16)
                es = e * S[rows, cut]
                total += e[:, :128] + e[:, 128:]
                inner += es[:, :128] + es[:, 128:]
            total = jnp.sum(total, axis=-1, keepdims=True)
            mean = jnp.sum(inner, axis=-1, keepdims=True) / total
            LI[rows, :] = jnp.broadcast_to(1.0 / total, (ROWS, HD))
            for j in range(16):
                cut = slice(j * 256, (j + 1) * 256)
                EB[raw, cut] = (EB[rows, cut].astype(F32) * (S[rows, cut] - mean)).astype(BF16)

    def products(s):
        AO[...] = jnp.zeros((2 * TB, 2 * HD), F32)

        @pl.loop(0, 8)
        def _(j):
            cut = pl.ds(pl.multiple_of(j * 512, 512), 512)
            AO[...] += jnp.dot(EB[:, cut], VB[j], preferred_element_type=F32)

    my_pair = zl * 8 + y * 2
    head_at = lax.rem(zh, 2)
    back = []

    def heads_back(s):
        inv = LI[...]
        primal = (AO[0:TB, :HD] * inv).astype(BF16)
        tangent = ((AO[0:TB, HD:] + AO[TB:, :HD] * ln2) * inv).astype(BF16)
        for t in range(2):
            HS[s, t, 0:HALF, :] = primal[t * HALF:(t + 1) * HALF, :]
            HS[s, t, HALF:, :] = tangent[t * HALF:(t + 1) * HALF, :]
        for g in range(2):
            q = 2 * s + g
            target = HB.at[my_pair + cw, q, :, head_cols]
            for t in range(2):
                zeta = 2 * c + block_at[t]
                source = HS.at[s, t, pl.ds(g * HALF, HALF), :]
                copy = pltpu.make_async_remote_copy(
                    src_ref=source, dst_ref=target, send_sem=bssem.at[2 * q + t],
                    recv_sem=brsem.at[2 * q + head_at],
                    device_id=dev(zh_=zeta, c_=cw), device_id_type=pl.DeviceIdType.MESH,
                )
                stay = pltpu.make_async_copy(source, target, lsem.at[2 * q + t])
                here = zeta == zh

                @pl.when(here)
                def _(stay=stay):
                    stay.start()
                    stay.wait()

                @pl.when(jnp.logical_not(here))
                def _(copy=copy):
                    copy.start()

                back.append((copy, here))

    def hp(zz, yy):
        return zz * 8 + yy * 2 + c

    def h_part(p, q):
        return HB.at[p, q]

    def h_half(p, q, h):
        return HB.at[p, q, pl.ds(h * (HALF // 2), HALF // 2), :]

    h_own, h_two, h_opp, swapped = {}, {}, {}, {}

    def heads_start(s):
        for q in (2 * s, 2 * s + 1):
            for h in range(2):
                came = pltpu.make_async_remote_copy(
                    src_ref=HS.at[s, h, pl.ds(0, HALF), :],
                    dst_ref=HB.at[sq, q, :, pl.ds(h * HD, HD)],
                    send_sem=bssem.at[2 * q + h], recv_sem=brsem.at[2 * q + h],
                    device_id=sibling, device_id_type=pl.DeviceIdType.MESH,
                )

                @pl.when(2 * c + h != zh)
                def _(came=came):
                    came.wait_recv()

            mine = h_part(sq, q)
            across = same(mine, pair)
            h_own[q] = (same(mine, y_right), same(mine, y_left), across)

    def heads_pair(s):
        for q in (2 * s, 2 * s + 1):
            h_own[q][2].wait_recv()
            p = hp(nz, y)
            h_two[q] = (same(h_part(p, q), y_right), same(h_part(p, q), y_left))

    def heads_relay(s, zz, arrivals):
        for q in (2 * s, 2 * s + 1):
            right, left = arrivals[q][:2]
            right.wait_recv()
            first = same(h_half(hp(zz, yl), q, 0), y_right)
            left.wait_recv()
            second = same(h_half(hp(zz, yr), q, 1), y_left)
            h_opp.setdefault((s, zz is zl), []).extend([first, second])

    def heads_relay_own(s):
        heads_relay(s, zl, h_own)

    def heads_relay_two(s):
        heads_relay(s, nz, h_two)

    def multiply(s, zz, near, first=False):
        total = None if first else ACC[s]
        for yy in (y, yl, yr) if near else (yo,):
            p = hp(zz, yy)
            part = lax.dot_general(
                WOB[pl.ds(p - c, 2)].reshape(2 * F, 2 * HD),
                HB[p, 2 * s:2 * s + 2].reshape(TB, 2 * HD), (((1,), (1,)), ((), ())),
                preferred_element_type=F32,
            )
            total = part if total is None else total + part
        ACC[s] = total

    def multiply_far(s):
        for zz in (zl, nz):
            wait(h_opp[s, zz is zl])
            multiply(s, zz, False)
        XS[s] = ACC[s, pl.ds(pl.multiple_of(c * F, 64), F), :].astype(BF16)
        swapped[s] = send(XS.at[s], XR.at[s], sibling)

    def finish(s):
        swapped[s].wait_recv()
        mine = ACC[s, pl.ds(pl.multiple_of((1 - c) * F, 64), F), :] + XR[s].astype(F32)
        cut = slice(s * HALF, (s + 1) * HALF)
        out_ref[0:F, cut] = mine[:, 0:HALF].astype(BF16)
        out_ref[F:, cut] = mine[:, HALF:].astype(BF16)

    for h in range(2):
        wait(a_own_opp[2 * h:2 * h + 2])
        for k in (2 * h, 2 * h + 1):
            a_own[k][1 - k % 2].wait_recv()
        turn(0, h)
    wait(w_sib[0])
    rs_opposite(0)
    rs_direct(0)
    for k in range(4):
        a_two_opp.append(a_relay(zl, a_two, k))
    w_relay(2)
    w_start(1)
    rs_own(0)
    rs_summed(0)
    for h in range(2):
        wait(a_two_opp[2 * h:2 * h + 2])
        for k in (2 * h, 2 * h + 1):
            a_two[k][1 - k % 2].wait_recv()
        turn(1, h)
    rs_opposite(1)
    rs_direct(1)
    w_last(2)
    w_relay(1)
    wo_send_x(zh)
    wait(w_sib[2])
    rs_opposite(4)
    rs_direct(4)
    rs_opposite(5)
    rs_summed(1)
    keys_out(0)
    rs_direct(5)
    w_last(1)
    wait(wo_z)
    wo_send_x(zf)
    wo_send_x(zr)
    wait(w_sib[1])
    rs_opposite(2)
    rs_own(1)
    rs_summed(4)
    rs_direct(2)
    keys_out(1)
    rs_opposite(3)
    rs_own(4)
    rs_own(5)
    rs_summed(5)
    rs_direct(3)
    g_relay(0, 0)
    values_out(0)
    g_relay(0, 1)
    rs_own(2)
    rs_own(3)
    rs_summed(2)
    g_last(0, 0)
    g_last(0, 1)
    values_out(1)
    g_relay(1, 0)
    rs_summed(3)
    for n in range(3):
        wo_relay_x(n)
    wo_zopp = wo_relay_z()
    g_last(1, 0)
    g_relay(1, 1)
    queries(0)
    arrived(0)
    scores(0)
    g_last(1, 1)
    softmax(0)
    arrived(1)
    products(0)
    heads_back(0)
    queries(1)
    scores(1)
    heads_start(0)
    softmax(1)
    wait(wo_zopp)
    wo_send_x(zo)
    heads_pair(0)
    heads_relay_own(0)
    products(1)
    heads_back(1)
    heads_relay_two(0)
    heads_start(1)
    wo_relay_x(3)
    heads_pair(1)
    heads_relay_own(1)
    wait(wo_xopp)
    multiply(0, zl, True, first=True)
    multiply(0, nz, True)
    multiply_far(0)
    heads_relay_two(1)
    multiply(1, zl, True, first=True)
    multiply(1, nz, True)
    multiply_far(1)
    finish(0)
    finish(1)

    for copy in sent:
        copy.wait_send()
    for copy, here in back:
        @pl.when(jnp.logical_not(here))
        def _(copy=copy):
            copy.wait_send()


def shards(
    inputs, tangents, query_weight, key_weight, value_weight, query_gain, key_gain, out_weight
):
    vmem = pl.BlockSpec(memory_space=pltpu.VMEM)
    v = pltpu.VMEM
    both = pl.pallas_call(
        kernel,
        out_shape=jax.ShapeDtypeStruct((2 * F, TB), BF16),
        in_specs=[vmem] * 8,
        out_specs=vmem,
        scratch_shapes=[
            v((2, 3, 4 * F, 256), BF16),
            v((2, 2, 8, 256), F32),
            v((2, 4 * F, 512), BF16),
            v((2, 2, 2, HALF, 4 * F), BF16),
            v((16, F, 256), BF16),
            v((2 * TB, HD), F32),
            v((6, 3, 2, TB, HD), BF16),
            v((6, 3, 2, TB, HD), BF16),
            v((6, 2, TB, HD), F32),
            v((6, 2, TB, HD), F32),
            v((8, 512, 256), BF16),
            v((8, 512, 256), BF16),
            v((2 * TB, 256), BF16),
            v((2 * TB, TOKENS), F32),
            v((TB, 128), F32),
            v((TB, HD), F32),
            v((2 * TB, TOKENS), BF16),
            v((2 * TB, 2 * HD), F32),
            v((2, 2, TB, HD), BF16),
            v((16, 4, HALF, 256), BF16),
            v((2, 2 * F, TB), F32),
            v((2, F, TB), BF16),
            v((2, F, TB), BF16),
            pltpu.SemaphoreType.DMA((N_SEMS,)),
            pltpu.SemaphoreType.DMA((N_SEMS,)),
            pltpu.SemaphoreType.DMA((8,)),
            pltpu.SemaphoreType.DMA((8,)),
            pltpu.SemaphoreType.DMA((8,)),
        ],
        compiler_params=pltpu.CompilerParams(
            collective_id=0, has_side_effects=True, vmem_limit_bytes=60 * 2**20
        ),
    )(
        inputs.T, tangents.T, query_weight, key_weight, value_weight,
        query_gain.reshape(1, 2 * HD), key_gain.reshape(1, 2 * HD), out_weight.T,
    )
    return both[:F].T, both[F:].T


def solution(mesh):
    in_specs = (
        P("seq", "dp"),
        P("seq", "dp"),
        P("dp", "seq"),
        P("dp", "seq"),
        P("dp", "seq"),
        P("seq"),
        P("seq"),
        P("seq", "dp"),
    )
    out_specs = (P("dp", "seq"), P("dp", "seq"))
    return jax.shard_map(shards, mesh=mesh, in_specs=in_specs, out_specs=out_specs, check_vma=False)
```

```python
import jax
import jax.numpy as jnp
from jax import lax
from jax.experimental import pallas as pl
from jax.experimental.pallas import tpu as pltpu
from jax.sharding import PartitionSpec as P

HD = 128
F = 320
TB = 256
TOKENS = 4096
HALF = 128
BF16 = jnp.bfloat16
F32 = jnp.float32
N_SEMS = 208


def kernel(
    in_ref, tin_ref, wq_ref, wk_ref, wv_ref, gq_ref, gk_ref, wo_ref,
    out_ref,
    WB, GB, AB, AN, WOB, PART, SB, RB, HOLD, OWN, KB, VB, QB, S, MX, LI, EB, AO, HS, HB, ACC, XS, XR,
    ssem, rsem, bssem, brsem, lsem,
):
    dp = lax.axis_index("dp")
    sq = lax.axis_index("seq")
    zh, x = lax.div(dp, 4), lax.rem(dp, 4)
    zl, y, c = lax.div(sq, 8), lax.rem(lax.div(sq, 2), 4), lax.rem(sq, 2)

    def dev(zh_=zh, x_=x, zl_=zl, y_=y, c_=c):
        return (zh_ * 4 + x_, zl_ * 8 + y_ * 2 + c_)

    def ring(v):
        return lax.rem(v + 1 + 2 * c, 4), lax.rem(v + 3 - 2 * c, 4), lax.rem(v + 2, 4)

    xr, xl, xo = ring(x)
    yr, yl, yo = ring(y)
    zr, zf, zo = ring(zh)
    x_right, x_left = dev(x_=xr), dev(x_=xl)
    y_right, y_left = dev(y_=yr), dev(y_=yl)
    z_right, z_left = dev(zh_=zr), dev(zh_=zf)
    nz = 1 - zl
    pair = dev(zl_=nz)
    sibling = dev(c_=1 - c)
    a_to = dev(x_=2 * lax.rem(y, 2) + c, zl_=1 - lax.div(y, 2), y_=x, c_=zl)
    a_from = dev(x_=y, zl_=c, y_=2 * nz + lax.div(x, 2), c_=lax.rem(x, 2))

    wo_row = 2 * lax.div(sq, 2) + 1 - lax.rem(dp, 2)
    wo_to = (wo_row, 2 * lax.div(dp, 2) + c)
    wo_from = (
        2 * lax.div(sq, 2) + 1 - lax.rem(dp, 2), 2 * lax.div(dp, 2) + c
    )

    barrier = pltpu.get_barrier_semaphore()
    greet = [x_right, x_left, y_right, y_left, pair, a_to, a_from, wo_to, wo_from]
    for k in range(1, 8):
        peer = lax.rem(zh * 2 + c + k, 8)
        greet.append(dev(zh_=lax.div(peer, 2), c_=lax.rem(peer, 2)))
    for d in greet:
        pl.semaphore_signal(barrier, inc=1, device_id=d, device_id_type=pl.DeviceIdType.MESH)

    def rows_of(xx):
        return pl.ds(pl.multiple_of(xx * F, 64), F)

    def half_rows(xx, h):
        return pl.ds(pl.multiple_of(xx * F + h * (F // 2), 32), F // 2)

    WB[c, 0, rows_of(x), :] = wk_ref[...]
    WB[c, 1, rows_of(x), :] = wq_ref[...]
    WB[c, 2, rows_of(x), :] = wv_ref[...]
    GB[c, 0] = jnp.broadcast_to(gq_ref[...], (8, 2 * HD))
    GB[c, 1] = jnp.broadcast_to(gk_ref[...], (8, 2 * HD))

    pl.semaphore_wait(barrier, len(greet))

    sent = []

    def send(src, dst, device):
        k = len(sent)
        copy = pltpu.make_async_remote_copy(
            src_ref=src, dst_ref=dst, send_sem=ssem.at[k], recv_sem=rsem.at[k],
            device_id=device, device_id_type=pl.DeviceIdType.MESH,
        )
        copy.start()
        sent.append(copy)
        return copy

    def same(ref, device):
        return send(ref, ref, device)

    def wait(copies):
        for copy in copies:
            copy.wait_recv()

    def w_piece(w, xx):
        return WB.at[c, w, rows_of(xx), :]

    def w_half(w, xx, h):
        return WB.at[c, w, half_rows(xx, h), :]

    w_near, w_far, w_sib = {}, {}, {0: [], 1: [], 2: []}

    def w_start(w):
        w_near[w] = (same(w_piece(w, x), x_right), same(w_piece(w, x), x_left))
        w_sib[w].append(same(w_piece(w, x), sibling))

    def w_relay(w):
        right, left = w_near[w]
        right.wait_recv()
        a = same(w_half(w, xl, 0), x_right)
        w_sib[w].append(same(w_piece(w, xl), sibling))
        left.wait_recv()
        b = same(w_half(w, xr, 1), x_left)
        w_sib[w].append(same(w_piece(w, xr), sibling))
        w_far[w] = (a, b)

    def w_last(w):
        for h in range(2):
            w_far[w][h].wait_recv()
            w_sib[w].append(same(w_half(w, xo, h), sibling))

    def cols_of(g):
        return pl.ds(g * TB, TB)

    def a_chunk(z, yy, k):
        return AB.at[z, half_rows(yy, k % 2), cols_of(k // 2)]

    a_perm = []
    for k in range(4):
        ref = (in_ref, tin_ref)[k // 2].at[pl.ds((k % 2) * (F // 2), F // 2), :]
        a_perm.append(
            send(ref, AB.at[lax.div(y, 2), half_rows(x, k % 2), cols_of(k // 2)], a_to)
        )

    w_start(0)
    w_sib[0].append(same(GB.at[c], sibling))

    a_own, a_pair, a_two, a_own_opp, a_two_opp = [], [], [], [], []

    def a_start(k):
        a_perm[k].wait_recv()
        own = a_chunk(nz, y, k)
        a_own.append((same(own, y_right), same(own, y_left)))
        a_pair.append(same(own, pair))

    def a_relay(z, arrivals, k):
        arrivals[k][k % 2].wait_recv()
        yy, to = ((yl, y_right), (yr, y_left))[k % 2]
        return same(a_chunk(z, yy, k), to)

    def wo_block(zz, xx):
        return zz * 4 + xx

    def wo_half(b, h):
        return WOB.at[b, pl.ds(h * (F // 2), F // 2), :]

    a_start(0)
    a_start(1)
    wo_perm = send(wo_ref, WOB.at[wo_row], wo_to)
    w_relay(0)
    a_start(2)
    a_own_opp.append(a_relay(nz, a_own, 0))
    a_start(3)
    w_last(0)
    w_start(2)
    a_own_opp.append(a_relay(nz, a_own, 1))
    a_own_opp.append(a_relay(nz, a_own, 2))
    a_own_opp.append(a_relay(nz, a_own, 3))
    for k in range(4):
        a_pair[k].wait_recv()
        two = a_chunk(zl, y, k)
        a_two.append((same(two, y_right), same(two, y_left)))

    def wo_start_z():
        block = WOB.at[wo_block(zh, x)]
        return same(block, z_right), same(block, z_left)

    def wo_relay_z():
        return [
            same(wo_half(wo_block(zf, x), 0), z_right),
            same(wo_half(wo_block(zr, x), 1), z_left),
        ]

    wo_perm.wait_recv()
    wo_z = wo_start_z()

    wo_x = []

    def wo_send_x(zz):
        b = WOB.at[wo_block(zz, x)]
        wo_x.append((zz, same(b, x_right), same(b, x_left)))

    block_at = (nz, zl)

    def turn(t, h):
        @pl.loop(0, 5)
        def _(i):
            cut = pl.ds(pl.multiple_of(i * 256, 256), 256)
            piece = AB[block_at[t], cut, h * TB:(h + 1) * TB].T
            for s in range(2):
                AN[t, h, s, :, cut] = piece[s * HALF:(s + 1) * HALF, :]

    def tile(kind, k):
        d = (zh, zr, zo, zf)[k]
        cw = lax.div(d, 2)
        cols = pl.ds(pl.multiple_of(lax.rem(d, 2) * HD, HD), HD)
        queries = kind // 2 == 1
        PART[...] = jnp.zeros((2 * TB, HD), F32)

        @pl.loop(0, 5)
        def _(i):
            deep = pl.ds(pl.multiple_of(i * 256, 256), 256)
            tokens = AN[:, :, kind % 2, :, deep] if queries else AN[kind % 2, :, :, :, deep]
            PART[...] += jnp.dot(
                tokens.reshape(2 * TB, 256), WB[cw, kind // 2, deep, cols],
                preferred_element_type=F32,
            )

        part = PART[...].reshape(2, 2, HALF, HD)
        return [(part[:, h] if queries else part[h]).reshape(TB, HD) for h in range(2)]

    relay, direct, summed = {}, {}, {}

    def rs_send(kind, slot, h, part, to):
        SB[kind, slot, h] = part.astype(BF16)
        return send(SB.at[kind, slot, h], RB.at[kind, slot, h], to)

    def rs_opposite(kind):
        part = tile(kind, 2)
        for h in range(2):
            relay[kind, h] = rs_send(kind, 0, h, part[h], z_right if h == 0 else z_left)

    def rs_direct(kind):
        for slot, k, h, to in ((1, 1, 1, z_right), (2, 3, 0, z_left)):
            part = tile(kind, k)
            direct[kind, slot] = rs_send(kind, slot, h, part[h], to)
            HOLD[kind, 1 - h] = part[1 - h]

    def rs_summed(kind):
        for slot, h, to in ((1, 0, z_right), (2, 1, z_left)):
            relay[kind, h].wait_recv()
            part = HOLD[kind, h] + RB[kind, 0, h].astype(F32)
            summed[kind, slot] = rs_send(kind, slot, h, part, to)

    def rs_own(kind):
        part = tile(kind, 0)
        for h in range(2):
            OWN[kind, h] = part[h]

    def rs_result(kind):
        for slot in (1, 2):
            direct[kind, slot].wait_recv()
            summed[kind, slot].wait_recv()
        return [
            OWN[kind, h] + RB[kind, 1, h].astype(F32) + RB[kind, 2, h].astype(F32)
            for h in range(2)
        ]

    cw = lax.div(zh, 2)
    head_cols = pl.ds(pl.multiple_of(lax.rem(zh, 2) * HD, HD), HD)

    def norm(raw, tan, gain):
        ms = jnp.mean(raw * raw, axis=-1, keepdims=True)
        inv = lax.rsqrt(ms + 1e-06)
        inner = jnp.mean(raw * tan, axis=-1, keepdims=True)
        normed = gain * raw * inv
        normed_tan = gain * inv * (tan - raw * inner * inv * inv)
        return normed.astype(BF16), normed_tan.astype(BF16)

    def slot_of(xx, cc):
        return xx * 2 + cc

    g_near, g_far = {}, {}
    g_sib = {(b, t, j): [] for b in range(2) for t in range(2) for j in range(4)}

    def g_block(b, t, xx, rows=0, count=TB):
        return (KB, VB)[b].at[slot_of(xx, c), pl.ds(t * TB + rows, count), :]

    def g_start(b, t):
        block = g_block(b, t, x)
        g_near[b, t] = (same(block, x_right), same(block, x_left))
        g_sib[b, t, 0].append(same(block, sibling))

    def g_relay(b, t):
        right, left = g_near[b, t]
        right.wait_recv()
        first = same(g_block(b, t, xl, 0, HALF), x_right)
        g_sib[b, t, 1].append(same(g_block(b, t, xl), sibling))
        left.wait_recv()
        second = same(g_block(b, t, xr, HALF, HALF), x_left)
        g_sib[b, t, 2].append(same(g_block(b, t, xr), sibling))
        g_far[b, t] = (first, second)

    def g_last(b, t):
        for h in range(2):
            g_far[b, t][h].wait_recv()
            g_sib[b, t, 3].append(same(g_block(b, t, xo, h * HALF, HALF), sibling))

    def keys_out(t):
        key, key_tan = norm(*rs_result(t), GB[cw, 1, 0:1, head_cols])
        rows = slice(t * TB, (t + 1) * TB)
        KB[slot_of(x, c), rows, 0:HD] = key
        KB[slot_of(x, c), rows, HD:] = key_tan
        g_start(0, t)

    def values_out(t):
        raw, tan = rs_result(4 + t)
        rows = slice(t * TB, (t + 1) * TB)
        VB[slot_of(x, c), rows, 0:HD] = raw.astype(BF16)
        VB[slot_of(x, c), rows, HD:] = tan.astype(BF16)
        g_start(1, t)

    wo_xopp = []

    def wo_relay_x(n):
        zz, right, left = wo_x[n]
        right.wait_recv()
        wo_xopp.append(same(wo_half(wo_block(zz, xl), 0), x_right))
        left.wait_recv()
        wo_xopp.append(same(wo_half(wo_block(zz, xr), 1), x_left))

    to_exp2 = HD ** -0.5 * 1.4426950408889634
    ln2 = 0.6931471805599453
    ROWS = 32

    def queries(s):
        gain = GB[cw, 0, 0:1, head_cols] * to_exp2
        query, query_tan = norm(*rs_result(2 + s), gain)
        QB[0:TB, 0:HD] = query_tan
        QB[0:TB, HD:] = query
        QB[TB:, 0:HD] = query
        QB[TB:, HD:] = jnp.zeros((TB, HD), BF16)

    def arrived(b):
        for t in range(2):
            for j in range(4):
                wait(g_sib[b, t, j])

    def scores(s):
        MX[...] = jnp.full((TB, 128), -jnp.inf, F32)

        @pl.loop(0, 8)
        def _(j):
            cut = pl.ds(pl.multiple_of(j * 512, 512), 512)
            part = lax.dot_general(
                QB[...], KB[j], (((1,), (1,)), ((), ())), preferred_element_type=F32
            )
            S[:, cut] = part
            part = part[TB:]
            top = jnp.maximum(
                jnp.maximum(part[:, 0:128], part[:, 128:256]),
                jnp.maximum(part[:, 256:384], part[:, 384:512]),
            )
            MX[...] = jnp.maximum(MX[...], top)

    def softmax(s):
        @pl.loop(0, TB // ROWS)
        def _(i):
            at = pl.multiple_of(i * ROWS, ROWS)
            rows = pl.ds(at, ROWS)
            raw = pl.ds(TB + at, ROWS)
            shift = jnp.max(MX[rows, :], axis=-1, keepdims=True)
            total = jnp.zeros((ROWS, 128), F32)
            inner = jnp.zeros((ROWS, 128), F32)
            for j in range(16):
                cut = slice(j * 256, (j + 1) * 256)
                e = jnp.exp2(S[raw, cut] - shift)
                EB[rows, cut] = e.astype(BF16)
                es = e * S[rows, cut]
                total += e[:, :128] + e[:, 128:]
                inner += es[:, :128] + es[:, 128:]
            total = jnp.sum(total, axis=-1, keepdims=True)
            mean = jnp.sum(inner, axis=-1, keepdims=True) / total
            LI[rows, :] = jnp.broadcast_to(1.0 / total, (ROWS, HD))
            for j in range(16):
                cut = slice(j * 256, (j + 1) * 256)
                EB[raw, cut] = (EB[rows, cut].astype(F32) * (S[rows, cut] - mean)).astype(BF16)

    def products(s):
        AO[...] = jnp.zeros((2 * TB, 2 * HD), F32)

        @pl.loop(0, 8)
        def _(j):
            cut = pl.ds(pl.multiple_of(j * 512, 512), 512)
            AO[...] += jnp.dot(EB[:, cut], VB[j], preferred_element_type=F32)

    my_pair = zl * 8 + y * 2
    head_at = lax.rem(zh, 2)
    back = []

    def heads_back(s):
        inv = LI[...]
        primal = (AO[0:TB, :HD] * inv).astype(BF16)
        tangent = ((AO[0:TB, HD:] + AO[TB:, :HD] * ln2) * inv).astype(BF16)
        for t in range(2):
            HS[s, t, 0:HALF, :] = primal[t * HALF:(t + 1) * HALF, :]
            HS[s, t, HALF:, :] = tangent[t * HALF:(t + 1) * HALF, :]
        for g in range(2):
            q = 2 * s + g
            target = HB.at[my_pair + cw, q, :, head_cols]
            for t in range(2):
                zeta = 2 * c + block_at[t]
                source = HS.at[s, t, pl.ds(g * HALF, HALF), :]
                copy = pltpu.make_async_remote_copy(
                    src_ref=source, dst_ref=target, send_sem=bssem.at[2 * q + t],
                    recv_sem=brsem.at[2 * q + head_at],
                    device_id=dev(zh_=zeta, c_=cw), device_id_type=pl.DeviceIdType.MESH,
                )
                stay = pltpu.make_async_copy(source, target, lsem.at[2 * q + t])
                here = zeta == zh

                @pl.when(here)
                def _(stay=stay):
                    stay.start()
                    stay.wait()

                @pl.when(jnp.logical_not(here))
                def _(copy=copy):
                    copy.start()

                back.append((copy, here))

    def hp(zz, yy):
        return zz * 8 + yy * 2 + c

    def h_part(p, q):
        return HB.at[p, q]

    def h_half(p, q, h):
        return HB.at[p, q, pl.ds(h * (HALF // 2), HALF // 2), :]

    h_own, h_two, h_opp, swapped = {}, {}, {}, {}

    def heads_start(s):
        for q in (2 * s, 2 * s + 1):
            for h in range(2):
                came = pltpu.make_async_remote_copy(
                    src_ref=HS.at[s, h, pl.ds(0, HALF), :],
                    dst_ref=HB.at[sq, q, :, pl.ds(h * HD, HD)],
                    send_sem=bssem.at[2 * q + h], recv_sem=brsem.at[2 * q + h],
                    device_id=sibling, device_id_type=pl.DeviceIdType.MESH,
                )

                @pl.when(2 * c + h != zh)
                def _(came=came):
                    came.wait_recv()

            mine = h_part(sq, q)
            across = same(mine, pair)
            h_own[q] = (same(mine, y_right), same(mine, y_left), across)

    def heads_pair(s):
        for q in (2 * s, 2 * s + 1):
            h_own[q][2].wait_recv()
            p = hp(nz, y)
            h_two[q] = (same(h_part(p, q), y_right), same(h_part(p, q), y_left))

    def heads_relay(s, zz, arrivals):
        for q in (2 * s, 2 * s + 1):
            right, left = arrivals[q][:2]
            right.wait_recv()
            first = same(h_half(hp(zz, yl), q, 0), y_right)
            left.wait_recv()
            second = same(h_half(hp(zz, yr), q, 1), y_left)
            h_opp.setdefault((s, zz is zl), []).extend([first, second])

    def heads_relay_own(s):
        heads_relay(s, zl, h_own)

    def heads_relay_two(s):
        heads_relay(s, nz, h_two)

    def multiply(s, zz, near, first=False):
        total = None if first else ACC[s]
        for yy in (y, yl, yr) if near else (yo,):
            p = hp(zz, yy)
            part = lax.dot_general(
                WOB[pl.ds(p - c, 2)].reshape(2 * F, 2 * HD),
                HB[p, 2 * s:2 * s + 2].reshape(TB, 2 * HD), (((1,), (1,)), ((), ())),
                preferred_element_type=F32,
            )
            total = part if total is None else total + part
        ACC[s] = total

    def multiply_far(s):
        for zz in (zl, nz):
            wait(h_opp[s, zz is zl])
            multiply(s, zz, False)
        XS[s] = ACC[s, pl.ds(pl.multiple_of(c * F, 64), F), :].astype(BF16)
        swapped[s] = send(XS.at[s], XR.at[s], sibling)

    def finish(s):
        swapped[s].wait_recv()
        mine = ACC[s, pl.ds(pl.multiple_of((1 - c) * F, 64), F), :] + XR[s].astype(F32)
        cut = slice(s * HALF, (s + 1) * HALF)
        out_ref[0:F, cut] = mine[:, 0:HALF].astype(BF16)
        out_ref[F:, cut] = mine[:, HALF:].astype(BF16)

    for h in range(2):
        wait(a_own_opp[2 * h:2 * h + 2])
        for k in (2 * h, 2 * h + 1):
            a_own[k][1 - k % 2].wait_recv()
        turn(0, h)
    wait(w_sib[0])
    rs_opposite(0)
    rs_direct(0)
    for k in range(4):
        a_two_opp.append(a_relay(zl, a_two, k))
    w_relay(2)
    w_start(1)
    rs_own(0)
    rs_summed(0)
    for h in range(2):
        wait(a_two_opp[2 * h:2 * h + 2])
        for k in (2 * h, 2 * h + 1):
            a_two[k][1 - k % 2].wait_recv()
        turn(1, h)
    rs_opposite(1)
    rs_direct(1)
    w_last(2)
    w_relay(1)
    wo_send_x(zh)
    wait(wo_z)
    wo_send_x(zf)
    wo_send_x(zr)
    wait(w_sib[2])
    rs_opposite(4)
    rs_summed(1)
    rs_direct(4)
    keys_out(0)
    rs_own(1)
    rs_opposite(5)
    w_last(1)
    rs_summed(4)
    rs_direct(5)
    keys_out(1)
    wait(w_sib[1])
    rs_opposite(2)
    g_relay(0, 0)
    rs_own(4)
    rs_summed(5)
    rs_direct(2)
    g_relay(0, 1)
    values_out(0)
    rs_own(5)
    rs_opposite(3)
    rs_own(2)
    rs_own(3)
    g_last(0, 0)
    g_last(0, 1)
    for n in range(3):
        wo_relay_x(n)
    rs_summed(2)
    rs_direct(3)
    values_out(1)
    g_relay(1, 0)
    rs_summed(3)
    wo_zopp = wo_relay_z()
    g_last(1, 0)
    g_relay(1, 1)
    queries(0)
    arrived(0)
    scores(0)
    g_last(1, 1)
    softmax(0)
    arrived(1)
    products(0)
    heads_back(0)
    queries(1)
    scores(1)
    heads_start(0)
    softmax(1)
    wait(wo_zopp)
    wo_send_x(zo)
    heads_pair(0)
    heads_relay_own(0)
    products(1)
    heads_back(1)
    heads_relay_two(0)
    heads_start(1)
    wo_relay_x(3)
    heads_pair(1)
    heads_relay_own(1)
    wait(wo_xopp)
    multiply(0, zl, True, first=True)
    multiply(0, nz, True)
    multiply_far(0)
    heads_relay_two(1)
    multiply(1, zl, True, first=True)
    multiply(1, nz, True)
    multiply_far(1)
    finish(0)
    finish(1)

    for copy in sent:
        copy.wait_send()
    for copy, here in back:
        @pl.when(jnp.logical_not(here))
        def _(copy=copy):
            copy.wait_send()


def shards(
    inputs, tangents, query_weight, key_weight, value_weight, query_gain, key_gain, out_weight
):
    vmem = pl.BlockSpec(memory_space=pltpu.VMEM)
    v = pltpu.VMEM
    both = pl.pallas_call(
        kernel,
        out_shape=jax.ShapeDtypeStruct((2 * F, TB), BF16),
        in_specs=[vmem] * 8,
        out_specs=vmem,
        scratch_shapes=[
            v((2, 3, 4 * F, 256), BF16),
            v((2, 2, 8, 256), F32),
            v((2, 4 * F, 512), BF16),
            v((2, 2, 2, HALF, 4 * F), BF16),
            v((16, F, 256), BF16),
            v((2 * TB, HD), F32),
            v((6, 3, 2, TB, HD), BF16),
            v((6, 3, 2, TB, HD), BF16),
            v((6, 2, TB, HD), F32),
            v((6, 2, TB, HD), F32),
            v((8, 512, 256), BF16),
            v((8, 512, 256), BF16),
            v((2 * TB, 256), BF16),
            v((2 * TB, TOKENS), F32),
            v((TB, 128), F32),
            v((TB, HD), F32),
            v((2 * TB, TOKENS), BF16),
            v((2 * TB, 2 * HD), F32),
            v((2, 2, TB, HD), BF16),
            v((16, 4, HALF, 256), BF16),
            v((2, 2 * F, TB), F32),
            v((2, F, TB), BF16),
            v((2, F, TB), BF16),
            pltpu.SemaphoreType.DMA((N_SEMS,)),
            pltpu.SemaphoreType.DMA((N_SEMS,)),
            pltpu.SemaphoreType.DMA((8,)),
            pltpu.SemaphoreType.DMA((8,)),
            pltpu.SemaphoreType.DMA((8,)),
        ],
        compiler_params=pltpu.CompilerParams(
            collective_id=0, has_side_effects=True, vmem_limit_bytes=60 * 2**20
        ),
    )(
        inputs.T, tangents.T, query_weight, key_weight, value_weight,
        query_gain.reshape(1, 2 * HD), key_gain.reshape(1, 2 * HD), out_weight.T,
    )
    return both[:F].T, both[F:].T


def solution(mesh):
    in_specs = (
        P("seq", "dp"),
        P("seq", "dp"),
        P("dp", "seq"),
        P("dp", "seq"),
        P("dp", "seq"),
        P("seq"),
        P("seq"),
        P("seq", "dp"),
    )
    out_specs = (P("dp", "seq"), P("dp", "seq"))
    return jax.shard_map(shards, mesh=mesh, in_specs=in_specs, out_specs=out_specs, check_vma=False)
```

```python
import jax
import jax.numpy as jnp
from jax import lax
from jax.experimental import pallas as pl
from jax.experimental.pallas import tpu as pltpu
from jax.sharding import PartitionSpec as P

HD = 128
F = 320
TB = 256
TOKENS = 4096
HALF = 128
BF16 = jnp.bfloat16
F32 = jnp.float32
N_SEMS = 208


def kernel(
    in_ref, tin_ref, wq_ref, wk_ref, wv_ref, gq_ref, gk_ref, wo_ref,
    out_ref,
    WB, GB, AB, AN, WOB, PART, SB, RB, HOLD, OWN, KB, VB, QB, S, MX, LI, EB, AO, HS, HB, ACC, XS, XR,
    ssem, rsem, bssem, brsem, lsem,
):
    dp = lax.axis_index("dp")
    sq = lax.axis_index("seq")
    zh, x = lax.div(dp, 4), lax.rem(dp, 4)
    zl, y, c = lax.div(sq, 8), lax.rem(lax.div(sq, 2), 4), lax.rem(sq, 2)

    def dev(zh_=zh, x_=x, zl_=zl, y_=y, c_=c):
        return (zh_ * 4 + x_, zl_ * 8 + y_ * 2 + c_)

    def ring(v):
        return lax.rem(v + 1 + 2 * c, 4), lax.rem(v + 3 - 2 * c, 4), lax.rem(v + 2, 4)

    xr, xl, xo = ring(x)
    yr, yl, yo = ring(y)
    zr, zf, zo = ring(zh)
    x_right, x_left = dev(x_=xr), dev(x_=xl)
    y_right, y_left = dev(y_=yr), dev(y_=yl)
    z_right, z_left = dev(zh_=zr), dev(zh_=zf)
    nz = 1 - zl
    pair = dev(zl_=nz)
    sibling = dev(c_=1 - c)
    a_to = dev(x_=2 * lax.rem(y, 2) + c, zl_=1 - lax.div(y, 2), y_=x, c_=zl)
    a_from = dev(x_=y, zl_=c, y_=2 * nz + lax.div(x, 2), c_=lax.rem(x, 2))

    wo_row = 2 * lax.div(sq, 2) + 1 - lax.rem(dp, 2)
    wo_to = (wo_row, 2 * lax.div(dp, 2) + c)
    wo_from = (
        2 * lax.div(sq, 2) + 1 - lax.rem(dp, 2), 2 * lax.div(dp, 2) + c
    )

    barrier = pltpu.get_barrier_semaphore()
    greet = [x_right, x_left, y_right, y_left, pair, a_to, a_from, wo_to, wo_from]
    for k in range(1, 8):
        peer = lax.rem(zh * 2 + c + k, 8)
        greet.append(dev(zh_=lax.div(peer, 2), c_=lax.rem(peer, 2)))
    for d in greet:
        pl.semaphore_signal(barrier, inc=1, device_id=d, device_id_type=pl.DeviceIdType.MESH)

    def rows_of(xx):
        return pl.ds(pl.multiple_of(xx * F, 64), F)

    def half_rows(xx, h):
        return pl.ds(pl.multiple_of(xx * F + h * (F // 2), 32), F // 2)

    WB[c, 0, rows_of(x), :] = wk_ref[...]
    WB[c, 1, rows_of(x), :] = wq_ref[...]
    WB[c, 2, rows_of(x), :] = wv_ref[...]
    GB[c, 0] = jnp.broadcast_to(gq_ref[...], (8, 2 * HD))
    GB[c, 1] = jnp.broadcast_to(gk_ref[...], (8, 2 * HD))

    pl.semaphore_wait(barrier, len(greet))

    sent = []

    def send(src, dst, device):
        k = len(sent)
        copy = pltpu.make_async_remote_copy(
            src_ref=src, dst_ref=dst, send_sem=ssem.at[k], recv_sem=rsem.at[k],
            device_id=device, device_id_type=pl.DeviceIdType.MESH,
        )
        copy.start()
        sent.append(copy)
        return copy

    def same(ref, device):
        return send(ref, ref, device)

    def wait(copies):
        for copy in copies:
            copy.wait_recv()

    def w_piece(w, xx):
        return WB.at[c, w, rows_of(xx), :]

    def w_half(w, xx, h):
        return WB.at[c, w, half_rows(xx, h), :]

    w_near, w_far, w_sib = {}, {}, {0: [], 1: [], 2: []}

    def w_start(w):
        w_near[w] = (same(w_piece(w, x), x_right), same(w_piece(w, x), x_left))
        w_sib[w].append(same(w_piece(w, x), sibling))

    def w_relay(w):
        right, left = w_near[w]
        right.wait_recv()
        a = same(w_half(w, xl, 0), x_right)
        w_sib[w].append(same(w_piece(w, xl), sibling))
        left.wait_recv()
        b = same(w_half(w, xr, 1), x_left)
        w_sib[w].append(same(w_piece(w, xr), sibling))
        w_far[w] = (a, b)

    def w_last(w):
        for h in range(2):
            w_far[w][h].wait_recv()
            w_sib[w].append(same(w_half(w, xo, h), sibling))

    def cols_of(g):
        return pl.ds(g * TB, TB)

    def a_chunk(z, yy, k):
        return AB.at[z, half_rows(yy, k % 2), cols_of(k // 2)]

    a_perm = []
    for k in range(4):
        ref = (in_ref, tin_ref)[k // 2].at[pl.ds((k % 2) * (F // 2), F // 2), :]
        a_perm.append(
            send(ref, AB.at[lax.div(y, 2), half_rows(x, k % 2), cols_of(k // 2)], a_to)
        )

    a_own, a_pair, a_two, a_own_opp, a_two_opp = [], [], [], [], []

    def a_start(k):
        a_perm[k].wait_recv()
        own = a_chunk(nz, y, k)
        a_own.append((same(own, y_right), same(own, y_left)))
        a_pair.append(same(own, pair))

    def a_relay(z, arrivals, k):
        arrivals[k][k % 2].wait_recv()
        yy, to = ((yl, y_right), (yr, y_left))[k % 2]
        return same(a_chunk(z, yy, k), to)

    def wo_block(zz, xx):
        return zz * 4 + xx

    def wo_half(b, h):
        return WOB.at[b, pl.ds(h * (F // 2), F // 2), :]

    a_start(0)
    a_start(1)
    a_start(2)
    a_own_opp.append(a_relay(nz, a_own, 0))
    a_start(3)
    w_start(0)
    w_sib[0].append(same(GB.at[c], sibling))
    wo_perm = send(wo_ref, WOB.at[wo_row], wo_to)
    a_own_opp.append(a_relay(nz, a_own, 1))
    w_relay(0)
    a_own_opp.append(a_relay(nz, a_own, 2))
    a_own_opp.append(a_relay(nz, a_own, 3))
    for k in range(4):
        a_pair[k].wait_recv()
        two = a_chunk(zl, y, k)
        a_two.append((same(two, y_right), same(two, y_left)))

    def wo_start_z():
        block = WOB.at[wo_block(zh, x)]
        return same(block, z_right), same(block, z_left)

    def wo_relay_z():
        return [
            same(wo_half(wo_block(zf, x), 0), z_right),
            same(wo_half(wo_block(zr, x), 1), z_left),
        ]

    w_start(2)
    wo_perm.wait_recv()
    wo_z = wo_start_z()
    w_last(0)

    wo_x = []

    def wo_send_x(zz):
        b = WOB.at[wo_block(zz, x)]
        wo_x.append((zz, same(b, x_right), same(b, x_left)))

    block_at = (nz, zl)

    def turn(t, h):
        @pl.loop(0, 5)
        def _(i):
            cut = pl.ds(pl.multiple_of(i * 256, 256), 256)
            piece = AB[block_at[t], cut, h * TB:(h + 1) * TB].T
            for s in range(2):
                AN[t, h, s, :, cut] = piece[s * HALF:(s + 1) * HALF, :]

    def tile(kind, k):
        d = (zh, zr, zo, zf)[k]
        cw = lax.div(d, 2)
        cols = pl.ds(pl.multiple_of(lax.rem(d, 2) * HD, HD), HD)
        queries = kind // 2 == 1
        PART[...] = jnp.zeros((2 * TB, HD), F32)

        @pl.loop(0, 5)
        def _(i):
            deep = pl.ds(pl.multiple_of(i * 256, 256), 256)
            tokens = AN[:, :, kind % 2, :, deep] if queries else AN[kind % 2, :, :, :, deep]
            PART[...] += jnp.dot(
                tokens.reshape(2 * TB, 256), WB[cw, kind // 2, deep, cols],
                preferred_element_type=F32,
            )

        part = PART[...].reshape(2, 2, HALF, HD)
        return [(part[:, h] if queries else part[h]).reshape(TB, HD) for h in range(2)]

    relay, direct, summed = {}, {}, {}

    def rs_send(kind, slot, h, part, to):
        SB[kind, slot, h] = part.astype(BF16)
        return send(SB.at[kind, slot, h], RB.at[kind, slot, h], to)

    def rs_opposite(kind):
        part = tile(kind, 2)
        for h in range(2):
            relay[kind, h] = rs_send(kind, 0, h, part[h], z_right if h == 0 else z_left)

    def rs_direct(kind):
        for slot, k, h, to in ((1, 1, 1, z_right), (2, 3, 0, z_left)):
            part = tile(kind, k)
            direct[kind, slot] = rs_send(kind, slot, h, part[h], to)
            HOLD[kind, 1 - h] = part[1 - h]

    def rs_summed(kind):
        for slot, h, to in ((1, 0, z_right), (2, 1, z_left)):
            relay[kind, h].wait_recv()
            part = HOLD[kind, h] + RB[kind, 0, h].astype(F32)
            summed[kind, slot] = rs_send(kind, slot, h, part, to)

    def rs_own(kind):
        part = tile(kind, 0)
        for h in range(2):
            OWN[kind, h] = part[h]

    def rs_result(kind):
        for slot in (1, 2):
            direct[kind, slot].wait_recv()
            summed[kind, slot].wait_recv()
        return [
            OWN[kind, h] + RB[kind, 1, h].astype(F32) + RB[kind, 2, h].astype(F32)
            for h in range(2)
        ]

    cw = lax.div(zh, 2)
    head_cols = pl.ds(pl.multiple_of(lax.rem(zh, 2) * HD, HD), HD)

    def norm(raw, tan, gain):
        ms = jnp.mean(raw * raw, axis=-1, keepdims=True)
        inv = lax.rsqrt(ms + 1e-06)
        inner = jnp.mean(raw * tan, axis=-1, keepdims=True)
        normed = gain * raw * inv
        normed_tan = gain * inv * (tan - raw * inner * inv * inv)
        return normed.astype(BF16), normed_tan.astype(BF16)

    def slot_of(xx, cc):
        return xx * 2 + cc

    g_near, g_far = {}, {}
    g_sib = {(b, t, j): [] for b in range(2) for t in range(2) for j in range(4)}

    def g_block(b, t, xx, rows=0, count=TB):
        return (KB, VB)[b].at[slot_of(xx, c), pl.ds(t * TB + rows, count), :]

    def g_start(b, t):
        block = g_block(b, t, x)
        g_near[b, t] = (same(block, x_right), same(block, x_left))
        g_sib[b, t, 0].append(same(block, sibling))

    def g_relay(b, t):
        right, left = g_near[b, t]
        right.wait_recv()
        first = same(g_block(b, t, xl, 0, HALF), x_right)
        g_sib[b, t, 1].append(same(g_block(b, t, xl), sibling))
        left.wait_recv()
        second = same(g_block(b, t, xr, HALF, HALF), x_left)
        g_sib[b, t, 2].append(same(g_block(b, t, xr), sibling))
        g_far[b, t] = (first, second)

    def g_last(b, t):
        for h in range(2):
            g_far[b, t][h].wait_recv()
            g_sib[b, t, 3].append(same(g_block(b, t, xo, h * HALF, HALF), sibling))

    def keys_out(t):
        key, key_tan = norm(*rs_result(t), GB[cw, 1, 0:1, head_cols])
        rows = slice(t * TB, (t + 1) * TB)
        KB[slot_of(x, c), rows, 0:HD] = key
        KB[slot_of(x, c), rows, HD:] = key_tan
        g_start(0, t)

    def values_out(t):
        raw, tan = rs_result(4 + t)
        rows = slice(t * TB, (t + 1) * TB)
        VB[slot_of(x, c), rows, 0:HD] = raw.astype(BF16)
        VB[slot_of(x, c), rows, HD:] = tan.astype(BF16)
        g_start(1, t)

    wo_xopp = []

    def wo_relay_x(n):
        zz, right, left = wo_x[n]
        right.wait_recv()
        wo_xopp.append(same(wo_half(wo_block(zz, xl), 0), x_right))
        left.wait_recv()
        wo_xopp.append(same(wo_half(wo_block(zz, xr), 1), x_left))

    to_exp2 = HD ** -0.5 * 1.4426950408889634
    ln2 = 0.6931471805599453
    ROWS = 32

    def queries(s):
        gain = GB[cw, 0, 0:1, head_cols] * to_exp2
        query, query_tan = norm(*rs_result(2 + s), gain)
        QB[0:TB, 0:HD] = query_tan
        QB[0:TB, HD:] = query
        QB[TB:, 0:HD] = query
        QB[TB:, HD:] = jnp.zeros((TB, HD), BF16)

    def arrived(b):
        for t in range(2):
            for j in range(4):
                wait(g_sib[b, t, j])

    def scores(s):
        MX[...] = jnp.full((TB, 128), -jnp.inf, F32)

        @pl.loop(0, 8)
        def _(j):
            cut = pl.ds(pl.multiple_of(j * 512, 512), 512)
            part = lax.dot_general(
                QB[...], KB[j], (((1,), (1,)), ((), ())), preferred_element_type=F32
            )
            S[:, cut] = part
            part = part[TB:]
            top = jnp.maximum(
                jnp.maximum(part[:, 0:128], part[:, 128:256]),
                jnp.maximum(part[:, 256:384], part[:, 384:512]),
            )
            MX[...] = jnp.maximum(MX[...], top)

    def softmax(s):
        @pl.loop(0, TB // ROWS)
        def _(i):
            at = pl.multiple_of(i * ROWS, ROWS)
            rows = pl.ds(at, ROWS)
            raw = pl.ds(TB + at, ROWS)
            shift = jnp.max(MX[rows, :], axis=-1, keepdims=True)
            total = jnp.zeros((ROWS, 128), F32)
            inner = jnp.zeros((ROWS, 128), F32)
            for j in range(16):
                cut = slice(j * 256, (j + 1) * 256)
                e = jnp.exp2(S[raw, cut] - shift)
                EB[rows, cut] = e.astype(BF16)
                es = e * S[rows, cut]
                total += e[:, :128] + e[:, 128:]
                inner += es[:, :128] + es[:, 128:]
            total = jnp.sum(total, axis=-1, keepdims=True)
            mean = jnp.sum(inner, axis=-1, keepdims=True) / total
            LI[rows, :] = jnp.broadcast_to(1.0 / total, (ROWS, HD))
            for j in range(16):
                cut = slice(j * 256, (j + 1) * 256)
                EB[raw, cut] = (EB[rows, cut].astype(F32) * (S[rows, cut] - mean)).astype(BF16)

    def products(s):
        AO[...] = jnp.zeros((2 * TB, 2 * HD), F32)

        @pl.loop(0, 8)
        def _(j):
            cut = pl.ds(pl.multiple_of(j * 512, 512), 512)
            AO[...] += jnp.dot(EB[:, cut], VB[j], preferred_element_type=F32)

    my_pair = zl * 8 + y * 2
    head_at = lax.rem(zh, 2)
    back = []

    def heads_back(s):
        inv = LI[...]
        primal = (AO[0:TB, :HD] * inv).astype(BF16)
        tangent = ((AO[0:TB, HD:] + AO[TB:, :HD] * ln2) * inv).astype(BF16)
        for t in range(2):
            HS[s, t, 0:HALF, :] = primal[t * HALF:(t + 1) * HALF, :]
            HS[s, t, HALF:, :] = tangent[t * HALF:(t + 1) * HALF, :]
        for g in range(2):
            q = 2 * s + g
            target = HB.at[my_pair + cw, q, :, head_cols]
            for t in range(2):
                zeta = 2 * c + block_at[t]
                source = HS.at[s, t, pl.ds(g * HALF, HALF), :]
                copy = pltpu.make_async_remote_copy(
                    src_ref=source, dst_ref=target, send_sem=bssem.at[2 * q + t],
                    recv_sem=brsem.at[2 * q + head_at],
                    device_id=dev(zh_=zeta, c_=cw), device_id_type=pl.DeviceIdType.MESH,
                )
                stay = pltpu.make_async_copy(source, target, lsem.at[2 * q + t])
                here = zeta == zh

                @pl.when(here)
                def _(stay=stay):
                    stay.start()
                    stay.wait()

                @pl.when(jnp.logical_not(here))
                def _(copy=copy):
                    copy.start()

                back.append((copy, here))

    def hp(zz, yy):
        return zz * 8 + yy * 2 + c

    def h_part(p, q):
        return HB.at[p, q]

    def h_half(p, q, h):
        return HB.at[p, q, pl.ds(h * (HALF // 2), HALF // 2), :]

    h_own, h_two, h_opp, swapped = {}, {}, {}, {}

    def heads_start(s):
        for q in (2 * s, 2 * s + 1):
            for h in range(2):
                came = pltpu.make_async_remote_copy(
                    src_ref=HS.at[s, h, pl.ds(0, HALF), :],
                    dst_ref=HB.at[sq, q, :, pl.ds(h * HD, HD)],
                    send_sem=bssem.at[2 * q + h], recv_sem=brsem.at[2 * q + h],
                    device_id=sibling, device_id_type=pl.DeviceIdType.MESH,
                )

                @pl.when(2 * c + h != zh)
                def _(came=came):
                    came.wait_recv()

            mine = h_part(sq, q)
            across = same(mine, pair)
            h_own[q] = (same(mine, y_right), same(mine, y_left), across)

    def heads_pair(s):
        for q in (2 * s, 2 * s + 1):
            h_own[q][2].wait_recv()
            p = hp(nz, y)
            h_two[q] = (same(h_part(p, q), y_right), same(h_part(p, q), y_left))

    def heads_relay(s, zz, arrivals):
        for q in (2 * s, 2 * s + 1):
            right, left = arrivals[q][:2]
            right.wait_recv()
            first = same(h_half(hp(zz, yl), q, 0), y_right)
            left.wait_recv()
            second = same(h_half(hp(zz, yr), q, 1), y_left)
            h_opp.setdefault((s, zz is zl), []).extend([first, second])

    def heads_relay_own(s):
        heads_relay(s, zl, h_own)

    def heads_relay_two(s):
        heads_relay(s, nz, h_two)

    def multiply(s, zz, near, first=False):
        total = None if first else ACC[s]
        for yy in (y, yl, yr) if near else (yo,):
            p = hp(zz, yy)
            part = lax.dot_general(
                WOB[pl.ds(p - c, 2)].reshape(2 * F, 2 * HD),
                HB[p, 2 * s:2 * s + 2].reshape(TB, 2 * HD), (((1,), (1,)), ((), ())),
                preferred_element_type=F32,
            )
            total = part if total is None else total + part
        ACC[s] = total

    def multiply_far(s):
        for zz in (zl, nz):
            wait(h_opp[s, zz is zl])
            multiply(s, zz, False)
        XS[s] = ACC[s, pl.ds(pl.multiple_of(c * F, 64), F), :].astype(BF16)
        swapped[s] = send(XS.at[s], XR.at[s], sibling)

    def finish(s):
        swapped[s].wait_recv()
        mine = ACC[s, pl.ds(pl.multiple_of((1 - c) * F, 64), F), :] + XR[s].astype(F32)
        cut = slice(s * HALF, (s + 1) * HALF)
        out_ref[0:F, cut] = mine[:, 0:HALF].astype(BF16)
        out_ref[F:, cut] = mine[:, HALF:].astype(BF16)

    for h in range(2):
        wait(a_own_opp[2 * h:2 * h + 2])
        for k in (2 * h, 2 * h + 1):
            a_own[k][1 - k % 2].wait_recv()
        turn(0, h)
    wait(w_sib[0])
    rs_opposite(0)
    rs_direct(0)
    for k in range(4):
        a_two_opp.append(a_relay(zl, a_two, k))
    w_relay(2)
    w_start(1)
    rs_own(0)
    rs_summed(0)
    for h in range(2):
        wait(a_two_opp[2 * h:2 * h + 2])
        for k in (2 * h, 2 * h + 1):
            a_two[k][1 - k % 2].wait_recv()
        turn(1, h)
    rs_opposite(1)
    rs_direct(1)
    w_last(2)
    w_relay(1)
    wo_send_x(zh)
    wait(wo_z)
    wo_send_x(zf)
    wo_send_x(zr)
    wait(w_sib[2])
    rs_opposite(4)
    rs_summed(1)
    rs_direct(4)
    keys_out(0)
    rs_own(1)
    rs_opposite(5)
    w_last(1)
    rs_summed(4)
    rs_direct(5)
    keys_out(1)
    wait(w_sib[1])
    rs_opposite(2)
    g_relay(0, 0)
    rs_own(4)
    rs_summed(5)
    rs_direct(2)
    g_relay(0, 1)
    values_out(0)
    rs_own(5)
    rs_opposite(3)
    rs_own(2)
    rs_own(3)
    g_last(0, 0)
    g_last(0, 1)
    for n in range(3):
        wo_relay_x(n)
    rs_summed(2)
    rs_direct(3)
    values_out(1)
    g_relay(1, 0)
    rs_summed(3)
    wo_zopp = wo_relay_z()
    g_last(1, 0)
    g_relay(1, 1)
    queries(0)
    arrived(0)
    scores(0)
    g_last(1, 1)
    softmax(0)
    arrived(1)
    products(0)
    heads_back(0)
    queries(1)
    scores(1)
    heads_start(0)
    softmax(1)
    wait(wo_zopp)
    wo_send_x(zo)
    heads_pair(0)
    heads_relay_own(0)
    products(1)
    heads_back(1)
    heads_relay_two(0)
    heads_start(1)
    wo_relay_x(3)
    heads_pair(1)
    heads_relay_own(1)
    wait(wo_xopp)
    multiply(0, zl, True, first=True)
    multiply(0, nz, True)
    multiply_far(0)
    heads_relay_two(1)
    multiply(1, zl, True, first=True)
    multiply(1, nz, True)
    multiply_far(1)
    finish(0)
    finish(1)

    for copy in sent:
        copy.wait_send()
    for copy, here in back:
        @pl.when(jnp.logical_not(here))
        def _(copy=copy):
            copy.wait_send()


def shards(
    inputs, tangents, query_weight, key_weight, value_weight, query_gain, key_gain, out_weight
):
    vmem = pl.BlockSpec(memory_space=pltpu.VMEM)
    v = pltpu.VMEM
    both = pl.pallas_call(
        kernel,
        out_shape=jax.ShapeDtypeStruct((2 * F, TB), BF16),
        in_specs=[vmem] * 8,
        out_specs=vmem,
        scratch_shapes=[
            v((2, 3, 4 * F, 256), BF16),
            v((2, 2, 8, 256), F32),
            v((2, 4 * F, 512), BF16),
            v((2, 2, 2, HALF, 4 * F), BF16),
            v((16, F, 256), BF16),
            v((2 * TB, HD), F32),
            v((6, 3, 2, TB, HD), BF16),
            v((6, 3, 2, TB, HD), BF16),
            v((6, 2, TB, HD), F32),
            v((6, 2, TB, HD), F32),
            v((8, 512, 256), BF16),
            v((8, 512, 256), BF16),
            v((2 * TB, 256), BF16),
            v((2 * TB, TOKENS), F32),
            v((TB, 128), F32),
            v((TB, HD), F32),
            v((2 * TB, TOKENS), BF16),
            v((2 * TB, 2 * HD), F32),
            v((2, 2, TB, HD), BF16),
            v((16, 4, HALF, 256), BF16),
            v((2, 2 * F, TB), F32),
            v((2, F, TB), BF16),
            v((2, F, TB), BF16),
            pltpu.SemaphoreType.DMA((N_SEMS,)),
            pltpu.SemaphoreType.DMA((N_SEMS,)),
            pltpu.SemaphoreType.DMA((8,)),
            pltpu.SemaphoreType.DMA((8,)),
            pltpu.SemaphoreType.DMA((8,)),
        ],
        compiler_params=pltpu.CompilerParams(
            collective_id=0, has_side_effects=True, vmem_limit_bytes=60 * 2**20
        ),
    )(
        inputs.T, tangents.T, query_weight, key_weight, value_weight,
        query_gain.reshape(1, 2 * HD), key_gain.reshape(1, 2 * HD), out_weight.T,
    )
    return both[:F].T, both[F:].T


def solution(mesh):
    in_specs = (
        P("seq", "dp"),
        P("seq", "dp"),
        P("dp", "seq"),
        P("dp", "seq"),
        P("dp", "seq"),
        P("seq"),
        P("seq"),
        P("seq", "dp"),
    )
    out_specs = (P("dp", "seq"), P("dp", "seq"))
    return jax.shard_map(shards, mesh=mesh, in_specs=in_specs, out_specs=out_specs, check_vma=False)
```
